32 devices in a mesh: dp: 2 (over core), ctx: 8 (over z, y), fsdp: 2 (over x).
Axes of the slice: x: 2, y: 2, z: 4, core: 2. Of those that a mesh axis runs over, the one named last changes fastest.
Arguments:
- tokens: bfloat16 [4, 1024, 1152], P(('dp', 'fsdp'), 'ctx'), may hold values from -6 to 6
- cotangent: bfloat16 [4, 1024, 1152], P(('dp', 'fsdp'), 'ctx'), may hold values from -6 to 6
- segments: int32 [4, 1024], P(('dp', 'fsdp')), may hold values from 0 to 15, never falling along the last dimension, each value on 1 to 640 neighbouring positions
- qkv_weight: float32 [1536, 1152], P(('ctx', 'fsdp')), may hold values from -0.1875 to 0.1875
- out_weight: float32 [1024, 1152], P(('ctx', 'fsdp')), may hold values from -0.1875 to 0.1875
- gate_up_weight: float32 [13824, 1152], P(('ctx', 'fsdp')), may hold values from -0.1875 to 0.1875
- down_weight: float32 [6912, 1152], P(('ctx', 'fsdp')), may hold values from -0.078125 to 0.078125
- gains: float32 [5120], P(('ctx', 'fsdp')), may hold values from -0.15 to 0.15
- qkv_first: float32 [1536, 1152], P(('ctx', 'fsdp')), may hold values from -90 to 90
- out_first: float32 [1024, 1152], P(('ctx', 'fsdp')), may hold values from -90 to 90
- gate_up_first: float32 [13824, 1152], P(('ctx', 'fsdp')), may hold values from -90 to 90
- down_first: float32 [6912, 1152], P(('ctx', 'fsdp')), may hold values from -90 to 90
- gains_first: float32 [5120], P(('ctx', 'fsdp')), may hold values from -90 to 90
- qkv_second: float32 [1536, 1152], P(('ctx', 'fsdp')), may hold values from 300 to 3000
- out_second: float32 [1024, 1152], P(('ctx', 'fsdp')), may hold values from 300 to 3000
- gate_up_second: float32 [13824, 1152], P(('ctx', 'fsdp')), may hold values from 300 to 3000
- down_second: float32 [6912, 1152], P(('ctx', 'fsdp')), may hold values from 300 to 3000
- gains_second: float32 [5120], P(('ctx', 'fsdp')), may hold values from 300 to 3000
Outputs:
- output: bfloat16 [4, 1024, 1152], P(('dp', 'fsdp'), 'ctx')
- input_grad: float32 [4, 1024, 1152], P(('dp', 'fsdp'), 'ctx')
- qkv_grad: float32 [1536, 1152], P(('ctx', 'fsdp'))
- out_grad: float32 [1024, 1152], P(('ctx', 'fsdp'))
- gate_up_grad: float32 [13824, 1152], P(('ctx', 'fsdp'))
- down_grad: float32 [6912, 1152], P(('ctx', 'fsdp'))
- gains_grad: float32 [5120], P(('ctx', 'fsdp'))
- qkv_new: float32 [1536, 1152], P(('ctx', 'fsdp'))
- out_new: float32 [1024, 1152], P(('ctx', 'fsdp'))
- gate_up_new: float32 [13824, 1152], P(('ctx', 'fsdp'))
- down_new: float32 [6912, 1152], P(('ctx', 'fsdp'))
- gains_new: float32 [5120], P(('ctx', 'fsdp'))
- qkv_first_new: float32 [1536, 1152], P(('ctx', 'fsdp'))
- out_first_new: float32 [1024, 1152], P(('ctx', 'fsdp'))
- gate_up_first_new: float32 [13824, 1152], P(('ctx', 'fsdp'))
- down_first_new: float32 [6912, 1152], P(('ctx', 'fsdp'))
- gains_first_new: float32 [5120], P(('ctx', 'fsdp'))
- qkv_second_new: float32 [1536, 1152], P(('ctx', 'fsdp'))
- out_second_new: float32 [1024, 1152], P(('ctx', 'fsdp'))
- gate_up_second_new: float32 [13824, 1152], P(('ctx', 'fsdp'))
- down_second_new: float32 [6912, 1152], P(('ctx', 'fsdp'))
- gains_second_new: float32 [5120], P(('ctx', 'fsdp'))
The draws below stay inside these ranges and needn't reach their ends.
Inputs may be any that keep to these rules, and one draw needn't show every extreme that they name: `segments`: in each sequence the segment numbers never fall, every number appears, each document has 1 to 640 tokens, and one has exactly 640.
All inputs are finite; a program needn't handle non-finite values.
Results may differ from the reference program's by a relative error of at most 0.018.
Values may be sent and summed in bfloat16 or wider, within the bound.
A program may use at most 320 MiB of HBM per device.

```python
import math
import jax
import jax.numpy as jnp
import numpy as np
from jax import lax

D = 1152
H = 4
HD = 256
FF = 6912
TOK_DEV = 128
DOCS = 16
STEP = 5
QKV = 1536
GAINS = 5120
SEQS = 4
LENGTH = 1024


def block_scale(key, dims, shards, low, largest):
    def one(position, shards_of):
        steps = jax.random.uniform(jax.random.fold_in(jax.random.fold_in(key, 6), position), (shards_of,), jnp.float32, low / len(shards), largest / len(shards))
        return jnp.repeat(jnp.exp(steps), dims[position] // shards_of).reshape((-1,) + (1,) * (len(dims) - position - 1))

    loudness = one(*shards[0])
    for cut in shards[1:]:
        loudness = loudness * one(*cut)
    return loudness


def length_profile(amount, total, bound, lean):
    weights = [(1 << 20) // math.isqrt(rank ** lean) + 1 for rank in range(2, amount + 1)]
    spare, counts = total - bound - (amount - 1), [1] * (amount - 1)
    while spare > 0:
        free = [i for i in range(amount - 1) if counts[i] < bound]
        whole, left = sum([weights[i] for i in free]), spare
        for i in free:
            addition = min(bound - counts[i], max(1, left * weights[i] // whole), spare)
            counts[i] = counts[i] + addition
            spare = spare - addition
    return np.array([bound] + counts)


def uneven_parts(own_key, count, total, bound, skew):
    if count == 2:
        one = jax.random.randint(own_key, (), max(1, total - bound), min(bound, total - 1) + 1)
        return jnp.stack([one, total - one])
    sizes = jnp.asarray(length_profile(count, total, bound, skew), jnp.int32)
    pairs = (count - 1) // 2
    donor, sink = sizes[1:1 + 2 * pairs:2], sizes[2:2 + 2 * pairs:2]
    margin = jnp.minimum(donor - 1, bound - sink)
    shifted = jax.random.randint(jax.random.fold_in(own_key, 1), (pairs,), 0, 1 << 20) % (margin + 1)
    sizes = sizes.at[1:1 + 2 * pairs:2].set(donor - shifted).at[2:2 + 2 * pairs:2].set(sink + shifted)
    return sizes[jax.random.permutation(jax.random.fold_in(own_key, 2), count)]


def gaussian(key, shape, spread, most, split=(), held_as=jnp.bfloat16):
    factor_of = block_scale(key, shape, split, -0.22, 0.18) if split else 1.0
    result = jax.random.normal(key, shape, jnp.float32) * spread * factor_of
    return jnp.minimum(jnp.maximum(result, -most), most).astype(held_as)


def setup_inputs(seed: int = 0) -> dict:
    key_list = jax.random.split(jax.random.key(seed), 19)
    return {
        "tokens": gaussian(key_list[0], (SEQS, LENGTH, D), 1.0, 6.0, ((0, 4), (1, 8))),
        "cotangent": gaussian(key_list[1], (SEQS, LENGTH, D), 1.0, 6.0, ((0, 4), (1, 8))),
        "segments": jax.vmap(lambda own: jnp.searchsorted(jnp.cumsum(uneven_parts(own, DOCS, LENGTH, LENGTH // 2 + TOK_DEV, 2)), jnp.arange(LENGTH), side="right"))(jax.random.split(key_list[2], SEQS)).reshape((SEQS, LENGTH)).astype(jnp.int32),
        "qkv_weight": gaussian(key_list[3], (QKV, D), D ** -0.5, 0.1875, ((0, 16),), jnp.float32),
        "out_weight": gaussian(key_list[4], (H * HD, D), (H * HD) ** -0.5, 0.1875, ((0, 16),), jnp.float32),
        "gate_up_weight": gaussian(key_list[5], (2 * FF, D), D ** -0.5, 0.1875, ((0, 16),), jnp.float32),
        "down_weight": gaussian(key_list[6], (FF, D), FF ** -0.5, 0.078125, ((0, 16),), jnp.float32),
        "gains": jnp.clip(jax.random.uniform(key_list[7], (GAINS,), jnp.float32, -0.15, 0.15) * block_scale(key_list[7], (GAINS,), ((0, 16),), -0.4, 0.0), -0.15, 0.15),
        "qkv_first": gaussian(key_list[8], (QKV, D), 15.0, 90.0, ((0, 16),), jnp.float32),
        "out_first": gaussian(key_list[9], (H * HD, D), 15.0, 90.0, ((0, 16),), jnp.float32),
        "gate_up_first": gaussian(key_list[10], (2 * FF, D), 15.0, 90.0, ((0, 16),), jnp.float32),
        "down_first": gaussian(key_list[11], (FF, D), 15.0, 90.0, ((0, 16),), jnp.float32),
        "gains_first": gaussian(key_list[12], (GAINS,), 15.0, 90.0, ((0, 16),), jnp.float32),
        "qkv_second": jnp.clip(jnp.exp(math.log(3000.0) - 2.3025851 * jax.random.uniform(key_list[13], (QKV, D), jnp.float32) ** block_scale(key_list[13], (QKV, D), ((0, 16),), -0.2, 0.2)), 300.0, 3000.0),
        "out_second": jnp.clip(jnp.exp(math.log(3000.0) - 2.3025851 * jax.random.uniform(key_list[14], (H * HD, D), jnp.float32) ** block_scale(key_list[14], (H * HD, D), ((0, 16),), -0.2, 0.2)), 300.0, 3000.0),
        "gate_up_second": jnp.clip(jnp.exp(math.log(3000.0) - 2.3025851 * jax.random.uniform(key_list[15], (2 * FF, D), jnp.float32) ** block_scale(key_list[15], (2 * FF, D), ((0, 16),), -0.2, 0.2)), 300.0, 3000.0),
        "down_second": jnp.clip(jnp.exp(math.log(3000.0) - 2.3025851 * jax.random.uniform(key_list[16], (FF, D), jnp.float32) ** block_scale(key_list[16], (FF, D), ((0, 16),), -0.2, 0.2)), 300.0, 3000.0),
        "gains_second": jnp.clip(jnp.exp(math.log(3000.0) - 2.3025851 * jax.random.uniform(key_list[17], (GAINS,), jnp.float32) ** block_scale(key_list[17], (GAINS,), ((0, 16),), -0.2, 0.2)), 300.0, 3000.0),
    }


@jax.custom_vjp
def low(v):
    return lax.optimization_barrier(v.astype(jnp.bfloat16)).astype(jnp.float32)

@jax.custom_vjp
def low_back(v):
    return v

def low_keep(v):
    return (low(v), None)

def low_pass(kept, grad):
    return (grad,)

def back_keep(v):
    return (v, None)

def back_low(kept, grad):
    return (low(grad),)
low.defvjp(low_keep, low_pass)
low_back.defvjp(back_keep, back_low)

def normalize(value, gain):
    scale = lax.rsqrt(lax.optimization_barrier(jnp.mean(value * value, axis=-1, keepdims=True)) + 1e-06)
    return value * scale * (1.0 + gain)

def rotate(value, angles):
    half = value.shape[-1] // 2
    first = value[..., :half]
    second = value[..., half:]
    cosine = jnp.cos(angles)
    sine = jnp.sin(angles)
    return jnp.concatenate([first * cosine - second * sine, second * cosine + first * sine], axis=-1)

def rope_angles(segments):
    count = segments.shape[0]
    index = jnp.arange(count, dtype=jnp.int32)
    change = jnp.concatenate([jnp.ones((1,), dtype=jnp.bool_), segments[1:] != segments[:-1]])
    starts = lax.cummax(jnp.where(change, index, 0), axis=0)
    offset = (index - starts).astype(jnp.float32)
    inverse = jnp.exp(-jnp.log(1000000.0) * (2.0 * jnp.arange(HD // 2, dtype=jnp.float32)) / HD)
    return offset[:, None] * inverse[None, :]

def matmul(left, right):
    return jnp.dot(left, right, precision=lax.Precision.HIGHEST, preferred_element_type=jnp.float32)

def forward(inputs, segments, qkv_matrix, out_matrix, gate_matrix, down_matrix, gain_vector):
    qkv_matrix = low(qkv_matrix)
    out_matrix = low(out_matrix)
    gate_matrix = low(gate_matrix)
    down_matrix = low(down_matrix)
    gain_vector = low(gain_vector)
    gain_input = gain_vector[:D]
    gain_attend = gain_vector[D:2 * D]
    gain_pre = gain_vector[2 * D:3 * D]
    gain_post = gain_vector[3 * D:4 * D]
    gain_query = gain_vector[4 * D:4 * D + HD]
    gain_key = gain_vector[4 * D + HD:]
    length = inputs.shape[0]
    angles = rope_angles(segments)
    normed = low(normalize(inputs, gain_input))
    projected = low_back(matmul(normed, qkv_matrix.T))
    query = low(rotate(normalize(projected[:, :H * HD].reshape(length, H, HD), gain_query), angles[:, None, :]))
    key = low(rotate(normalize(projected[:, H * HD:H * HD + HD], gain_key), angles))
    value = low(projected[:, H * HD + HD:])
    span = min(512, length)
    index = jnp.arange(length, dtype=jnp.int32)

    def attend(start):
        rows_query = lax.dynamic_slice_in_dim(query, start, span, 0)
        rows_ids = lax.dynamic_slice_in_dim(segments, start, span, 0)
        rows_pos = start + jnp.arange(span, dtype=jnp.int32)
        allowed = (index[None, :] <= rows_pos[:, None]) & (segments[None, :] == rows_ids[:, None])
        scores = low_back(jnp.einsum('ihd,jd->hij', rows_query, key, precision=lax.Precision.HIGHEST) * HD ** (-0.5))
        probs = jax.nn.softmax(jnp.where(allowed[None], scores, -1e+30), axis=-1)
        return jnp.einsum('hij,jd->ihd', low(probs), value, precision=lax.Precision.HIGHEST)
    starts = jnp.arange(length // span, dtype=jnp.int32) * span
    attended = lax.map(jax.checkpoint(attend), starts).reshape(length, H * HD)
    attended = low(low_back(attended))
    branch = low_back(matmul(attended, out_matrix))
    hidden = inputs + normalize(branch, gain_attend)
    hidden_low = low(normalize(hidden, gain_pre))
    gate_up = low_back(matmul(hidden_low, gate_matrix.T))
    mixed = low(jax.nn.gelu(gate_up[:, :FF], approximate=True) * gate_up[:, FF:])
    down = low_back(matmul(mixed, down_matrix))
    return hidden + normalize(down, gain_post)

def adamw(weight, grad, first, second):
    first_new = 0.9 * first + 0.1 * grad
    second_new = 0.95 * second + 0.05 * grad * grad
    first_hat = first_new / (1.0 - 0.9 ** STEP)
    second_hat = second_new / (1.0 - 0.95 ** STEP)
    weight_new = weight - 0.03 * (first_hat / (jnp.sqrt(second_hat) + 1e-08) + 0.1 * weight)
    return (weight_new, first_new, second_new)

def reference(tokens, cotangent, segments, qkv_weight, out_weight, gate_up_weight, down_weight, gains, qkv_first, out_first, gate_up_first, down_first, gains_first, qkv_second, out_second, gate_up_second, down_second, gains_second):

    def run(inputs, qkv_matrix, out_matrix, gate_matrix, down_matrix, gain_vector):

        def single(item):
            return forward(item[0], item[1], qkv_matrix, out_matrix, gate_matrix, down_matrix, gain_vector)
        return lax.map(jax.checkpoint(single), (inputs, segments))
    outputs, pullback = jax.vjp(run, tokens.astype(jnp.float32), qkv_weight, out_weight, gate_up_weight, down_weight, gains)
    input_grad, qkv_grad, out_grad, gate_up_grad, down_grad, gains_grad = pullback(cotangent.astype(jnp.float32))
    qkv_new, qkv_first_new, qkv_second_new = adamw(qkv_weight, qkv_grad, qkv_first, qkv_second)
    out_new, out_first_new, out_second_new = adamw(out_weight, out_grad, out_first, out_second)
    gate_up_new, gate_up_first_new, gate_up_second_new = adamw(gate_up_weight, gate_up_grad, gate_up_first, gate_up_second)
    down_new, down_first_new, down_second_new = adamw(down_weight, down_grad, down_first, down_second)
    gains_new, gains_first_new, gains_second_new = adamw(gains, gains_grad, gains_first, gains_second)
    return (outputs.astype(jnp.bfloat16), input_grad, qkv_grad, out_grad, gate_up_grad, down_grad, gains_grad, qkv_new, out_new, gate_up_new, down_new, gains_new, qkv_first_new, out_first_new, gate_up_first_new, down_first_new, gains_first_new, qkv_second_new, out_second_new, gate_up_second_new, down_second_new, gains_second_new)
```

```python
import functools

import jax
import jax.numpy as jnp
from jax import lax
from jax.experimental import pallas as pl
from jax.experimental.pallas import tpu as pltpu
from jax.sharding import PartitionSpec as P

MESH = pl.DeviceIdType.MESH
ANY = pl.BlockSpec(memory_space=pl.ANY)
VMEM = pl.BlockSpec(memory_space=pltpu.VMEM)
BF = jnp.bfloat16
F32 = jnp.float32

H = 4
HD = 256
STEP = 5


def normalize(value, gain):
    scale = lax.rsqrt(jnp.mean(value * value, axis=-1, keepdims=True) + 1e-06)
    return value * scale * (1.0 + gain)


def rotate(value, angles):
    half = value.shape[-1] // 2
    first = value[..., :half]
    second = value[..., half:]
    cosine = jnp.cos(angles)
    sine = jnp.sin(angles)
    return jnp.concatenate(
        [first * cosine - second * sine, second * cosine + first * sine], axis=-1
    )


def rope_angles(segments, first, rows):
    own = lax.dynamic_slice_in_dim(segments, first, rows, 0)
    starts = jnp.sum((segments[None, :] < own[:, None]).astype(jnp.int32), axis=1)
    offset = (first + jnp.arange(rows, dtype=jnp.int32) - starts).astype(jnp.float32)
    inverse = jnp.exp(-jnp.log(1000000.0) * (2.0 * jnp.arange(HD // 2, dtype=jnp.float32)) / HD)
    return offset[:, None] * inverse[None, :]


def contract_last(left, right):
    return lax.dot_general(
        left, right, (((1,), (1,)), ((), ())), preferred_element_type=jnp.float32
    )


def contract_first(left, right):
    return lax.dot_general(
        left, right, (((0,), (0,)), ((), ())), preferred_element_type=jnp.float32
    )


def activate(gate_up):
    half = gate_up.shape[-1] // 2
    return jax.nn.gelu(gate_up[:, :half], approximate=True) * gate_up[:, half:]


def adamw(weight, grad, first, second):
    first_new = 0.9 * first + 0.1 * grad
    second_new = 0.95 * second + 0.05 * grad * grad
    first_hat = first_new / (1.0 - 0.9**STEP)
    second_hat = second_new / (1.0 - 0.95**STEP)
    weight_new = weight - 0.03 * (first_hat / (jnp.sqrt(second_hat) + 1e-08) + 0.1 * weight)
    return (weight_new, first_new, second_new)


def gather_weights_body(
    tokens,
    cotangent,
    segments,
    qkv_weight,
    out_weight,
    gate_up_weight,
    down_weight,
    gains,
    qkv_first,
    out_first,
    gate_up_first,
    down_first,
    gains_first,
    qkv_second,
    out_second,
    gate_up_second,
    down_second,
    gains_second,
):
    rows = tokens.shape[1]
    width = tokens.shape[2]
    length = segments.shape[1]
    query_width = H * HD
    scale = HD ** (-0.5)
    reach = lax.axis_size("ctx") // 2 + 1
    front = reach * rows
    window = front + rows
    qkv_full, out_full, gains_full = (
        lax.all_gather(qkv_weight.astype(jnp.bfloat16), ("ctx", "fsdp"), axis=0, tiled=True),
        lax.all_gather(out_weight.astype(jnp.bfloat16), ("ctx", "fsdp"), axis=0, tiled=True),
        lax.all_gather(gains.astype(jnp.bfloat16), ("ctx", "fsdp"), axis=0, tiled=True),
    )
    gain_all = gains_full.astype(jnp.float32)
    gain_input = gain_all[:width]
    gain_attend = gain_all[width : 2 * width]
    gain_pre = gain_all[2 * width : 3 * width]
    gain_post = gain_all[3 * width : 4 * width]
    gain_query = gain_all[4 * width : 4 * width + HD]
    gain_key = gain_all[4 * width + HD :]
    first_row = lax.axis_index("ctx") * rows
    sequence_ids = segments[0]
    angles = rope_angles(sequence_ids, first_row, rows)
    query_ids = lax.dynamic_slice_in_dim(sequence_ids, first_row, rows, 0)
    query_pos = first_row + jnp.arange(rows, dtype=jnp.int32)
    window_pos = first_row - front + jnp.arange(window, dtype=jnp.int32)
    padded_ids = jnp.concatenate([jnp.full((front,), -1, dtype=jnp.int32), sequence_ids])
    window_ids = lax.dynamic_slice_in_dim(padded_ids, first_row, window, 0)
    allowed = (window_pos[None, :] <= query_pos[:, None]) & (
        window_ids[None, :] == query_ids[:, None]
    )
    allowed = allowed[:, None, :]
    x_rows = tokens[0].astype(jnp.float32)
    normed, input_back = jax.vjp(normalize, x_rows, gain_input)
    normed_low = normed.astype(jnp.bfloat16)
    projected = contract_last(normed_low, qkv_full)
    proj_query = projected[:, :query_width].reshape(rows, H, HD)
    proj_key = projected[:, query_width : query_width + HD]
    proj_value = projected[:, query_width + HD :]

    def query_key(part_query, part_key, query_gain, key_gain):
        return (
            rotate(normalize(part_query, query_gain), angles[:, None, :]),
            rotate(normalize(part_key, key_gain), angles),
        )

    (rotated_query, rotated_key), rotate_back = jax.vjp(
        query_key, proj_query, proj_key, gain_query, gain_key
    )
    query = rotated_query.astype(jnp.bfloat16)
    key_low = rotated_key.astype(jnp.bfloat16)
    value_low = proj_value.astype(jnp.bfloat16)
    keys_all, values_all = (
        lax.all_gather(key_low, "ctx", axis=0, tiled=True),
        lax.all_gather(value_low, "ctx", axis=0, tiled=True),
    )
    blank = jnp.zeros((front, HD), jnp.bfloat16)
    keys = lax.dynamic_slice_in_dim(jnp.concatenate([blank, keys_all]), first_row, window, 0)
    values = lax.dynamic_slice_in_dim(jnp.concatenate([blank, values_all]), first_row, window, 0)
    scores = jnp.einsum("thd,ld->thl", query, keys, preferred_element_type=jnp.float32) * scale
    masked = jnp.where(allowed, scores, -1e30)
    largest = jnp.max(masked, axis=-1, keepdims=True)
    log_total = largest + jnp.log(jnp.sum(jnp.exp(masked - largest), axis=-1, keepdims=True))
    probs_low = jnp.exp(masked - log_total).astype(jnp.bfloat16)
    attended = jnp.einsum("thl,ld->thd", probs_low, values, preferred_element_type=jnp.float32)
    attended = attended.reshape(rows, query_width).astype(jnp.bfloat16)
    branch = jnp.dot(attended, out_full, preferred_element_type=jnp.float32)
    branch_normed, attend_back = jax.vjp(normalize, branch, gain_attend)
    hidden = x_rows + branch_normed
    gate_up_full, down_full = (
        lax.all_gather(gate_up_weight.astype(jnp.bfloat16), ("ctx", "fsdp"), axis=0, tiled=True),
        lax.all_gather(down_weight.astype(jnp.bfloat16), ("ctx", "fsdp"), axis=0, tiled=True),
    )
    hidden_normed, pre_back = jax.vjp(normalize, hidden, gain_pre)
    hidden_low = hidden_normed.astype(jnp.bfloat16)
    gate_up = contract_last(hidden_low, gate_up_full)
    mixed, mix_back = jax.vjp(activate, gate_up)
    mixed_low = mixed.astype(jnp.bfloat16)
    down = jnp.dot(mixed_low, down_full, preferred_element_type=jnp.float32)
    down_normed, post_back = jax.vjp(normalize, down, gain_post)
    output = (hidden + down_normed).astype(jnp.bfloat16)
    gate_up_back, down_back = (
        lax.all_gather(gate_up_weight.astype(jnp.bfloat16), ("ctx", "fsdp"), axis=0, tiled=True),
        lax.all_gather(down_weight.astype(jnp.bfloat16), ("ctx", "fsdp"), axis=0, tiled=True),
    )
    grad_rows = cotangent[0].astype(jnp.float32)
    grad_down, grad_gain_post = post_back(grad_rows)
    grad_down_low = grad_down.astype(jnp.bfloat16)
    down_grad = contract_first(mixed_low, grad_down_low)
    grad_mixed = contract_last(grad_down_low, down_back)
    (grad_gate_up,) = mix_back(grad_mixed)
    grad_gate_up_low = grad_gate_up.astype(jnp.bfloat16)
    gate_up_grad = contract_first(grad_gate_up_low, hidden_low)
    grad_hidden_low = jnp.dot(grad_gate_up_low, gate_up_back, preferred_element_type=jnp.float32)
    grad_from_pre, grad_gain_pre = pre_back(grad_hidden_low)
    grad_hidden = grad_rows + grad_from_pre
    gate_up_part, down_part = (
        lax.psum_scatter(gate_up_grad, ("ctx", "fsdp"), scatter_dimension=0, tiled=True),
        lax.psum_scatter(down_grad, ("ctx", "fsdp"), scatter_dimension=0, tiled=True),
    )
    qkv_back, out_back = (
        lax.all_gather(qkv_weight.astype(jnp.bfloat16), ("ctx", "fsdp"), axis=0, tiled=True),
        lax.all_gather(out_weight.astype(jnp.bfloat16), ("ctx", "fsdp"), axis=0, tiled=True),
    )
    grad_branch, grad_gain_attend = attend_back(grad_hidden)
    grad_branch_low = grad_branch.astype(jnp.bfloat16)
    out_grad = contract_first(attended, grad_branch_low)
    grad_attended = (
        contract_last(grad_branch_low, out_back).astype(jnp.bfloat16).reshape(rows, H, HD)
    )
    scores_again = (
        jnp.einsum("thd,ld->thl", query, keys, preferred_element_type=jnp.float32) * scale
    )
    probs = jnp.exp(jnp.where(allowed, scores_again, -1e30) - log_total)
    grad_probs = jnp.einsum(
        "thd,ld->thl", grad_attended, values, preferred_element_type=jnp.float32
    )
    row_term = jnp.sum(probs * grad_probs, axis=-1, keepdims=True)
    grad_scores = (probs * (grad_probs - row_term)).astype(jnp.bfloat16)
    grad_query = (
        jnp.einsum("thl,ld->thd", grad_scores, keys, preferred_element_type=jnp.float32) * scale
    )
    grad_keys = (
        jnp.einsum("thl,thd->ld", grad_scores, query, preferred_element_type=jnp.float32) * scale
    )
    grad_values = jnp.einsum(
        "thl,thd->ld", probs.astype(jnp.bfloat16), grad_attended, preferred_element_type=jnp.float32
    )
    empty = jnp.zeros((front + length, HD), jnp.float32)
    keys_spread = lax.dynamic_update_slice_in_dim(empty, grad_keys, first_row, 0)[front:]
    values_spread = lax.dynamic_update_slice_in_dim(empty, grad_values, first_row, 0)[front:]
    grad_key, grad_value = (
        lax.psum_scatter(keys_spread, "ctx", scatter_dimension=0, tiled=True),
        lax.psum_scatter(values_spread, "ctx", scatter_dimension=0, tiled=True),
    )
    grad_proj_query, grad_proj_key, grad_gain_query, grad_gain_key = rotate_back(
        (grad_query, grad_key)
    )
    grad_projected = jnp.concatenate(
        [grad_proj_query.reshape(rows, query_width), grad_proj_key, grad_value], axis=1
    ).astype(jnp.bfloat16)
    qkv_grad = contract_first(grad_projected, normed_low)
    grad_normed = jnp.dot(grad_projected, qkv_back, preferred_element_type=jnp.float32)
    grad_from_input, grad_gain_input = input_back(grad_normed)
    input_grad = grad_hidden + grad_from_input
    gains_grad = jnp.concatenate(
        [
            grad_gain_input,
            grad_gain_attend,
            grad_gain_pre,
            grad_gain_post,
            grad_gain_query,
            grad_gain_key,
        ]
    )
    qkv_part, out_part, gains_part = (
        lax.psum_scatter(qkv_grad, ("ctx", "fsdp"), scatter_dimension=0, tiled=True),
        lax.psum_scatter(out_grad, ("ctx", "fsdp"), scatter_dimension=0, tiled=True),
        lax.psum_scatter(gains_grad, ("ctx", "fsdp"), scatter_dimension=0, tiled=True),
    )
    qkv_total, out_total, gate_up_total, down_total, gains_total = (
        lax.psum(qkv_part.astype(jnp.bfloat16), "dp").astype(jnp.float32),
        lax.psum(out_part.astype(jnp.bfloat16), "dp").astype(jnp.float32),
        lax.psum(gate_up_part.astype(jnp.bfloat16), "dp").astype(jnp.float32),
        lax.psum(down_part.astype(jnp.bfloat16), "dp").astype(jnp.float32),
        lax.psum(gains_part.astype(jnp.bfloat16), "dp").astype(jnp.float32),
    )
    qkv_new, qkv_first_new, qkv_second_new = adamw(qkv_weight, qkv_total, qkv_first, qkv_second)
    out_new, out_first_new, out_second_new = adamw(out_weight, out_total, out_first, out_second)
    gate_up_new, gate_up_first_new, gate_up_second_new = adamw(
        gate_up_weight, gate_up_total, gate_up_first, gate_up_second
    )
    down_new, down_first_new, down_second_new = adamw(
        down_weight, down_total, down_first, down_second
    )
    gains_new, gains_first_new, gains_second_new = adamw(
        gains, gains_total, gains_first, gains_second
    )
    return (
        output[None],
        input_grad[None],
        qkv_total,
        out_total,
        gate_up_total,
        down_total,
        gains_total,
        qkv_new,
        out_new,
        gate_up_new,
        down_new,
        gains_new,
        qkv_first_new,
        out_first_new,
        gate_up_first_new,
        down_first_new,
        gains_first_new,
        qkv_second_new,
        out_second_new,
        gate_up_second_new,
        down_second_new,
        gains_second_new,
    )


def place():
    return lax.axis_index("dp"), lax.axis_index("ctx"), lax.axis_index("fsdp")


def greet(devices, extra=0):
    barrier = pltpu.get_barrier_semaphore()
    for device in devices:
        pl.semaphore_signal(barrier, inc=1, device_id=device, device_id_type=MESH)
    pl.semaphore_wait(barrier, len(devices))


def remote(source, target, send, recv, device):
    return pltpu.make_async_remote_copy(
        src_ref=source,
        dst_ref=target,
        send_sem=send,
        recv_sem=recv,
        device_id=device,
        device_id_type=MESH,
    )


def layers_of(z, y, count, dp, x):
    return [(dp, lax.rem(z + step, count) * 2 + y, x) for step in range(1, count)]


def gather_kernel(wq, wo, gn, wgu, wd, qkv, out, gain, gu, dn, send, recv, local, send_f, recv_f):
    dp, ctx, x = place()
    layers = qkv.shape[0]
    z, y = ctx // 2, ctx % 2
    cube = ctx // 4
    sibling = (1 - dp, ctx, x)
    y2, x2 = jnp.where(dp == 0, 1 - y, y), jnp.where(dp == 0, x, 1 - x)
    y3, x3 = jnp.where(dp == 0, y, 1 - y), jnp.where(dp == 0, 1 - x, x)
    second = (dp, z * 2 + y2, x2)
    third = (dp, z * 2 + y3, x3)
    others = layers_of(z, y, layers, dp, x)
    down_to = (x, ctx // 2 + 4 * dp, ctx % 2)
    group = (ctx % 4) * 2 + x
    down_from = (cube, group, dp)
    stays = (dp == x) & (ctx == down_to[1]) & (x == ctx % 2)
    barrier = pltpu.get_barrier_semaphore()
    for device in others + [second, third, sibling]:
        pl.semaphore_signal(barrier, inc=1, device_id=device, device_id_type=MESH)

    @pl.when(jnp.logical_not(stays))
    def _():
        for device in (down_to, down_from):
            pl.semaphore_signal(barrier, inc=1, device_id=device, device_id_type=MESH)

    pl.semaphore_wait(barrier, jnp.where(stays, layers + 2, layers + 4))

    triples = ((wq, qkv), (gn, gain), (wo, out))
    started = []

    def start(copy):
        copy.start()
        started.append(copy)
        return copy

    own, first = [], []
    for t, (part, full) in enumerate(triples):
        copy = pltpu.make_async_copy(part.at[dp], full.at[z, y, x, dp], local.at[t])
        copy.start()
        own.append(copy)
        first.append(
            [
                start(remote(part.at[dp], full.at[z, y, x, dp], send.at[t, i], recv.at[t, i], device))
                for i, device in enumerate(others)
            ]
        )
    gu_own = pltpu.make_async_copy(wgu, gu.at[cube], local.at[3])
    gu_own.start()
    gu_cross = start(
        remote(wgu.at[dp], gu.at[cube, dp], send_f.at[0], recv_f.at[0], (dp, (ctx + 4) % 8, x))
    )
    down_local = pltpu.make_async_copy(wd, dn.at[x], recv_f.at[1])
    down_move = remote(wd, dn.at[x], send_f.at[1], recv_f.at[1], down_to)

    @pl.when(stays)
    def _():
        down_local.start()

    @pl.when(jnp.logical_not(stays))
    def _():
        down_move.start()

    line, third_own, sib = [], [], []
    for t, (_, full) in enumerate(triples):
        own[t].wait()
        for copy in first[t]:
            copy.wait_recv()
        mine = full.at[:, y, x, dp]
        line.append(start(remote(mine, mine, send.at[t, 3], recv.at[t, 3], second)))
        third_own.append(start(remote(mine, mine, send.at[t, 4], recv.at[t, 4], third)))
        sib.append(start(remote(mine, mine, send.at[t, 5], recv.at[t, 5], sibling)))
    third_line = []
    for t, (_, full) in enumerate(triples):
        line[t].wait_recv()
        seconds = full.at[:, y2, x2, dp]
        third_line.append(start(remote(seconds, seconds, send.at[t, 6], recv.at[t, 6], third)))
        sib.append(start(remote(seconds, seconds, send.at[t, 7], recv.at[t, 7], sibling)))
    for t, (_, full) in enumerate(triples):
        third_own[t].wait_recv()
        thirds = full.at[:, y3, x3, dp]
        sib.append(start(remote(thirds, thirds, send.at[t, 8], recv.at[t, 8], sibling)))
        third_line[t].wait_recv()
        far = full.at[:, 1 - y, 1 - x, dp]
        sib.append(start(remote(far, far, send.at[t, 9], recv.at[t, 9], sibling)))
    gu_cross.wait_recv()
    crossed = gu.at[1 - cube, dp]
    sib.append(start(remote(crossed, crossed, send_f.at[2], recv_f.at[2], sibling)))
    down_local.wait()
    landed = dn.at[dp]
    sib.append(start(remote(landed, landed, send_f.at[3], recv_f.at[3], sibling)))
    for copy in sib:
        copy.wait_recv()
    gu_own.wait()
    for copy in started:
        copy.wait_send()

    @pl.when(jnp.logical_not(stays))
    def _():
        down_move.wait_send()


def gather_weights(wq, wo, gn, wgu, wd, layers):
    lead = (layers, 2, 2)

    def full(part):
        return jax.ShapeDtypeStruct(lead + part.shape, part.dtype)

    return pl.pallas_call(
        gather_kernel,
        out_shape=(
            full(wq),
            full(wo),
            full(gn),
            jax.ShapeDtypeStruct((2,) + wgu.shape, BF),
            jax.ShapeDtypeStruct((2,) + wd.shape, BF),
        ),
        in_specs=[ANY] * 5,
        out_specs=(ANY,) * 5,
        scratch_shapes=[
            pltpu.SemaphoreType.DMA((3, 10)),
            pltpu.SemaphoreType.DMA((3, 10)),
            pltpu.SemaphoreType.DMA((4,)),
            pltpu.SemaphoreType.DMA((4,)),
            pltpu.SemaphoreType.DMA((4,)),
        ],
        compiler_params=pltpu.CompilerParams(collective_id=0, has_side_effects=True),
    )(wq, wo, gn, wgu, wd)


def keys_kernel(part, full, send, recv, local):
    dp, ctx, x = place()
    layers = full.shape[0]
    z, y = ctx // 2, ctx % 2
    others = layers_of(z, y, layers, dp, x)
    beside = (dp, z * 2 + 1 - y, x)
    greet(others + [beside])
    own = pltpu.make_async_copy(part, full.at[z, y], local.at[0])
    own.start()
    copies = [
        remote(part, full.at[z, y], send.at[i], recv.at[i], device)
        for i, device in enumerate(others)
    ]
    for copy in copies:
        copy.start()
    own.wait()
    for copy in copies:
        copy.wait_recv()
    line = remote(full.at[:, y], full.at[:, y], send.at[3], recv.at[3], beside)
    line.start()
    line.wait()
    for copy in copies:
        copy.wait_send()


def gather_keys(part, layers):
    return pl.pallas_call(
        keys_kernel,
        out_shape=jax.ShapeDtypeStruct((layers, 2) + part.shape, part.dtype),
        in_specs=[VMEM],
        out_specs=VMEM,
        scratch_shapes=[
            pltpu.SemaphoreType.DMA((4,)),
            pltpu.SemaphoreType.DMA((4,)),
            pltpu.SemaphoreType.DMA((1,)),
        ],
        compiler_params=pltpu.CompilerParams(collective_id=1, has_side_effects=True),
    )(part)


def scatter_keys_kernel(part, total, beside_in, sums, layer_in, send, recv):
    dp, ctx, x = place()
    layers = part.shape[0]
    z, y = ctx // 2, ctx % 2
    others = layers_of(z, y, layers, dp, x)
    beside = (dp, z * 2 + 1 - y, x)
    greet(others + [beside])
    line = remote(part.at[:, 1 - y], beside_in, send.at[3], recv.at[3], beside)
    line.start()
    line.wait_recv()
    for i in range(layers):
        sums[i] = (part[i, y].astype(F32) + beside_in[i].astype(F32)).astype(BF)
    copies = [
        remote(sums.at[lax.rem(z + i + 1, layers)], layer_in.at[i], send.at[i], recv.at[i], device)
        for i, device in enumerate(others)
    ]
    for copy in copies:
        copy.start()
    for copy in copies:
        copy.wait_recv()
    total[...] = sums[z].astype(F32)
    for i in range(layers - 1):
        total[...] += layer_in[i].astype(F32)
    line.wait_send()
    for copy in copies:
        copy.wait_send()


def scatter_keys(part):
    layers, _, rows, width = part.shape
    return pl.pallas_call(
        scatter_keys_kernel,
        out_shape=jax.ShapeDtypeStruct((rows, width), F32),
        in_specs=[VMEM],
        out_specs=VMEM,
        scratch_shapes=[
            pltpu.VMEM((layers, rows, width), BF),
            pltpu.VMEM((layers, rows, width), BF),
            pltpu.VMEM((layers - 1, rows, width), BF),
            pltpu.SemaphoreType.DMA((4,)),
            pltpu.SemaphoreType.DMA((4,)),
        ],
        compiler_params=pltpu.CompilerParams(collective_id=2, has_side_effects=True),
    )(part)


def cube_parts(rows):
    third = -(-rows // 48) * 16
    return ((0, third), (third, third), (2 * third, rows - 2 * third))


class Cube:
    def __init__(self, rows, gather_send, gather_recv, scatter_send, scatter_recv):
        dp, ctx, x = place()
        self.me = (ctx % 4) * 2 + x
        self.masks = (1, 2, 4)
        self.peers = (
            (dp, ctx, 1 - x),
            (dp, ctx + 1 - 2 * (ctx % 2), x),
            (dp, ctx + 2 - 4 * (ctx // 2 % 2), x),
        )
        self.parts = cube_parts(rows)
        self.sems = (gather_send, gather_recv, scatter_send, scatter_recv)

    def block(self, mask):
        me, result = self.me, 0
        for bit in (1, 2, 4):
            own = me // bit % 2
            result = result + bit * (1 - own if mask & bit else own)
        return result

    def gather(self, buf):
        send, recv = self.sems[:2]

        def copy(p, index, mask, dim):
            start, size = self.parts[p]
            ref = buf.at[self.block(mask), pl.ds(start, size)]
            return remote(ref, ref, send.at[p, index], recv.at[p, index], self.peers[dim])

        orders = [(p, (p + 1) % 3, (p + 2) % 3) for p in range(3)]
        sent = {}

        def go(p, index, mask, dim):
            sent[p, index] = copy(p, index, mask, dim)
            sent[p, index].start()

        for p, (a, b, c) in enumerate(orders):
            go(p, 0, 0, a)
        for p, (a, b, c) in enumerate(orders):
            go(p, 1, 0, b)
        for p, (a, b, c) in enumerate(orders):
            go(p, 3, 0, c)
        for p, (a, b, c) in enumerate(orders):
            sent[p, 0].wait_recv()
            go(p, 2, self.masks[a], b)
            go(p, 4, self.masks[a], c)
        for p, (a, b, c) in enumerate(orders):
            sent[p, 1].wait_recv()
            go(p, 5, self.masks[b], c)
            sent[p, 2].wait_recv()
            go(p, 6, self.masks[a] | self.masks[b], c)
        for index in (3, 4, 5, 6):
            for p in range(3):
                sent[p, index].wait_recv()
        for item in sent.values():
            item.wait_send()

    def scatter(self, buf, one, two, three, beside=None):
        send, recv = self.sems[2:]
        orders = [(p, (p + 1) % 3, (p + 2) % 3) for p in range(3)]
        sent = {}

        def go(p, index, mask, slot, dim):
            start, size = self.parts[p]
            rows = pl.ds(start, size)
            sent[p, index] = remote(
                buf.at[self.block(mask), rows],
                slot.at[rows],
                send.at[p, index],
                recv.at[p, index],
                self.peers[dim],
            )
            sent[p, index].start()

        def add(p, mask, slot):
            start, size = self.parts[p]
            rows = pl.ds(start, size)
            j = self.block(mask)
            buf[j, rows] = (buf[j, rows].astype(F32) + slot[rows].astype(F32)).astype(BF)

        for index in range(4):
            for p, (a, b, c) in enumerate(orders):
                ma, mb, mc = (self.masks[d] for d in (a, b, c))
                mask = (mb, mb | ma, ma, 0)[index]
                go(p, index, mc | mask, one.at[index], c)
        if beside is not None:
            beside()
        for index in range(2):
            for p, (a, b, c) in enumerate(orders):
                ma, mb = self.masks[a], self.masks[b]
                mask = (ma, 0)[index]
                sent[p, 1 - index].wait_recv()
                add(p, mb | mask, one.at[1 - index])
                go(p, 4 + index, mb | mask, two.at[index], b)
        for p, (a, b, c) in enumerate(orders):
            ma = self.masks[a]
            sent[p, 2].wait_recv()
            add(p, ma, one.at[2])
            sent[p, 4].wait_recv()
            add(p, ma, two.at[0])
            go(p, 6, ma, three, a)
        for p in range(3):
            sent[p, 3].wait_recv()
            add(p, 0, one.at[3])
            sent[p, 5].wait_recv()
            add(p, 0, two.at[1])
            sent[p, 6].wait_recv()
        for item in sent.values():
            item.wait_send()


def norm_scale(value):
    return lax.rsqrt(jnp.mean(value * value, axis=-1, keepdims=True) + 1e-06)


def norm_back(value, scale, gained):
    inner = jnp.mean(gained * value, axis=-1, keepdims=True)
    return scale * gained - value * (scale * scale * scale * inner)


ROOT = 0.7978845608028654


def gelu_parts(v):
    t = jnp.tanh(ROOT * (v + 0.044715 * (v * v * v)))
    value = 0.5 * v * (1.0 + t)
    slope = 0.5 * (1.0 + t) + 0.5 * v * (1.0 - t * t) * (ROOT * (1.0 + 0.134145 * (v * v)))
    return value, slope


def feed_kernel(
    hidden,
    cot,
    gains,
    gu_in,
    dn_in,
    output,
    grad_hidden,
    grad_gains,
    gu_grad,
    dn_grad,
    wg,
    wu,
    wd,
    acts,
    downs,
    gate,
    up,
    mixed,
    sums,
    one,
    two,
    three,
    gsend,
    grecv,
    ssend,
    srecv,
    local,
):
    rows, width = hidden.shape
    units = gu_in.shape[1] * gu_in.shape[2]
    half = gu_in.shape[2]
    wide = wg.shape[0]
    cube = Cube(rows, gsend, grecv, ssend, srecv)
    loads = []
    for i, (source, target) in enumerate(
        ((gu_in.at[0], wg), (gu_in.at[1], wu), (dn_in, wd))
    ):
        for h in range(2):
            loads.append(
                pltpu.make_async_copy(
                    source.at[h], target.at[pl.ds(h * half, half)], local.at[i, h]
                )
            )
            loads[-1].start()
    for target in (wg, wu, wd):
        target[units:, :] = jnp.zeros((wide - units, width), BF)
    greet(cube.peers)
    me = cube.me
    value = hidden[...]
    pre_scale = norm_scale(value)
    pre_gain = 1.0 + gains[0:1, :]
    acts[me] = (value * pre_scale * pre_gain).astype(BF)
    cube.gather(acts)
    for load in loads:
        load.wait()

    def forward(j, carry):
        a = acts[j]
        g = contract_last(a, wg[...])
        u = contract_last(a, wu[...])
        gate[j] = g
        up[j] = u
        m = (gelu_parts(g)[0] * u).astype(BF)
        mixed[j] = m
        sums[j] = jnp.dot(m, wd[...], preferred_element_type=F32).astype(BF)
        return carry

    lax.fori_loop(0, 8, forward, 0)
    cube.scatter(sums, one, two, three)
    down = sums[me].astype(F32) + three[...].astype(F32)
    scale = norm_scale(down)
    post_gain = 1.0 + gains[1:2, :]
    normal = down * scale
    output[...] = (value + normal * post_gain).astype(BF)
    dy = cot[...].astype(F32)
    grad_gains[1:2, :] = jnp.sum(dy * normal, axis=0, keepdims=True)
    downs[me] = norm_back(down, scale, dy * post_gain).astype(BF)
    cube.gather(downs)

    def backward(j, carry):
        d = contract_last(downs[j], wd[...])
        value, slope = gelu_parts(gate[j])
        dg = (d * up[j] * slope).astype(BF)
        du = (d * value).astype(BF)
        gate[j] = dg.astype(F32)
        up[j] = du.astype(F32)
        sums[j] = (
            jnp.dot(dg, wg[...], preferred_element_type=F32)
            + jnp.dot(du, wu[...], preferred_element_type=F32)
        ).astype(BF)
        return carry

    lax.fori_loop(0, 8, backward, 0)

    def weights():
        tokens = 8 * rows
        acts_all = acts[...].reshape(tokens, width)
        downs_all = downs[...].reshape(tokens, width)
        for lo in range(0, wide, 128):
            hi = min(lo + 128, units)
            cut = slice(lo, lo + 128)
            kept = hi - lo
            dg = gate[:, :, cut].reshape(tokens, 128).astype(BF)
            du = up[:, :, cut].reshape(tokens, 128).astype(BF)
            mx = mixed[:, :, cut].reshape(tokens, 128)
            gu_grad[0, lo:hi, :] = contract_first(dg, acts_all)[:kept].astype(BF)
            gu_grad[1, lo:hi, :] = contract_first(du, acts_all)[:kept].astype(BF)
            dn_grad[lo:hi, :] = contract_first(mx, downs_all)[:kept].astype(BF)

    cube.scatter(sums, one, two, three, weights)
    total = sums[me].astype(F32) + three[...].astype(F32)
    grad_gains[0:1, :] = jnp.sum(total * (value * pre_scale), axis=0, keepdims=True)
    grad_hidden[...] = dy + norm_back(value, pre_scale, total * pre_gain)


def feed_forward(hidden, cot, gains, gu, dn):
    rows, width = hidden.shape
    units = gu.shape[1] * gu.shape[2]
    wide = -(-units // 128) * 128
    return pl.pallas_call(
        feed_kernel,
        out_shape=(
            jax.ShapeDtypeStruct((rows, width), BF),
            jax.ShapeDtypeStruct((rows, width), F32),
            jax.ShapeDtypeStruct((2, width), F32),
            jax.ShapeDtypeStruct((2, units, width), BF),
            jax.ShapeDtypeStruct((units, width), BF),
        ),
        in_specs=[VMEM, VMEM, VMEM, ANY, ANY],
        out_specs=(VMEM,) * 5,
        scratch_shapes=[
            pltpu.VMEM((wide, width), BF),
            pltpu.VMEM((wide, width), BF),
            pltpu.VMEM((wide, width), BF),
            pltpu.VMEM((8, rows, width), BF),
            pltpu.VMEM((8, rows, width), BF),
            pltpu.VMEM((8, rows, wide), F32),
            pltpu.VMEM((8, rows, wide), F32),
            pltpu.VMEM((8, rows, wide), BF),
            pltpu.VMEM((8, rows, width), BF),
            pltpu.VMEM((4, rows, width), BF),
            pltpu.VMEM((2, rows, width), BF),
            pltpu.VMEM((rows, width), BF),
            pltpu.SemaphoreType.DMA((3, 7)),
            pltpu.SemaphoreType.DMA((3, 7)),
            pltpu.SemaphoreType.DMA((3, 7)),
            pltpu.SemaphoreType.DMA((3, 7)),
            pltpu.SemaphoreType.DMA((3, 2)),
        ],
        compiler_params=pltpu.CompilerParams(
            collective_id=3, has_side_effects=True, vmem_limit_bytes=60 * 2**20
        ),
    )(hidden, cot, gains, gu, dn)


def reduce_kernel(
    pq,
    po,
    pg,
    pgu,
    pd,
    rq,
    ro,
    rg,
    rgu,
    rd,
    q_in,
    q_sum,
    o_in,
    o_sum,
    q_one,
    o_one,
    q_two,
    o_two,
    q_far,
    o_far,
    g_in,
    g_sum,
    gu_in,
    gu_far,
    d_in,
    d_far,
    send,
    recv,
    send_f,
    recv_f,
    local,
):
    dp, ctx, x = place()
    layers = pq.shape[0]
    z, y = ctx // 2, ctx % 2
    cube = ctx // 4
    sibling = (1 - dp, ctx, x)
    y2, x2 = jnp.where(dp == 0, 1 - y, y), jnp.where(dp == 0, x, 1 - x)
    y3, x3 = jnp.where(dp == 0, y, 1 - y), jnp.where(dp == 0, 1 - x, x)
    mine2, mine3 = jnp.where(dp == 0, y, x), jnp.where(dp == 0, x, y)
    second = (dp, z * 2 + y2, x2)
    third = (dp, z * 2 + y3, x3)
    others = layers_of(z, y, layers, dp, x)
    group = (ctx % 4) * 2 + x
    down_to = (cube, group, dp)
    down_from = (x, ctx // 2 + 4 * dp, ctx % 2)
    stays = (dp == cube) & (ctx == group) & (x == dp)
    barrier = pltpu.get_barrier_semaphore()
    for device in others + [second, third, sibling]:
        pl.semaphore_signal(barrier, inc=1, device_id=device, device_id_type=MESH)

    @pl.when(jnp.logical_not(stays))
    def _():
        for device in (down_to, down_from):
            pl.semaphore_signal(barrier, inc=1, device_id=device, device_id_type=MESH)

    pl.semaphore_wait(barrier, jnp.where(stays, layers + 2, layers + 4))

    started = []

    def start(copy):
        copy.start()
        started.append(copy)
        return copy

    gu_swap = start(remote(pgu.at[:, 1 - dp], gu_in, send_f.at[0], recv_f.at[0], sibling))
    d_swap = start(remote(pd.at[1 - dp], d_in, send_f.at[1], recv_f.at[1], sibling))
    swaps = [
        start(remote(pq.at[:, :, :, 1 - dp], q_in, send.at[0, 0], recv.at[0, 0], sibling)),
        start(remote(po.at[:, :, :, 1 - dp], o_in, send.at[1, 0], recv.at[1, 0], sibling)),
    ]
    gains0 = start(remote(pg, g_in.at[0], send_f.at[2], recv_f.at[2], sibling))
    gu_swap.wait_recv()
    for q in range(2):
        gu_in[q] = (gu_in[q].astype(F32) + pgu[q, dp].astype(F32)).astype(BF)
    gu_cross = start(
        remote(
            gu_in.at[1 - cube], gu_far, send_f.at[3], recv_f.at[3], (dp, (ctx + 4) % 8, x)
        )
    )
    d_swap.wait_recv()
    d_in[...] = (d_in[...].astype(F32) + pd[dp].astype(F32)).astype(BF)
    d_local = pltpu.make_async_copy(d_in, d_far.at[cube], recv_f.at[4])
    d_move = remote(d_in, d_far.at[cube], send_f.at[4], recv_f.at[4], down_to)

    @pl.when(stays)
    def _():
        d_local.start()

    @pl.when(jnp.logical_not(stays))
    def _():
        d_move.start()

    gains0.wait_recv()
    g_sum[0] = pg[...] + g_in[0]
    gains1 = start(remote(g_sum.at[0], g_in.at[1], send_f.at[5], recv_f.at[5], (dp, ctx, 1 - x)))
    sets = (
        (pq, q_in, q_sum, q_one, q_two, q_far, rq),
        (po, o_in, o_sum, o_one, o_two, o_far, ro),
    )
    ones = []
    for t, (part, came, total, _, _, _, _) in enumerate(sets):
        swaps[t].wait_recv()
        for i in range(layers):
            for a in range(2):
                for b in range(2):
                    yy, xx = jnp.where(dp == 0, a, b), jnp.where(dp == 0, b, a)
                    total[a, b, i] = (
                        part[i, yy, xx, dp].astype(F32) + came[i, yy, xx].astype(F32)
                    ).astype(BF)
        ones.append(
            start(
                remote(
                    total.at[:, 1 - mine3], sets[t][3], send.at[t, 1], recv.at[t, 1], third
                )
            )
        )
    gains1.wait_recv()
    g_sum[1] = g_sum[0] + g_in[1]
    gains2 = start(
        remote(g_sum.at[1], g_in.at[2], send_f.at[6], recv_f.at[6], (dp, z * 2 + 1 - y, x))
    )
    twos = []
    for t, (_, _, total, first, second_in, _, _) in enumerate(sets):
        ones[t].wait_recv()
        for i in range(layers):
            for a in range(2):
                total[a, mine3, i] = (
                    total[a, mine3, i].astype(F32) + first[a, i].astype(F32)
                ).astype(BF)
        twos.append(
            start(
                remote(
                    total.at[1 - mine2, mine3],
                    second_in,
                    send.at[t, 2],
                    recv.at[t, 2],
                    second,
                )
            )
        )
    gains2.wait_recv()
    g_sum[2] = g_sum[1] + g_in[2]
    gains3 = [
        start(remote(g_sum.at[2], g_in.at[3 + z], send_f.at[8 + i], recv_f.at[8 + i], device))
        for i, device in enumerate(others)
    ]
    own_gains = pltpu.make_async_copy(g_sum.at[2], g_in.at[3 + z], local.at[0])
    own_gains.start()
    fars = []
    for t, (_, _, total, _, second_in, far, _) in enumerate(sets):
        twos[t].wait_recv()
        for i in range(layers):
            total[mine2, mine3, i] = (
                total[mine2, mine3, i].astype(F32) + second_in[i].astype(F32)
            ).astype(BF)
        fars.append(
            [
                start(
                    remote(
                        total.at[mine2, mine3, lax.rem(z + i + 1, layers)],
                        far.at[i],
                        send.at[t, 3 + i],
                        recv.at[t, 3 + i],
                        device,
                    )
                )
                for i, device in enumerate(others)
            ]
        )
    last = []
    for t, (_, _, total, _, _, far, result) in enumerate(sets):
        value = total[mine2, mine3, z].astype(F32)
        for i in range(layers - 1):
            fars[t][i].wait_recv()
            value = value + far[i].astype(F32)
        result[dp] = value.astype(BF)
        last.append(start(remote(result.at[dp], result.at[dp], send.at[t, 6], recv.at[t, 6], sibling)))
    own_gains.wait()
    for copy in gains3:
        copy.wait_recv()
    value = g_in[3]
    for i in range(1, layers):
        value = value + g_in[3 + i]
    rg[...] = value
    gu_cross.wait_recv()
    rgu[dp] = (gu_in[cube].astype(F32) + gu_far[...].astype(F32)).astype(BF)
    last.append(start(remote(rgu.at[dp], rgu.at[dp], send_f.at[11], recv_f.at[11], sibling)))
    d_local.wait()
    landed = d_far.at[dp]
    d_last = start(remote(landed, landed, send_f.at[12], recv_f.at[12], sibling))
    d_last.wait_recv()
    rd[...] = (d_far[0].astype(F32) + d_far[1].astype(F32)).astype(BF)
    for copy in last:
        copy.wait_recv()
    for copy in started:
        copy.wait_send()

    @pl.when(jnp.logical_not(stays))
    def _():
        d_move.wait_send()


def reduce_grads(pq, po, pg, pgu, pd):
    layers = pq.shape[0]
    hq, width = pq.shape[-2:]
    ho = po.shape[-2]
    hgu = pgu.shape[-2]
    down_rows = pd.shape[-2]
    return pl.pallas_call(
        reduce_kernel,
        out_shape=(
            jax.ShapeDtypeStruct((2, hq, width), BF),
            jax.ShapeDtypeStruct((2, ho, width), BF),
            jax.ShapeDtypeStruct(pg.shape, F32),
            jax.ShapeDtypeStruct((2, hgu, width), BF),
            jax.ShapeDtypeStruct((down_rows, width), BF),
        ),
        in_specs=[VMEM] * 5,
        out_specs=(VMEM,) * 5,
        scratch_shapes=[
            pltpu.VMEM((layers, 2, 2, hq, width), BF),
            pltpu.VMEM((2, 2, layers, hq, width), BF),
            pltpu.VMEM((layers, 2, 2, ho, width), BF),
            pltpu.VMEM((2, 2, layers, ho, width), BF),
            pltpu.VMEM((2, layers, hq, width), BF),
            pltpu.VMEM((2, layers, ho, width), BF),
            pltpu.VMEM((layers, hq, width), BF),
            pltpu.VMEM((layers, ho, width), BF),
            pltpu.VMEM((layers - 1, hq, width), BF),
            pltpu.VMEM((layers - 1, ho, width), BF),
            pltpu.VMEM((3 + layers,) + pg.shape, F32),
            pltpu.VMEM((3,) + pg.shape, F32),
            pltpu.VMEM((2, hgu, width), BF),
            pltpu.VMEM((hgu, width), BF),
            pltpu.VMEM((down_rows, width), BF),
            pltpu.VMEM((2, down_rows, width), BF),
            pltpu.SemaphoreType.DMA((2, 7)),
            pltpu.SemaphoreType.DMA((2, 7)),
            pltpu.SemaphoreType.DMA((13,)),
            pltpu.SemaphoreType.DMA((13,)),
            pltpu.SemaphoreType.DMA((1,)),
        ],
        compiler_params=pltpu.CompilerParams(
            collective_id=4, has_side_effects=True, vmem_limit_bytes=60 * 2**20
        ),
    )(pq, po, pg, pgu, pd)


def moves_tokens(mesh):
    return mesh.shape["ctx"] == 8 and mesh.shape["fsdp"] == 2 and mesh.shape["dp"] == 2


def move_tokens_body(
    tokens,
    cotangent,
    segments,
    qkv_weight,
    out_weight,
    gate_up_weight,
    down_weight,
    gains,
    qkv_first,
    out_first,
    gate_up_first,
    down_first,
    gains_first,
    qkv_second,
    out_second,
    gate_up_second,
    down_second,
    gains_second,
):
    rows = tokens.shape[1]
    width = tokens.shape[2]
    length = segments.shape[1]
    query_width = H * HD
    scale = HD ** (-0.5)
    layers = lax.axis_size("ctx") // 2
    reach = lax.axis_size("ctx") // 2 + 1
    front = reach * rows
    window = front + rows
    ctx = lax.axis_index("ctx")
    chip = ctx * 2 + lax.axis_index("fsdp")
    own_gains = gains.shape[0]
    gain_rows = -(-own_gains * 4 * layers // 1024) * 8 + 8

    def halves(weight):
        return weight.astype(BF).reshape(2, weight.shape[0] // 2, width)

    gain_part = lax.dynamic_update_slice_in_dim(
        jnp.zeros((gain_rows * 128,), F32),
        gains.astype(BF).astype(F32),
        chip * own_gains,
        0,
    )
    qkv_parts, out_parts, gain_parts, gu, dn = gather_weights(
        halves(qkv_weight),
        halves(out_weight),
        gain_part.reshape(2, gain_rows // 2, 128),
        halves(gate_up_weight),
        down_weight.astype(BF),
        layers,
    )
    qkv_full = qkv_parts.reshape(-1, width)
    out_full = out_parts.reshape(-1, width)
    gain_all = jnp.sum(gain_parts, axis=(0, 1, 2)).reshape(-1)
    gain_input = gain_all[:width]
    gain_attend = gain_all[width : 2 * width]
    gain_pre = gain_all[2 * width : 3 * width]
    gain_post = gain_all[3 * width : 4 * width]
    gain_query = gain_all[4 * width : 4 * width + HD]
    gain_key = gain_all[4 * width + HD : 4 * width + 2 * HD]
    first_row = ctx * rows
    sequence_ids = segments[0]
    query_ids = lax.dynamic_slice_in_dim(sequence_ids, first_row, rows, 0)
    query_pos = first_row + jnp.arange(rows, dtype=jnp.int32)
    angles = rope_angles(sequence_ids, first_row, rows)
    window_pos = first_row - front + jnp.arange(window, dtype=jnp.int32)
    padded_ids = jnp.concatenate([jnp.full((front,), -1, dtype=jnp.int32), sequence_ids])
    window_ids = lax.dynamic_slice_in_dim(padded_ids, first_row, window, 0)
    allowed = (window_pos[None, :] <= query_pos[:, None]) & (
        window_ids[None, :] == query_ids[:, None]
    )
    allowed = allowed[:, None, :]
    x_rows = tokens[0].astype(F32)
    normed, input_back = jax.vjp(normalize, x_rows, gain_input)
    normed_low = normed.astype(BF)
    projected = contract_last(normed_low, qkv_full)
    proj_query = projected[:, :query_width].reshape(rows, H, HD)
    proj_key = projected[:, query_width : query_width + HD]
    proj_value = projected[:, query_width + HD :]

    def query_key(part_query, part_key, query_gain, key_gain):
        return (
            rotate(normalize(part_query, query_gain), angles[:, None, :]),
            rotate(normalize(part_key, key_gain), angles),
        )

    (rotated_query, rotated_key), rotate_back = jax.vjp(
        query_key, proj_query, proj_key, gain_query, gain_key
    )
    query = rotated_query.astype(BF)
    pairs = jnp.concatenate([rotated_key.astype(BF), proj_value.astype(BF)], axis=1)
    pairs_all = gather_keys(pairs, layers).reshape(length, 2 * HD)
    blank = jnp.zeros((front, 2 * HD), BF)
    pairs_near = lax.dynamic_slice_in_dim(
        jnp.concatenate([blank, pairs_all]), first_row, window, 0
    )
    keys, values = pairs_near[:, :HD], pairs_near[:, HD:]
    scores = jnp.einsum("thd,ld->thl", query, keys, preferred_element_type=F32) * scale
    masked = jnp.where(allowed, scores, -1e30)
    largest = jnp.max(masked, axis=-1, keepdims=True)
    log_total = largest + jnp.log(jnp.sum(jnp.exp(masked - largest), axis=-1, keepdims=True))
    probs = jnp.exp(masked - log_total)
    probs_low = probs.astype(BF)
    attended = jnp.einsum("thl,ld->thd", probs_low, values, preferred_element_type=F32)
    attended = attended.reshape(rows, query_width).astype(BF)
    branch = jnp.dot(attended, out_full, preferred_element_type=F32)
    branch_normed, attend_back = jax.vjp(normalize, branch, gain_attend)
    hidden = x_rows + branch_normed
    output, grad_hidden, grad_gain_feed, gate_up_grad, down_grad = feed_forward(
        hidden, cotangent[0], jnp.stack([gain_pre, gain_post]), gu, dn
    )
    grad_branch, grad_gain_attend = attend_back(grad_hidden)
    grad_branch_low = grad_branch.astype(BF)
    out_grad = contract_first(attended, grad_branch_low)
    grad_attended = contract_last(grad_branch_low, out_full).astype(BF).reshape(rows, H, HD)
    grad_probs = jnp.einsum("thd,ld->thl", grad_attended, values, preferred_element_type=F32)
    row_term = jnp.sum(probs * grad_probs, axis=-1, keepdims=True)
    grad_scores = (probs * (grad_probs - row_term)).astype(BF)
    grad_query = jnp.einsum("thl,ld->thd", grad_scores, keys, preferred_element_type=F32) * scale
    grad_keys = jnp.einsum("thl,thd->ld", grad_scores, query, preferred_element_type=F32) * scale
    grad_values = jnp.einsum("thl,thd->ld", probs_low, grad_attended, preferred_element_type=F32)
    grad_pairs = jnp.concatenate([grad_keys, grad_values], axis=1)
    spread = lax.dynamic_update_slice_in_dim(
        jnp.zeros((front + length, 2 * HD), F32), grad_pairs, first_row, 0
    )[front:]
    grad_pair = scatter_keys(spread.astype(BF).reshape(layers, 2, rows, 2 * HD))
    grad_key, grad_value = grad_pair[:, :HD], grad_pair[:, HD:]
    grad_proj_query, grad_proj_key, grad_gain_query, grad_gain_key = rotate_back(
        (grad_query, grad_key)
    )
    grad_projected = jnp.concatenate(
        [grad_proj_query.reshape(rows, query_width), grad_proj_key, grad_value], axis=1
    ).astype(BF)
    qkv_grad = contract_first(grad_projected, normed_low)
    grad_normed = jnp.dot(grad_projected, qkv_full, preferred_element_type=F32)
    grad_from_input, grad_gain_input = input_back(grad_normed)
    input_grad = grad_hidden + grad_from_input
    gains_grad = jnp.concatenate(
        [
            grad_gain_input,
            grad_gain_attend,
            grad_gain_feed.reshape(-1),
            grad_gain_query,
            grad_gain_key,
        ]
    )
    gains_grad = jnp.pad(gains_grad, (0, gain_rows * 128 - gains_grad.shape[0]))
    qkv_low, out_low, gains_sum, gate_up_low, down_low = reduce_grads(
        qkv_grad.astype(BF).reshape(layers, 2, 2, 2, -1, width),
        out_grad.astype(BF).reshape(layers, 2, 2, 2, -1, width),
        gains_grad.reshape(gain_rows, 128),
        gate_up_grad.reshape(2, 2, -1, width),
        down_grad.reshape(2, -1, width),
    )
    qkv_total = qkv_low.reshape(-1, width).astype(F32)
    out_total = out_low.reshape(-1, width).astype(F32)
    gate_up_total = gate_up_low.reshape(-1, width).astype(F32)
    down_total = down_low.astype(F32)
    gains_total = lax.dynamic_slice_in_dim(gains_sum.reshape(-1), chip * own_gains, own_gains, 0)
    qkv_new, qkv_first_new, qkv_second_new = adamw(qkv_weight, qkv_total, qkv_first, qkv_second)
    out_new, out_first_new, out_second_new = adamw(out_weight, out_total, out_first, out_second)
    gate_up_new, gate_up_first_new, gate_up_second_new = adamw(
        gate_up_weight, gate_up_total, gate_up_first, gate_up_second
    )
    down_new, down_first_new, down_second_new = adamw(
        down_weight, down_total, down_first, down_second
    )
    gains_new, gains_first_new, gains_second_new = adamw(
        gains, gains_total, gains_first, gains_second
    )
    return (
        output[None],
        input_grad[None],
        qkv_total,
        out_total,
        gate_up_total,
        down_total,
        gains_total,
        qkv_new,
        out_new,
        gate_up_new,
        down_new,
        gains_new,
        qkv_first_new,
        out_first_new,
        gate_up_first_new,
        down_first_new,
        gains_first_new,
        qkv_second_new,
        out_second_new,
        gate_up_second_new,
        down_second_new,
        gains_second_new,
    )


def solution(mesh):
    in_specs = (
        P(("dp", "fsdp"), "ctx", None),
        P(("dp", "fsdp"), "ctx", None),
        P(("dp", "fsdp"), None),
        P(("ctx", "fsdp"), None),
        P(("ctx", "fsdp"), None),
        P(("ctx", "fsdp"), None),
        P(("ctx", "fsdp"), None),
        P(("ctx", "fsdp")),
        P(("ctx", "fsdp"), None),
        P(("ctx", "fsdp"), None),
        P(("ctx", "fsdp"), None),
        P(("ctx", "fsdp"), None),
        P(("ctx", "fsdp")),
        P(("ctx", "fsdp"), None),
        P(("ctx", "fsdp"), None),
        P(("ctx", "fsdp"), None),
        P(("ctx", "fsdp"), None),
        P(("ctx", "fsdp")),
    )
    out_specs = (
        P(("dp", "fsdp"), "ctx", None),
        P(("dp", "fsdp"), "ctx", None),
        P(("ctx", "fsdp"), None),
        P(("ctx", "fsdp"), None),
        P(("ctx", "fsdp"), None),
        P(("ctx", "fsdp"), None),
        P(("ctx", "fsdp")),
        P(("ctx", "fsdp"), None),
        P(("ctx", "fsdp"), None),
        P(("ctx", "fsdp"), None),
        P(("ctx", "fsdp"), None),
        P(("ctx", "fsdp")),
        P(("ctx", "fsdp"), None),
        P(("ctx", "fsdp"), None),
        P(("ctx", "fsdp"), None),
        P(("ctx", "fsdp"), None),
        P(("ctx", "fsdp")),
        P(("ctx", "fsdp"), None),
        P(("ctx", "fsdp"), None),
        P(("ctx", "fsdp"), None),
        P(("ctx", "fsdp"), None),
        P(("ctx", "fsdp")),
    )
    body = move_tokens_body if moves_tokens(mesh) else gather_weights_body
    return jax.shard_map(body, mesh=mesh, in_specs=in_specs, out_specs=out_specs, check_vma=False)
```

```python
import functools

import jax
import jax.numpy as jnp
from jax import lax
from jax.experimental import pallas as pl
from jax.experimental.pallas import tpu as pltpu
from jax.sharding import PartitionSpec as P

MESH = pl.DeviceIdType.MESH
ANY = pl.BlockSpec(memory_space=pl.ANY)
VMEM = pl.BlockSpec(memory_space=pltpu.VMEM)
BF = jnp.bfloat16
F32 = jnp.float32

H = 4
HD = 256
STEP = 5


def normalize(value, gain):
    scale = lax.rsqrt(jnp.mean(value * value, axis=-1, keepdims=True) + 1e-06)
    return value * scale * (1.0 + gain)


def rotate(value, angles):
    half = value.shape[-1] // 2
    first = value[..., :half]
    second = value[..., half:]
    cosine = jnp.cos(angles)
    sine = jnp.sin(angles)
    return jnp.concatenate(
        [first * cosine - second * sine, second * cosine + first * sine], axis=-1
    )


def rope_angles(segments, first, rows):
    own = lax.dynamic_slice_in_dim(segments, first, rows, 0)
    starts = jnp.sum((segments[None, :] < own[:, None]).astype(jnp.int32), axis=1)
    offset = (first + jnp.arange(rows, dtype=jnp.int32) - starts).astype(jnp.float32)
    inverse = jnp.exp(-jnp.log(1000000.0) * (2.0 * jnp.arange(HD // 2, dtype=jnp.float32)) / HD)
    return offset[:, None] * inverse[None, :]


def contract_last(left, right):
    return lax.dot_general(
        left, right, (((1,), (1,)), ((), ())), preferred_element_type=jnp.float32
    )


def contract_first(left, right):
    return lax.dot_general(
        left, right, (((0,), (0,)), ((), ())), preferred_element_type=jnp.float32
    )


def activate(gate_up):
    half = gate_up.shape[-1] // 2
    return jax.nn.gelu(gate_up[:, :half], approximate=True) * gate_up[:, half:]


def adamw(weight, grad, first, second):
    first_new = 0.9 * first + 0.1 * grad
    second_new = 0.95 * second + 0.05 * grad * grad
    first_hat = first_new / (1.0 - 0.9**STEP)
    second_hat = second_new / (1.0 - 0.95**STEP)
    weight_new = weight - 0.03 * (first_hat / (jnp.sqrt(second_hat) + 1e-08) + 0.1 * weight)
    return (weight_new, first_new, second_new)


def gather_weights_body(
    tokens,
    cotangent,
    segments,
    qkv_weight,
    out_weight,
    gate_up_weight,
    down_weight,
    gains,
    qkv_first,
    out_first,
    gate_up_first,
    down_first,
    gains_first,
    qkv_second,
    out_second,
    gate_up_second,
    down_second,
    gains_second,
):
    rows = tokens.shape[1]
    width = tokens.shape[2]
    length = segments.shape[1]
    query_width = H * HD
    scale = HD ** (-0.5)
    reach = lax.axis_size("ctx") // 2 + 1
    front = reach * rows
    window = front + rows
    qkv_full, out_full, gains_full = (
        lax.all_gather(qkv_weight.astype(jnp.bfloat16), ("ctx", "fsdp"), axis=0, tiled=True),
        lax.all_gather(out_weight.astype(jnp.bfloat16), ("ctx", "fsdp"), axis=0, tiled=True),
        lax.all_gather(gains.astype(jnp.bfloat16), ("ctx", "fsdp"), axis=0, tiled=True),
    )
    gain_all = gains_full.astype(jnp.float32)
    gain_input = gain_all[:width]
    gain_attend = gain_all[width : 2 * width]
    gain_pre = gain_all[2 * width : 3 * width]
    gain_post = gain_all[3 * width : 4 * width]
    gain_query = gain_all[4 * width : 4 * width + HD]
    gain_key = gain_all[4 * width + HD :]
    first_row = lax.axis_index("ctx") * rows
    sequence_ids = segments[0]
    angles = rope_angles(sequence_ids, first_row, rows)
    query_ids = lax.dynamic_slice_in_dim(sequence_ids, first_row, rows, 0)
    query_pos = first_row + jnp.arange(rows, dtype=jnp.int32)
    window_pos = first_row - front + jnp.arange(window, dtype=jnp.int32)
    padded_ids = jnp.concatenate([jnp.full((front,), -1, dtype=jnp.int32), sequence_ids])
    window_ids = lax.dynamic_slice_in_dim(padded_ids, first_row, window, 0)
    allowed = (window_pos[None, :] <= query_pos[:, None]) & (
        window_ids[None, :] == query_ids[:, None]
    )
    allowed = allowed[:, None, :]
    x_rows = tokens[0].astype(jnp.float32)
    normed, input_back = jax.vjp(normalize, x_rows, gain_input)
    normed_low = normed.astype(jnp.bfloat16)
    projected = contract_last(normed_low, qkv_full)
    proj_query = projected[:, :query_width].reshape(rows, H, HD)
    proj_key = projected[:, query_width : query_width + HD]
    proj_value = projected[:, query_width + HD :]

    def query_key(part_query, part_key, query_gain, key_gain):
        return (
            rotate(normalize(part_query, query_gain), angles[:, None, :]),
            rotate(normalize(part_key, key_gain), angles),
        )

    (rotated_query, rotated_key), rotate_back = jax.vjp(
        query_key, proj_query, proj_key, gain_query, gain_key
    )
    query = rotated_query.astype(jnp.bfloat16)
    key_low = rotated_key.astype(jnp.bfloat16)
    value_low = proj_value.astype(jnp.bfloat16)
    keys_all, values_all = (
        lax.all_gather(key_low, "ctx", axis=0, tiled=True),
        lax.all_gather(value_low, "ctx", axis=0, tiled=True),
    )
    blank = jnp.zeros((front, HD), jnp.bfloat16)
    keys = lax.dynamic_slice_in_dim(jnp.concatenate([blank, keys_all]), first_row, window, 0)
    values = lax.dynamic_slice_in_dim(jnp.concatenate([blank, values_all]), first_row, window, 0)
    scores = jnp.einsum("thd,ld->thl", query, keys, preferred_element_type=jnp.float32) * scale
    masked = jnp.where(allowed, scores, -1e30)
    largest = jnp.max(masked, axis=-1, keepdims=True)
    log_total = largest + jnp.log(jnp.sum(jnp.exp(masked - largest), axis=-1, keepdims=True))
    probs_low = jnp.exp(masked - log_total).astype(jnp.bfloat16)
    attended = jnp.einsum("thl,ld->thd", probs_low, values, preferred_element_type=jnp.float32)
    attended = attended.reshape(rows, query_width).astype(jnp.bfloat16)
    branch = jnp.dot(attended, out_full, preferred_element_type=jnp.float32)
    branch_normed, attend_back = jax.vjp(normalize, branch, gain_attend)
    hidden = x_rows + branch_normed
    gate_up_full, down_full = (
        lax.all_gather(gate_up_weight.astype(jnp.bfloat16), ("ctx", "fsdp"), axis=0, tiled=True),
        lax.all_gather(down_weight.astype(jnp.bfloat16), ("ctx", "fsdp"), axis=0, tiled=True),
    )
    hidden_normed, pre_back = jax.vjp(normalize, hidden, gain_pre)
    hidden_low = hidden_normed.astype(jnp.bfloat16)
    gate_up = contract_last(hidden_low, gate_up_full)
    mixed, mix_back = jax.vjp(activate, gate_up)
    mixed_low = mixed.astype(jnp.bfloat16)
    down = jnp.dot(mixed_low, down_full, preferred_element_type=jnp.float32)
    down_normed, post_back = jax.vjp(normalize, down, gain_post)
    output = (hidden + down_normed).astype(jnp.bfloat16)
    gate_up_back, down_back = (
        lax.all_gather(gate_up_weight.astype(jnp.bfloat16), ("ctx", "fsdp"), axis=0, tiled=True),
        lax.all_gather(down_weight.astype(jnp.bfloat16), ("ctx", "fsdp"), axis=0, tiled=True),
    )
    grad_rows = cotangent[0].astype(jnp.float32)
    grad_down, grad_gain_post = post_back(grad_rows)
    grad_down_low = grad_down.astype(jnp.bfloat16)
    down_grad = contract_first(mixed_low, grad_down_low)
    grad_mixed = contract_last(grad_down_low, down_back)
    (grad_gate_up,) = mix_back(grad_mixed)
    grad_gate_up_low = grad_gate_up.astype(jnp.bfloat16)
    gate_up_grad = contract_first(grad_gate_up_low, hidden_low)
    grad_hidden_low = jnp.dot(grad_gate_up_low, gate_up_back, preferred_element_type=jnp.float32)
    grad_from_pre, grad_gain_pre = pre_back(grad_hidden_low)
    grad_hidden = grad_rows + grad_from_pre
    gate_up_part, down_part = (
        lax.psum_scatter(gate_up_grad, ("ctx", "fsdp"), scatter_dimension=0, tiled=True),
        lax.psum_scatter(down_grad, ("ctx", "fsdp"), scatter_dimension=0, tiled=True),
    )
    qkv_back, out_back = (
        lax.all_gather(qkv_weight.astype(jnp.bfloat16), ("ctx", "fsdp"), axis=0, tiled=True),
        lax.all_gather(out_weight.astype(jnp.bfloat16), ("ctx", "fsdp"), axis=0, tiled=True),
    )
    grad_branch, grad_gain_attend = attend_back(grad_hidden)
    grad_branch_low = grad_branch.astype(jnp.bfloat16)
    out_grad = contract_first(attended, grad_branch_low)
    grad_attended = (
        contract_last(grad_branch_low, out_back).astype(jnp.bfloat16).reshape(rows, H, HD)
    )
    scores_again = (
        jnp.einsum("thd,ld->thl", query, keys, preferred_element_type=jnp.float32) * scale
    )
    probs = jnp.exp(jnp.where(allowed, scores_again, -1e30) - log_total)
    grad_probs = jnp.einsum(
        "thd,ld->thl", grad_attended, values, preferred_element_type=jnp.float32
    )
    row_term = jnp.sum(probs * grad_probs, axis=-1, keepdims=True)
    grad_scores = (probs * (grad_probs - row_term)).astype(jnp.bfloat16)
    grad_query = (
        jnp.einsum("thl,ld->thd", grad_scores, keys, preferred_element_type=jnp.float32) * scale
    )
    grad_keys = (
        jnp.einsum("thl,thd->ld", grad_scores, query, preferred_element_type=jnp.float32) * scale
    )
    grad_values = jnp.einsum(
        "thl,thd->ld", probs.astype(jnp.bfloat16), grad_attended, preferred_element_type=jnp.float32
    )
    empty = jnp.zeros((front + length, HD), jnp.float32)
    keys_spread = lax.dynamic_update_slice_in_dim(empty, grad_keys, first_row, 0)[front:]
    values_spread = lax.dynamic_update_slice_in_dim(empty, grad_values, first_row, 0)[front:]
    grad_key, grad_value = (
        lax.psum_scatter(keys_spread, "ctx", scatter_dimension=0, tiled=True),
        lax.psum_scatter(values_spread, "ctx", scatter_dimension=0, tiled=True),
    )
    grad_proj_query, grad_proj_key, grad_gain_query, grad_gain_key = rotate_back(
        (grad_query, grad_key)
    )
    grad_projected = jnp.concatenate(
        [grad_proj_query.reshape(rows, query_width), grad_proj_key, grad_value], axis=1
    ).astype(jnp.bfloat16)
    qkv_grad = contract_first(grad_projected, normed_low)
    grad_normed = jnp.dot(grad_projected, qkv_back, preferred_element_type=jnp.float32)
    grad_from_input, grad_gain_input = input_back(grad_normed)
    input_grad = grad_hidden + grad_from_input
    gains_grad = jnp.concatenate(
        [
            grad_gain_input,
            grad_gain_attend,
            grad_gain_pre,
            grad_gain_post,
            grad_gain_query,
            grad_gain_key,
        ]
    )
    qkv_part, out_part, gains_part = (
        lax.psum_scatter(qkv_grad, ("ctx", "fsdp"), scatter_dimension=0, tiled=True),
        lax.psum_scatter(out_grad, ("ctx", "fsdp"), scatter_dimension=0, tiled=True),
        lax.psum_scatter(gains_grad, ("ctx", "fsdp"), scatter_dimension=0, tiled=True),
    )
    qkv_total, out_total, gate_up_total, down_total, gains_total = (
        lax.psum(qkv_part.astype(jnp.bfloat16), "dp").astype(jnp.float32),
        lax.psum(out_part.astype(jnp.bfloat16), "dp").astype(jnp.float32),
        lax.psum(gate_up_part.astype(jnp.bfloat16), "dp").astype(jnp.float32),
        lax.psum(down_part.astype(jnp.bfloat16), "dp").astype(jnp.float32),
        lax.psum(gains_part.astype(jnp.bfloat16), "dp").astype(jnp.float32),
    )
    qkv_new, qkv_first_new, qkv_second_new = adamw(qkv_weight, qkv_total, qkv_first, qkv_second)
    out_new, out_first_new, out_second_new = adamw(out_weight, out_total, out_first, out_second)
    gate_up_new, gate_up_first_new, gate_up_second_new = adamw(
        gate_up_weight, gate_up_total, gate_up_first, gate_up_second
    )
    down_new, down_first_new, down_second_new = adamw(
        down_weight, down_total, down_first, down_second
    )
    gains_new, gains_first_new, gains_second_new = adamw(
        gains, gains_total, gains_first, gains_second
    )
    return (
        output[None],
        input_grad[None],
        qkv_total,
        out_total,
        gate_up_total,
        down_total,
        gains_total,
        qkv_new,
        out_new,
        gate_up_new,
        down_new,
        gains_new,
        qkv_first_new,
        out_first_new,
        gate_up_first_new,
        down_first_new,
        gains_first_new,
        qkv_second_new,
        out_second_new,
        gate_up_second_new,
        down_second_new,
        gains_second_new,
    )


def place():
    return lax.axis_index("dp"), lax.axis_index("ctx"), lax.axis_index("fsdp")


class Links:
    def __init__(self, send, recv):
        self.send, self.recv, self.used, self.sent, self.some = send, recv, 0, [], []

    def slot(self):
        self.used += 1
        return self.send.at[self.used - 1], self.recv.at[self.used - 1]

    def make(self, source, target, device):
        send, recv = self.slot()
        return pltpu.make_async_remote_copy(
            src_ref=source,
            dst_ref=target,
            send_sem=send,
            recv_sem=recv,
            device_id=device,
            device_id_type=MESH,
        )

    def go(self, source, target, device):
        copy = self.make(source, target, device)
        copy.start()
        self.sent.append(copy)
        return copy

    def go_if(self, condition, source, target, device):
        copy = self.make(source, target, device)
        pl.when(condition)(copy.start)
        self.some.append((condition, copy))
        return copy

    def drain(self):
        for copy in self.sent:
            copy.wait_send()
        for condition, copy in self.some:
            pl.when(condition)(copy.wait_send)
        self.sent, self.some = [], []


TILE = 16
AXES = (1, 2, 4)
ORDERS = ((0, 1, 2), (1, 2, 0), (2, 0, 1))


class Cube:
    def __init__(self, links, tiles):
        dp, ctx, x = place()
        self.links, self.tiles = links, tiles
        self.me = (ctx % 4) * 2 + x
        self.peers = (
            (dp, ctx, 1 - x),
            (dp, ctx + 1 - 2 * (ctx % 2), x),
            (dp, ctx + 2 - 4 * (ctx // 2 % 2), x),
        )
        third = -(-tiles // 3)
        self.parts = ((0, third), (third, third), (2 * third, tiles - 2 * third))

    def block(self, mask):
        result = 0
        for bit in AXES:
            own = self.me // bit % 2
            result = result + bit * (1 - own if mask & bit else own)
        return result

    def cut(self, buf, p, mask):
        start, size = self.parts[p]
        return buf.at[pl.ds(self.block(mask) * self.tiles + start, size)]

    def gather(self, buf):
        sent = {}

        def go(p, index, mask, dim):
            ref = self.cut(buf, p, mask)
            sent[p, index] = self.links.go(ref, ref, self.peers[dim])

        for index, where in ((0, 0), (1, 1), (3, 2)):
            for p, order in enumerate(ORDERS):
                go(p, index, 0, order[where])
        for p, (a, b, c) in enumerate(ORDERS):
            sent[p, 0].wait_recv()
            go(p, 2, AXES[a], b)
            go(p, 4, AXES[a], c)
        for p, (a, b, c) in enumerate(ORDERS):
            sent[p, 1].wait_recv()
            go(p, 5, AXES[b], c)
            sent[p, 2].wait_recv()
            go(p, 6, AXES[a] | AXES[b], c)
        for index in (3, 4, 5, 6):
            for p in range(3):
                sent[p, index].wait_recv()

    def scatter(self, buf, one, two, three, beside=None):
        sent = {}

        def go(p, index, mask, slot, dim):
            start, size = self.parts[p]
            target = slot.at[pl.ds(start, size)]
            sent[p, index] = self.links.go(self.cut(buf, p, mask), target, self.peers[dim])

        def add(p, mask, slot):
            start, size = self.parts[p]
            mine = self.cut(buf, p, mask)
            mine[...] = (mine[...].astype(F32) + slot[pl.ds(start, size)].astype(F32)).astype(BF)

        for index in range(4):
            for p, (a, b, c) in enumerate(ORDERS):
                mask = (AXES[b], AXES[b] | AXES[a], AXES[a], 0)[index]
                go(p, index, AXES[c] | mask, one.at[index], c)
        if beside is not None:
            beside()
        for index in range(2):
            for p, (a, b, c) in enumerate(ORDERS):
                mask = AXES[b] | (AXES[a], 0)[index]
                sent[p, 1 - index].wait_recv()
                add(p, mask, one.at[1 - index])
                go(p, 4 + index, mask, two.at[index], b)
        for p, (a, b, c) in enumerate(ORDERS):
            sent[p, 2].wait_recv()
            add(p, AXES[a], one.at[2])
            sent[p, 4].wait_recv()
            add(p, AXES[a], two.at[0])
            go(p, 6, AXES[a], three, a)
        for p in range(3):
            sent[p, 3].wait_recv()
            add(p, 0, one.at[3])
            sent[p, 5].wait_recv()
            add(p, 0, two.at[1])
            sent[p, 6].wait_recv()


def flat(value):
    return value.reshape(-1, value.shape[-1])


def tiled(value):
    return value.reshape(-1, TILE, value.shape[-1])


def norm_scale(value):
    return lax.rsqrt(jnp.mean(value * value, axis=-1, keepdims=True) + 1e-06)


def norm_back(value, scale, gained):
    inner = jnp.mean(gained * value, axis=-1, keepdims=True)
    return scale * gained - value * (scale * scale * scale * inner)


ROOT = 0.7978845608028654


def gelu_parts(v):
    t = jnp.tanh(ROOT * (v + 0.044715 * (v * v * v)))
    value = 0.5 * v * (1.0 + t)
    slope = 0.5 * (1.0 + t) + 0.5 * v * (1.0 - t * t) * (ROOT * (1.0 + 0.134145 * (v * v)))
    return value, slope


def add_low(left, right):
    return (left.astype(F32) + right.astype(F32)).astype(BF)


def layer_kernel(
    tok,
    cot,
    seg,
    gpad,
    wq,
    wo,
    wgu_in,
    wd_in,
    output,
    input_grad,
    rq,
    ro,
    rg,
    rgu,
    rd,
    qkv_w,
    out_w,
    gains,
    wgu,
    wd,
    stage,
    acts,
    downs,
    gate,
    up,
    mixed,
    sums,
    one,
    two,
    three,
    pairs,
    query,
    proj,
    probs,
    attended,
    xn,
    turn,
    dscores,
    dpairs,
    kv_in,
    kv_sum,
    kv_far,
    pool,
    q_two,
    o_two,
    q_far,
    o_far,
    g_in,
    g_sum,
    gu_in,
    gu_far,
    d_in,
    d_far,
    send,
    recv,
    local,
):
    dp, ctx, x = place()
    rows, width = tok.shape
    layers = pairs.shape[0]
    length = seg.shape[0] * seg.shape[1]
    tiles = rows // TILE
    hq, ho = qkv_w.shape[4], out_w.shape[4]
    tq, to = hq // TILE, ho // TILE
    half = wd_in.shape[0]
    units = 2 * half
    thalf = half // TILE
    wide = wd.shape[0] * TILE
    query_width = H * HD
    scale = HD ** (-0.5)
    z, y = ctx // 2, ctx % 2
    cube_of = ctx // 4
    links = Links(send, recv)
    cube = Cube(links, tiles)
    sibling = (1 - dp, ctx, x)
    beside = (dp, z * 2 + 1 - y, x)
    across = (dp, lax.rem(ctx + 4, 8), x)
    others = [(dp, lax.rem(z + step, layers) * 2 + y, x) for step in range(1, layers)]
    y2, x2 = jnp.where(dp == 0, 1 - y, y), jnp.where(dp == 0, x, 1 - x)
    y3, x3 = jnp.where(dp == 0, y, 1 - y), jnp.where(dp == 0, 1 - x, x)
    mine2, mine3 = jnp.where(dp == 0, y, x), jnp.where(dp == 0, x, y)
    second = (dp, z * 2 + y2, x2)
    third = (dp, z * 2 + y3, x3)
    group = (ctx % 4) * 2 + x
    user = (x, ctx // 2 + 4 * dp, ctx % 2)
    owner = (cube_of, group, dp)
    stays_in = (dp == x) & (ctx == ctx // 2 + 4 * dp) & (x == ctx % 2)
    stays_back = (dp == cube_of) & (ctx == group)  & (x == dp)

    def bring(source, first, index):
        copy = pltpu.make_async_copy(
            source, stage.at[pl.ds(first, source.shape[0])], local.at[index]
        )
        copy.start()
        return copy

    bring_q = bring(wq, 0, 0)
    bring_o = bring(wo, 2 * hq, 1)
    bring_gu = bring(wgu_in.at[pl.ds(dp * half, half)], 2 * hq + 2 * ho, 2)

    pairs[...] = jnp.zeros(pairs.shape, BF)
    barrier = pltpu.get_barrier_semaphore()
    for device in others + [second, third, sibling, cube.peers[2]]:
        pl.semaphore_signal(barrier, inc=1, device_id=device, device_id_type=MESH)

    @pl.when(jnp.logical_not(stays_in))
    def _():
        for device in (user, owner):
            pl.semaphore_signal(barrier, inc=1, device_id=device, device_id_type=MESH)

    gains[z, y, x, dp] = gpad[dp]
    bring_q.wait()
    qkv_w[z, y, x, dp] = stage[pl.ds(dp * hq, hq), :].astype(BF)
    pl.semaphore_wait(barrier, jnp.where(stays_in, layers + 3, layers + 5))
    fulls = (gains, qkv_w, out_w)

    def first_steps(full):
        part = full.at[z, y, x, dp]
        return [links.go(part, part, device) for device in others]

    def pass_on(zz, yy, xx, *devices):
        part = qkv_w.at[zz, yy, xx, dp]
        return [links.go(part, part, device) for device in devices]

    firsts = [first_steps(gains), first_steps(qkv_w)]
    passed = [pass_on(z, y, x, second, third, sibling)]
    bring_o.wait()
    out_w[z, y, x, dp] = stage[pl.ds(2 * hq + dp * ho, ho), :].astype(BF)
    bring_gu.wait()
    low = 2 * hq + 2 * ho
    wgu[cube_of, pl.ds(dp * half, half), :] = stage[low : low + half, :].astype(BF)
    bring_d = bring(wd_in, 0, 3)

    row_id = lax.broadcasted_iota(jnp.int32, (rows, rows), 0)
    lane_id = lax.broadcasted_iota(jnp.int32, (rows, rows), 1)
    own_ids = seg[pl.ds(ctx, 1), :]
    ids = jnp.sum(jnp.where(row_id == lane_id, own_ids, 0), axis=1, keepdims=True)
    start = jnp.zeros((rows, 1), jnp.int32)
    for b in range(length // rows):
        start = start + jnp.sum((seg[b : b + 1, :] < ids).astype(jnp.int32), axis=1, keepdims=True)
    position = ctx * rows + lax.broadcasted_iota(jnp.int32, (rows, 1), 0)
    offset = (position - start).astype(F32)
    lane = lax.broadcasted_iota(jnp.int32, (1, HD // 2), 1).astype(F32)
    angle = offset * jnp.exp(lane * (-2.0 * 13.815510557964274 / HD))
    turn[0] = jnp.cos(angle)
    turn[1] = jnp.sin(angle)

    bring_d.wait()
    d_in[...] = tiled(stage[0:half, :].astype(BF))
    bring_rest = bring(wgu_in.at[pl.ds((1 - dp) * half, half)], 0, 4)
    bring_rest.wait()
    wgu[cube_of, pl.ds((1 - dp) * half, half), :] = stage[0:half, :].astype(BF)
    wgu[:, units:, :] = jnp.zeros((2, wide - units, width), BF)
    wd[2 * thalf :] = jnp.zeros((wide // TILE - 2 * thalf, TILE, width), BF)

    sib, seconds, thirds = {0: [], 2: []}, {}, {}

    def second_steps(t):
        for copy in firsts[t]:
            copy.wait_recv()
        line = fulls[t].at[:, y, x, dp]
        seconds[t] = links.go(line, line, second)
        thirds[t] = [links.go(line, line, third)]
        sib[t].append(links.go(line, line, sibling))

    def third_steps(t):
        seconds[t].wait_recv()
        line = fulls[t].at[:, y2, x2, dp]
        thirds[t].append(links.go(line, line, third))
        sib[t].append(links.go(line, line, sibling))

    def last_steps(t):
        for copy, (yy, xx) in zip(thirds[t], ((y3, x3), (1 - y, 1 - x))):
            copy.wait_recv()
            line = fulls[t].at[:, yy, xx, dp]
            sib[t].append(links.go(line, line, sibling))

    second_steps(0)
    behind = [lax.rem(z + layers - 1 - i, layers) for i in range(layers - 1)]
    for i, copy in enumerate(firsts[1]):
        copy.wait_recv()
        passed.append(pass_on(behind[i], y, x, second, third, sibling))
    half_rows = wgu.at[cube_of, pl.ds(dp * half, half)]
    gu_cross = links.go(half_rows, half_rows, across)
    firsts.append(first_steps(out_w))
    third_steps(0)
    line_order = [z] + behind
    far = []
    for i, zz in enumerate(line_order):
        passed[i][0].wait_recv()
        far.append(pass_on(zz, y2, x2, third, sibling))
    last_steps(0)
    ends_q = []
    for i, zz in enumerate(line_order):
        passed[i][1].wait_recv()
        ends_q += pass_on(zz, y3, x3, sibling)
        far[i][0].wait_recv()
        ends_q += pass_on(zz, 1 - y, 1 - x, sibling)
    second_steps(2)
    ends_q += [copies[2] for copies in passed] + [copies[1] for copies in far]
    for copy in ends_q + sib[0]:
        copy.wait_recv()

    total = jnp.zeros(gains.shape[-2:], F32)
    for h in range(2):
        part = jnp.zeros(gains.shape[-2:], F32)
        for zz in range(layers):
            for yy in range(2):
                for xx in range(2):
                    part = part + gains[zz, yy, xx, h]
        g_in[0, h * part.shape[0] : (h + 1) * part.shape[0], :] = part

    def gain_row(first, size):
        lo = first // 128
        return 1.0 + jnp.concatenate(
            [g_in[0, lo + i : lo + i + 1, :] for i in range(size // 128)], axis=1
        )

    gain_in = gain_row(0, width)
    gain_query = gain_row(4 * width, HD)
    gain_key = gain_row(4 * width + HD, HD)

    value = tok[...].astype(F32)
    xn[...] = (value * norm_scale(value) * gain_in).astype(BF)
    proj[...] = contract_last(xn[...], flat(qkv_w[...]))

    def turned(part, gain):
        part = part * norm_scale(part) * gain
        first, last = part[:, : HD // 2], part[:, HD // 2 :]
        cosine, sine = turn[0], turn[1]
        return jnp.concatenate(
            [first * cosine - last * sine, last * cosine + first * sine], axis=1
        )

    pairs[z, y, :, :HD] = turned(proj[:, query_width : query_width + HD], gain_key).astype(BF)
    pairs[z, y, :, HD:] = proj[:, query_width + HD :].astype(BF)
    own_pairs = pairs.at[z, y]
    upper = (dp, lax.rem(z + 1, layers) * 2 + y, x)
    rises = z < layers - 1
    pair_up = [links.go_if(rises, own_pairs, own_pairs, upper)]
    pair_side = [links.go(own_pairs, own_pairs, beside)]
    for h in range(H):
        query[h * rows : (h + 1) * rows, :] = turned(
            proj[:, h * HD : (h + 1) * HD], gain_query
        ).astype(BF)
    third_steps(2)
    for k in range(1, layers):
        below = z >= k
        part = pairs.at[lax.rem(z + layers - k, layers), y]
        pl.when(below)(pair_up[k - 1].wait_recv)
        if k < layers - 1:
            pair_up.append(links.go_if(below & rises, part, part, upper))
        pair_side.append(links.go_if(below, part, part, beside))
    own_down = wd.at[pl.ds(x * thalf, thalf)]
    down_local = pltpu.make_async_copy(d_in, own_down, local.at[5])
    down_move = links.make(d_in, own_down, user)

    @pl.when(stays_in)
    def _():
        down_local.start()

    @pl.when(jnp.logical_not(stays_in))
    def _():
        down_move.start()

    last_steps(2)
    pair_side[0].wait_recv()
    for k in range(1, layers):
        pl.when(z >= k)(pair_side[k].wait_recv)

    def allowed(b):
        key_pos = b * rows + lax.broadcasted_iota(jnp.int32, (1, rows), 1)
        return (key_pos <= position) & (seg[b : b + 1, :] == ids)

    keep = jnp.concatenate([allowed(b) for b in range(length // rows)], axis=1)
    keys = flat(pairs[:, :, :, :HD])
    values = flat(pairs[:, :, :, HD:])
    for h in range(H):
        part = slice(h * rows, (h + 1) * rows)
        scores = jnp.where(keep, contract_last(query[part, :], keys) * scale, -1e30)
        largest = jnp.max(scores, axis=-1, keepdims=True)
        raised = jnp.exp(scores - largest)
        p = raised / jnp.sum(raised, axis=-1, keepdims=True)
        probs[part, :] = p
        attended[:, h * HD : (h + 1) * HD] = jnp.dot(
            p.astype(BF), values, preferred_element_type=F32
        ).astype(BF)
    for copy in sib[2]:
        copy.wait_recv()
    branch = stage.at[0:rows]
    hidden = stage.at[rows : 2 * rows]
    grad_hidden = stage.at[2 * rows : 3 * rows]
    branch[...] = jnp.dot(attended[...], flat(out_w[...]), preferred_element_type=F32)
    gain_attend = gain_row(width, width)
    value = branch[...]
    hidden[...] = tok[...].astype(F32) + value * norm_scale(value) * gain_attend
    value = hidden[...]
    gain_pre = gain_row(2 * width, width)
    gain_post = gain_row(3 * width, width)

    def block_of(buf, j):
        return flat(buf[pl.ds(j * tiles, tiles)])

    def put_block(buf, j, block):
        buf[pl.ds(j * tiles, tiles)] = tiled(block)

    me = cube.me
    put_block(acts, me, (value * norm_scale(value) * gain_pre).astype(BF))
    cube.gather(acts)
    gu_cross.wait_recv()
    landed = wgu.at[1 - cube_of, pl.ds(dp * half, half)]
    links.go(landed, landed, sibling).wait_recv()

    def forward(j, carry):
        a = block_of(acts, j)
        g = contract_last(a, wgu[0])
        u = contract_last(a, wgu[1])
        gate[j] = g
        up[j] = u
        mixed[j] = (gelu_parts(g)[0] * u).astype(BF)
        return carry

    lax.fori_loop(0, 8, forward, 0)

    @pl.when(stays_in)
    def _():
        down_local.wait()

    @pl.when(jnp.logical_not(stays_in))
    def _():
        down_move.wait_send()

    @pl.when(jnp.logical_not(stays_in))
    def _():
        down_move.wait_recv()

    landed = wd.at[pl.ds(dp * thalf, thalf)]
    links.go(landed, landed, sibling).wait_recv()

    def project(j, carry):
        put_block(sums, j, jnp.dot(mixed[j], flat(wd[...]), preferred_element_type=F32).astype(BF))
        return carry

    lax.fori_loop(0, 8, project, 0)
    links.drain()
    cube.scatter(sums, one, two, three)
    links.drain()
    down = block_of(sums, me).astype(F32) + flat(three[...]).astype(F32)
    down_scale = norm_scale(down)
    normal = down * down_scale
    output[...] = (hidden[...] + normal * gain_post).astype(BF)
    dy = cot[...].astype(F32)
    put_block(downs, me, norm_back(down, down_scale, dy * gain_post).astype(BF))

    def put_gain(first, row):
        lo = first // 128
        for i in range(row.shape[1] // 128):
            g_sum[0, lo + i : lo + i + 1, :] = row[:, i * 128 : (i + 1) * 128]

    g_sum[0] = jnp.zeros(g_sum.shape[1:], F32)
    put_gain(3 * width, jnp.sum(dy * normal, axis=0, keepdims=True))
    cube.gather(downs)

    def put_rows(first, limit, block):
        kept = min(block.shape[0], limit)
        pool[first // TILE : (first + kept) // TILE] = tiled(block[:kept].astype(BF))

    downs_all = flat(downs[...])
    acts_all = flat(acts[...])
    tokens = 8 * rows
    for lo in range(0, wide, 128):
        cut = slice(lo, lo + 128)
        mx = mixed[:, :, cut].reshape(tokens, 128)
        put_rows(2 * units + lo, units - lo, contract_first(mx, downs_all))

    def slab(first, size):
        return pool.at[pl.ds(first, size)]

    d_swap = links.go(slab(4 * thalf + (1 - dp) * thalf, thalf), d_in, sibling)

    def backward(j, carry):
        d = contract_last(block_of(downs, j), flat(wd[...]))
        value, slope = gelu_parts(gate[j])
        dg = (d * up[j] * slope).astype(BF)
        du = (d * value).astype(BF)
        gate[j] = dg.astype(F32)
        up[j] = du.astype(F32)
        put_block(
            sums,
            j,
            (
                jnp.dot(dg, wgu[0], preferred_element_type=F32)
                + jnp.dot(du, wgu[1], preferred_element_type=F32)
            ).astype(BF),
        )
        return carry

    links.drain()
    lax.fori_loop(0, 8, backward, 0)
    moved = {}

    def weights():
        d_swap.wait_recv()
        d_in[...] = add_low(d_in[...], pool[pl.ds(4 * thalf + dp * thalf, thalf)])
        moved["local"] = pltpu.make_async_copy(d_in, d_far.at[cube_of], local.at[6])
        moved["down"] = links.make(d_in, d_far.at[cube_of], owner)

        @pl.when(stays_back)
        def _():
            moved["local"].start()

        @pl.when(jnp.logical_not(stays_back))
        def _():
            moved["down"].start()

        for lo in range(0, wide, 128):
            cut = slice(lo, lo + 128)
            for i, buf in enumerate((gate, up)):
                grad = buf[:, :, cut].reshape(tokens, 128).astype(BF)
                put_rows(i * units + lo, units - lo, contract_first(grad, acts_all))
        swap = [
            links.go(slab(i * 2 * thalf + (1 - dp) * thalf, thalf), gu_in.at[i], sibling)
            for i in range(2)
        ]
        for i in range(2):
            swap[i].wait_recv()
            gu_in[i] = add_low(gu_in[i], pool[pl.ds(i * 2 * thalf + dp * thalf, thalf)])
        moved["gu"] = links.go(gu_in.at[1 - cube_of], gu_far, across)

    cube.scatter(sums, one, two, three, weights)
    value = hidden[...]
    hidden_scale = norm_scale(value)
    total = block_of(sums, me).astype(F32) + flat(three[...]).astype(F32)
    put_gain(2 * width, jnp.sum(total * (value * hidden_scale), axis=0, keepdims=True))
    grad = cot[...].astype(F32) + norm_back(value, hidden_scale, total * gain_pre)
    grad_hidden[...] = grad
    value = branch[...]
    branch_scale = norm_scale(value)
    put_gain(width, jnp.sum(grad * (value * branch_scale), axis=0, keepdims=True))
    grad_branch = norm_back(value, branch_scale, grad * gain_attend).astype(BF)
    links.drain()

    def spot(h, zz, yy, xx):
        a, b = (yy, xx) if h == 0 else (xx, yy)
        return (b * 2 + a) * layers + zz

    def put_parts(base, count, block):
        for zz in range(layers):
            for yy in range(2):
                for xx in range(2):
                    for h in range(2):
                        first = (((zz * 2 + yy) * 2 + xx) * 2 + h) * count * TILE
                        at = base + (h * 4 * layers + spot(h, zz, yy, xx)) * count
                        pool[at : at + count] = tiled(
                            block[first : first + count * TILE].astype(BF)
                        )

    base_out = 8 * layers * tq
    q_in = downs.at[pl.ds(0, 4 * layers * tq)]
    o_in = acts.at[pl.ds(0, 4 * layers * to)]
    q_one = acts.at[pl.ds(4 * layers * to, 2 * layers * tq)]
    o_one = downs.at[pl.ds(4 * layers * tq, 2 * layers * to)]
    put_parts(base_out, to, contract_first(attended[...], grad_branch))
    per_out = 4 * layers * to
    per_qkv = 4 * layers * tq
    o_swap = links.go(slab(base_out + (1 - dp) * per_out, per_out), o_in, sibling)
    grad_att = contract_last(grad_branch, flat(out_w[...])).astype(BF)
    for h in range(H):
        part = slice(h * rows, (h + 1) * rows)
        p = probs[part, :]
        grad_p = contract_last(grad_att[:, h * HD : (h + 1) * HD], values)
        row = jnp.sum(p * grad_p, axis=-1, keepdims=True)
        dscores[part, :] = (p * (grad_p - row)).astype(BF)
    grad_heads = jnp.concatenate([grad_att[:, h * HD : (h + 1) * HD] for h in range(H)], axis=0)
    grad_keys = contract_first(dscores[...], query[...]) * scale
    dpairs[:, :, :, :HD] = grad_keys.astype(BF).reshape(layers, 2, rows, HD)
    grad_values = contract_first(probs[...].astype(BF), grad_heads)
    dpairs[:, :, :, HD:] = grad_values.astype(BF).reshape(layers, 2, rows, HD)
    kv_line = links.go(dpairs.at[:, 1 - y], kv_in, beside)

    def turned_back(part, gain, grad):
        cosine, sine = turn[0], turn[1]
        first, last = grad[:, : HD // 2], grad[:, HD // 2 :]
        grad = jnp.concatenate(
            [first * cosine + last * sine, last * cosine - first * sine], axis=1
        )
        part_scale = norm_scale(part)
        gain_term = jnp.sum(grad * (part * part_scale), axis=0, keepdims=True)
        return norm_back(part, part_scale, grad * gain), gain_term

    o_swap.wait_recv()
    mine_out = pl.ds(base_out + dp * per_out, per_out)
    pool[mine_out] = add_low(pool[mine_out], o_in[...])
    o_third = links.go(
        slab(base_out + dp * per_out + (1 - mine3) * per_out // 2, per_out // 2), o_one, third
    )
    query_term = jnp.zeros((1, HD), F32)
    grads = []
    for h in range(H):
        part = slice(h * rows, (h + 1) * rows)
        grad_query = jnp.dot(dscores[part, :], keys, preferred_element_type=F32) * scale
        grad, term = turned_back(proj[:, h * HD : (h + 1) * HD], gain_query, grad_query)
        grads.append(grad.astype(BF))
        query_term = query_term + term
    put_gain(4 * width, query_term)
    kv_line.wait_recv()
    for i in range(layers):
        kv_sum[i] = add_low(kv_in[i], dpairs[i, y])
    kv_copies = []
    for i, device in enumerate(others):
        to_layer = lax.rem(z + i + 1, layers)
        kv_copies.append(
            links.go_if(to_layer < z, kv_sum.at[to_layer], kv_far.at[i], device)
        )
    o_third.wait_recv()
    quarter_out = per_out // 4
    at_out = base_out + dp * per_out + mine3 * (per_out // 2)
    near = pl.ds(at_out, per_out // 2)
    pool[near] = add_low(pool[near], o_one[...])
    o_second = links.go(slab(at_out + (1 - mine2) * quarter_out, quarter_out), o_two, second)
    kv_total = stage.at[3 * rows : 4 * rows, 0 : 2 * HD]
    kv_total[...] = kv_sum[z].astype(F32)
    for i, copy in enumerate(kv_copies):

        @pl.when(behind[i] > z)
        def _():
            copy.wait_recv()
            kv_total[...] += kv_far[i].astype(F32)

    grad_pair = kv_total[...]
    grad, term = turned_back(
        proj[:, query_width : query_width + HD], gain_key, grad_pair[:, :HD]
    )
    put_gain(4 * width + HD, term)
    grads += [grad.astype(BF), grad_pair[:, HD:].astype(BF)]
    grad_proj = jnp.concatenate(grads, axis=1)
    put_parts(0, tq, contract_first(grad_proj, xn[...]))
    q_swap = links.go(slab((1 - dp) * per_qkv, per_qkv), q_in, sibling)
    grad_normed = jnp.dot(grad_proj, flat(qkv_w[...]), preferred_element_type=F32)
    value = tok[...].astype(F32)
    in_scale = norm_scale(value)
    put_gain(0, jnp.sum(grad_normed * (value * in_scale), axis=0, keepdims=True))
    g_swap = links.go(g_sum.at[0], g_in.at[1], sibling)
    input_grad[...] = grad_hidden[...] + norm_back(value, in_scale, grad_normed * gain_in)
    o_second.wait_recv()
    at_out = at_out + mine2 * quarter_out
    near = pl.ds(at_out, quarter_out)
    pool[near] = add_low(pool[near], o_two[...])
    o_fars = [
        links.go(slab(at_out + lax.rem(z + i + 1, layers) * to, to), o_far.at[i], device)
        for i, device in enumerate(others)
    ]
    g_swap.wait_recv()
    g_sum[1] = g_sum[0] + g_in[1]
    g_x = links.go(g_sum.at[1], g_in.at[2], cube.peers[0])
    q_swap.wait_recv()
    mine_qkv = pl.ds(dp * per_qkv, per_qkv)
    pool[mine_qkv] = add_low(pool[mine_qkv], q_in[...])
    q_third = links.go(slab(dp * per_qkv + (1 - mine3) * per_qkv // 2, per_qkv // 2), q_one, third)
    g_x.wait_recv()
    g_sum[2] = g_sum[1] + g_in[2]
    g_y = links.go(g_sum.at[2], g_in.at[3], beside)
    q_third.wait_recv()
    quarter_qkv = per_qkv // 4
    at_qkv = dp * per_qkv + mine3 * (per_qkv // 2)
    near = pl.ds(at_qkv, per_qkv // 2)
    pool[near] = add_low(pool[near], q_one[...])
    q_second = links.go(slab(at_qkv + (1 - mine2) * quarter_qkv, quarter_qkv), q_two, second)
    g_y.wait_recv()
    g_sum[3] = g_sum[2] + g_in[3]
    g_in[4 + z] = g_sum[3]
    g_z = [links.go(g_sum.at[3], g_in.at[4 + z], device) for device in others]
    q_second.wait_recv()
    at_qkv = at_qkv + mine2 * quarter_qkv
    near = pl.ds(at_qkv, quarter_qkv)
    pool[near] = add_low(pool[near], q_two[...])
    q_fars = [
        links.go(slab(at_qkv + lax.rem(z + i + 1, layers) * tq, tq), q_far.at[i], device)
        for i, device in enumerate(others)
    ]
    ends = []

    def finish(fars, far, at, count, result):
        value = pool[pl.ds(at + z * count, count)].astype(F32)
        for i, copy in enumerate(fars):
            copy.wait_recv()
            value = value + far[i].astype(F32)
        result[dp] = value.astype(BF)
        ends.append(links.go(result.at[dp], result.at[dp], sibling))

    finish(o_fars, o_far, at_out, to, ro)
    for copy in g_z:
        copy.wait_recv()
    value = g_in[4]
    for i in range(1, layers):
        value = value + g_in[4 + i]
    rg[...] = value

    @pl.when(stays_back)
    def _():
        moved["local"].wait()

    @pl.when(jnp.logical_not(stays_back))
    def _():
        moved["down"].wait_send()

    @pl.when(jnp.logical_not(stays_back))
    def _():
        moved["down"].wait_recv()

    landed = d_far.at[dp]
    d_end = links.go(landed, landed, sibling)
    finish(q_fars, q_far, at_qkv, tq, rq)
    d_end.wait_recv()
    d_in[...] = add_low(d_far[0], d_far[1])
    keep_d = pltpu.make_async_copy(d_in, rd, local.at[7])
    keep_d.start()
    moved["gu"].wait_recv()
    gu_far[...] = add_low(gu_in[cube_of], gu_far[...])
    keep_gu = pltpu.make_async_copy(gu_far, rgu.at[dp], local.at[8])
    keep_gu.start()
    ends.append(links.go(gu_far, rgu.at[dp], sibling))
    for copy in ends:
        copy.wait_recv()
    keep_d.wait()
    keep_gu.wait()
    links.drain()


def whole_layer(tok, cot, seg, gpad, wq, wo, wgu, wd, layers):
    rows, width = tok.shape
    units = 2 * wd.shape[0]
    wide = -(-units // 128) * 128
    hq, ho, half = wq.shape[0] // 2, wo.shape[0] // 2, wd.shape[0]
    tq, to, thalf, tiles = hq // TILE, ho // TILE, half // TILE, rows // TILE
    gain_rows = gpad.shape[0] * gpad.shape[1]
    length = seg.shape[0] * seg.shape[1]
    pool = max(6 * thalf, 8 * layers * (tq + to))

    def low(*shape):
        return pltpu.VMEM(shape, BF)

    def full(*shape):
        return pltpu.VMEM(shape, F32)

    def tile(*lead):
        return pltpu.VMEM(lead + (TILE, width), BF)

    return pl.pallas_call(
        layer_kernel,
        out_shape=(
            jax.ShapeDtypeStruct((rows, width), BF),
            jax.ShapeDtypeStruct((rows, width), F32),
            jax.ShapeDtypeStruct((2, tq, TILE, width), BF),
            jax.ShapeDtypeStruct((2, to, TILE, width), BF),
            jax.ShapeDtypeStruct((gain_rows, 128), F32),
            jax.ShapeDtypeStruct((2, thalf, TILE, width), BF),
            jax.ShapeDtypeStruct((thalf, TILE, width), BF),
        ),
        in_specs=[VMEM] * 4 + [ANY] * 4,
        out_specs=(VMEM,) * 5 + (ANY, ANY),
        scratch_shapes=[
            low(layers, 2, 2, 2, hq, width),
            low(layers, 2, 2, 2, ho, width),
            full(layers, 2, 2, 2, gain_rows // 2, 128),
            low(2, wide, width),
            tile(wide // TILE),
            full(2 * hq + 2 * ho + half, width),
            tile(8 * tiles),
            tile(8 * tiles),
            full(8, rows, wide),
            full(8, rows, wide),
            low(8, rows, wide),
            tile(8 * tiles),
            tile(4, tiles),
            tile(2, tiles),
            tile(tiles),
            low(layers, 2, rows, 2 * HD),
            low(H * rows, HD),
            full(rows, (H + 2) * HD),
            full(H * rows, length),
            low(rows, H * HD),
            low(rows, width),
            full(2, rows, HD // 2),
            low(H * rows, length),
            low(layers, 2, rows, 2 * HD),
            low(layers, rows, 2 * HD),
            low(layers, rows, 2 * HD),
            low(layers - 1, rows, 2 * HD),
            tile(pool),
            tile(layers * tq),
            tile(layers * to),
            tile(layers - 1, tq),
            tile(layers - 1, to),
            full(4 + layers, gain_rows, 128),
            full(4, gain_rows, 128),
            tile(2, thalf),
            tile(thalf),
            tile(thalf),
            tile(2, thalf),
            pltpu.SemaphoreType.DMA((220,)),
            pltpu.SemaphoreType.DMA((220,)),
            pltpu.SemaphoreType.DMA((9,)),
        ],
        compiler_params=pltpu.CompilerParams(
            collective_id=0, has_side_effects=True, vmem_limit_bytes=62 * 2**20
        ),
    )(tok, cot, seg, gpad, wq, wo, wgu, wd)


def moves_tokens(mesh):
    return mesh.shape["ctx"] == 8 and mesh.shape["fsdp"] == 2 and mesh.shape["dp"] == 2


def move_tokens_body(
    tokens,
    cotangent,
    segments,
    qkv_weight,
    out_weight,
    gate_up_weight,
    down_weight,
    gains,
    qkv_first,
    out_first,
    gate_up_first,
    down_first,
    gains_first,
    qkv_second,
    out_second,
    gate_up_second,
    down_second,
    gains_second,
):
    rows = tokens.shape[1]
    width = tokens.shape[2]
    layers = lax.axis_size("ctx") // 2
    chip = lax.axis_index("ctx") * 2 + lax.axis_index("fsdp")
    own_gains = gains.shape[0]
    gain_rows = -(-own_gains * 4 * layers // 1024) * 8 + 8
    gain_part = lax.dynamic_update_slice_in_dim(
        jnp.zeros((gain_rows * 128,), F32),
        gains.astype(BF).astype(F32),
        chip * own_gains,
        0,
    )
    output, input_grad, qkv_low, out_low, gains_sum, gate_up_low, down_low = whole_layer(
        tokens[0],
        cotangent[0],
        segments.reshape(-1, rows),
        gain_part.reshape(2, gain_rows // 2, 128),
        qkv_weight,
        out_weight,
        gate_up_weight,
        down_weight,
        layers,
    )
    qkv_total = qkv_low.reshape(-1, width).astype(F32)
    out_total = out_low.reshape(-1, width).astype(F32)
    gate_up_total = gate_up_low.reshape(-1, width).astype(F32)
    down_total = down_low.reshape(-1, width).astype(F32)
    gains_total = lax.dynamic_slice_in_dim(gains_sum.reshape(-1), chip * own_gains, own_gains, 0)
    qkv_new, qkv_first_new, qkv_second_new = adamw(qkv_weight, qkv_total, qkv_first, qkv_second)
    out_new, out_first_new, out_second_new = adamw(out_weight, out_total, out_first, out_second)
    gate_up_new, gate_up_first_new, gate_up_second_new = adamw(
        gate_up_weight, gate_up_total, gate_up_first, gate_up_second
    )
    down_new, down_first_new, down_second_new = adamw(
        down_weight, down_total, down_first, down_second
    )
    gains_new, gains_first_new, gains_second_new = adamw(
        gains, gains_total, gains_first, gains_second
    )
    return (
        output[None],
        input_grad[None],
        qkv_total,
        out_total,
        gate_up_total,
        down_total,
        gains_total,
        qkv_new,
        out_new,
        gate_up_new,
        down_new,
        gains_new,
        qkv_first_new,
        out_first_new,
        gate_up_first_new,
        down_first_new,
        gains_first_new,
        qkv_second_new,
        out_second_new,
        gate_up_second_new,
        down_second_new,
        gains_second_new,
    )


def solution(mesh):
    in_specs = (
        P(("dp", "fsdp"), "ctx", None),
        P(("dp", "fsdp"), "ctx", None),
        P(("dp", "fsdp"), None),
        P(("ctx", "fsdp"), None),
        P(("ctx", "fsdp"), None),
        P(("ctx", "fsdp"), None),
        P(("ctx", "fsdp"), None),
        P(("ctx", "fsdp")),
        P(("ctx", "fsdp"), None),
        P(("ctx", "fsdp"), None),
        P(("ctx", "fsdp"), None),
        P(("ctx", "fsdp"), None),
        P(("ctx", "fsdp")),
        P(("ctx", "fsdp"), None),
        P(("ctx", "fsdp"), None),
        P(("ctx", "fsdp"), None),
        P(("ctx", "fsdp"), None),
        P(("ctx", "fsdp")),
    )
    out_specs = (
        P(("dp", "fsdp"), "ctx", None),
        P(("dp", "fsdp"), "ctx", None),
        P(("ctx", "fsdp"), None),
        P(("ctx", "fsdp"), None),
        P(("ctx", "fsdp"), None),
        P(("ctx", "fsdp"), None),
        P(("ctx", "fsdp")),
        P(("ctx", "fsdp"), None),
        P(("ctx", "fsdp"), None),
        P(("ctx", "fsdp"), None),
        P(("ctx", "fsdp"), None),
        P(("ctx", "fsdp")),
        P(("ctx", "fsdp"), None),
        P(("ctx", "fsdp"), None),
        P(("ctx", "fsdp"), None),
        P(("ctx", "fsdp"), None),
        P(("ctx", "fsdp")),
        P(("ctx", "fsdp"), None),
        P(("ctx", "fsdp"), None),
        P(("ctx", "fsdp"), None),
        P(("ctx", "fsdp"), None),
        P(("ctx", "fsdp")),
    )
    body = move_tokens_body if moves_tokens(mesh) else gather_weights_body
    return jax.shard_map(body, mesh=mesh, in_specs=in_specs, out_specs=out_specs, check_vma=False)
```

```python
import functools

import jax
import jax.numpy as jnp
from jax import lax
from jax.experimental import pallas as pl
from jax.experimental.pallas import tpu as pltpu
from jax.sharding import PartitionSpec as P

MESH = pl.DeviceIdType.MESH
ANY = pl.BlockSpec(memory_space=pl.ANY)
VMEM = pl.BlockSpec(memory_space=pltpu.VMEM)
BF = jnp.bfloat16
F32 = jnp.float32

H = 4
HD = 256
STEP = 5


def normalize(value, gain):
    scale = lax.rsqrt(jnp.mean(value * value, axis=-1, keepdims=True) + 1e-06)
    return value * scale * (1.0 + gain)


def rotate(value, angles):
    half = value.shape[-1] // 2
    first = value[..., :half]
    second = value[..., half:]
    cosine = jnp.cos(angles)
    sine = jnp.sin(angles)
    return jnp.concatenate(
        [first * cosine - second * sine, second * cosine + first * sine], axis=-1
    )


def rope_angles(segments, first, rows):
    own = lax.dynamic_slice_in_dim(segments, first, rows, 0)
    starts = jnp.sum((segments[None, :] < own[:, None]).astype(jnp.int32), axis=1)
    offset = (first + jnp.arange(rows, dtype=jnp.int32) - starts).astype(jnp.float32)
    inverse = jnp.exp(-jnp.log(1000000.0) * (2.0 * jnp.arange(HD // 2, dtype=jnp.float32)) / HD)
    return offset[:, None] * inverse[None, :]


def contract_last(left, right):
    return lax.dot_general(
        left, right, (((1,), (1,)), ((), ())), preferred_element_type=jnp.float32
    )


def contract_first(left, right):
    return lax.dot_general(
        left, right, (((0,), (0,)), ((), ())), preferred_element_type=jnp.float32
    )


def activate(gate_up):
    half = gate_up.shape[-1] // 2
    return jax.nn.gelu(gate_up[:, :half], approximate=True) * gate_up[:, half:]


def adamw(weight, grad, first, second):
    first_new = 0.9 * first + 0.1 * grad
    second_new = 0.95 * second + 0.05 * grad * grad
    first_hat = first_new / (1.0 - 0.9**STEP)
    second_hat = second_new / (1.0 - 0.95**STEP)
    weight_new = weight - 0.03 * (first_hat / (jnp.sqrt(second_hat) + 1e-08) + 0.1 * weight)
    return (weight_new, first_new, second_new)


def gather_weights_body(
    tokens,
    cotangent,
    segments,
    qkv_weight,
    out_weight,
    gate_up_weight,
    down_weight,
    gains,
    qkv_first,
    out_first,
    gate_up_first,
    down_first,
    gains_first,
    qkv_second,
    out_second,
    gate_up_second,
    down_second,
    gains_second,
):
    rows = tokens.shape[1]
    width = tokens.shape[2]
    length = segments.shape[1]
    query_width = H * HD
    scale = HD ** (-0.5)
    reach = lax.axis_size("ctx") // 2 + 1
    front = reach * rows
    window = front + rows
    qkv_full, out_full, gains_full = (
        lax.all_gather(qkv_weight.astype(jnp.bfloat16), ("ctx", "fsdp"), axis=0, tiled=True),
        lax.all_gather(out_weight.astype(jnp.bfloat16), ("ctx", "fsdp"), axis=0, tiled=True),
        lax.all_gather(gains.astype(jnp.bfloat16), ("ctx", "fsdp"), axis=0, tiled=True),
    )
    gain_all = gains_full.astype(jnp.float32)
    gain_input = gain_all[:width]
    gain_attend = gain_all[width : 2 * width]
    gain_pre = gain_all[2 * width : 3 * width]
    gain_post = gain_all[3 * width : 4 * width]
    gain_query = gain_all[4 * width : 4 * width + HD]
    gain_key = gain_all[4 * width + HD :]
    first_row = lax.axis_index("ctx") * rows
    sequence_ids = segments[0]
    angles = rope_angles(sequence_ids, first_row, rows)
    query_ids = lax.dynamic_slice_in_dim(sequence_ids, first_row, rows, 0)
    query_pos = first_row + jnp.arange(rows, dtype=jnp.int32)
    window_pos = first_row - front + jnp.arange(window, dtype=jnp.int32)
    padded_ids = jnp.concatenate([jnp.full((front,), -1, dtype=jnp.int32), sequence_ids])
    window_ids = lax.dynamic_slice_in_dim(padded_ids, first_row, window, 0)
    allowed = (window_pos[None, :] <= query_pos[:, None]) & (
        window_ids[None, :] == query_ids[:, None]
    )
    allowed = allowed[:, None, :]
    x_rows = tokens[0].astype(jnp.float32)
    normed, input_back = jax.vjp(normalize, x_rows, gain_input)
    normed_low = normed.astype(jnp.bfloat16)
    projected = contract_last(normed_low, qkv_full)
    proj_query = projected[:, :query_width].reshape(rows, H, HD)
    proj_key = projected[:, query_width : query_width + HD]
    proj_value = projected[:, query_width + HD :]

    def query_key(part_query, part_key, query_gain, key_gain):
        return (
            rotate(normalize(part_query, query_gain), angles[:, None, :]),
            rotate(normalize(part_key, key_gain), angles),
        )

    (rotated_query, rotated_key), rotate_back = jax.vjp(
        query_key, proj_query, proj_key, gain_query, gain_key
    )
    query = rotated_query.astype(jnp.bfloat16)
    key_low = rotated_key.astype(jnp.bfloat16)
    value_low = proj_value.astype(jnp.bfloat16)
    keys_all, values_all = (
        lax.all_gather(key_low, "ctx", axis=0, tiled=True),
        lax.all_gather(value_low, "ctx", axis=0, tiled=True),
    )
    blank = jnp.zeros((front, HD), jnp.bfloat16)
    keys = lax.dynamic_slice_in_dim(jnp.concatenate([blank, keys_all]), first_row, window, 0)
    values = lax.dynamic_slice_in_dim(jnp.concatenate([blank, values_all]), first_row, window, 0)
    scores = jnp.einsum("thd,ld->thl", query, keys, preferred_element_type=jnp.float32) * scale
    masked = jnp.where(allowed, scores, -1e30)
    largest = jnp.max(masked, axis=-1, keepdims=True)
    log_total = largest + jnp.log(jnp.sum(jnp.exp(masked - largest), axis=-1, keepdims=True))
    probs_low = jnp.exp(masked - log_total).astype(jnp.bfloat16)
    attended = jnp.einsum("thl,ld->thd", probs_low, values, preferred_element_type=jnp.float32)
    attended = attended.reshape(rows, query_width).astype(jnp.bfloat16)
    branch = jnp.dot(attended, out_full, preferred_element_type=jnp.float32)
    branch_normed, attend_back = jax.vjp(normalize, branch, gain_attend)
    hidden = x_rows + branch_normed
    gate_up_full, down_full = (
        lax.all_gather(gate_up_weight.astype(jnp.bfloat16), ("ctx", "fsdp"), axis=0, tiled=True),
        lax.all_gather(down_weight.astype(jnp.bfloat16), ("ctx", "fsdp"), axis=0, tiled=True),
    )
    hidden_normed, pre_back = jax.vjp(normalize, hidden, gain_pre)
    hidden_low = hidden_normed.astype(jnp.bfloat16)
    gate_up = contract_last(hidden_low, gate_up_full)
    mixed, mix_back = jax.vjp(activate, gate_up)
    mixed_low = mixed.astype(jnp.bfloat16)
    down = jnp.dot(mixed_low, down_full, preferred_element_type=jnp.float32)
    down_normed, post_back = jax.vjp(normalize, down, gain_post)
    output = (hidden + down_normed).astype(jnp.bfloat16)
    gate_up_back, down_back = (
        lax.all_gather(gate_up_weight.astype(jnp.bfloat16), ("ctx", "fsdp"), axis=0, tiled=True),
        lax.all_gather(down_weight.astype(jnp.bfloat16), ("ctx", "fsdp"), axis=0, tiled=True),
    )
    grad_rows = cotangent[0].astype(jnp.float32)
    grad_down, grad_gain_post = post_back(grad_rows)
    grad_down_low = grad_down.astype(jnp.bfloat16)
    down_grad = contract_first(mixed_low, grad_down_low)
    grad_mixed = contract_last(grad_down_low, down_back)
    (grad_gate_up,) = mix_back(grad_mixed)
    grad_gate_up_low = grad_gate_up.astype(jnp.bfloat16)
    gate_up_grad = contract_first(grad_gate_up_low, hidden_low)
    grad_hidden_low = jnp.dot(grad_gate_up_low, gate_up_back, preferred_element_type=jnp.float32)
    grad_from_pre, grad_gain_pre = pre_back(grad_hidden_low)
    grad_hidden = grad_rows + grad_from_pre
    gate_up_part, down_part = (
        lax.psum_scatter(gate_up_grad, ("ctx", "fsdp"), scatter_dimension=0, tiled=True),
        lax.psum_scatter(down_grad, ("ctx", "fsdp"), scatter_dimension=0, tiled=True),
    )
    qkv_back, out_back = (
        lax.all_gather(qkv_weight.astype(jnp.bfloat16), ("ctx", "fsdp"), axis=0, tiled=True),
        lax.all_gather(out_weight.astype(jnp.bfloat16), ("ctx", "fsdp"), axis=0, tiled=True),
    )
    grad_branch, grad_gain_attend = attend_back(grad_hidden)
    grad_branch_low = grad_branch.astype(jnp.bfloat16)
    out_grad = contract_first(attended, grad_branch_low)
    grad_attended = (
        contract_last(grad_branch_low, out_back).astype(jnp.bfloat16).reshape(rows, H, HD)
    )
    scores_again = (
        jnp.einsum("thd,ld->thl", query, keys, preferred_element_type=jnp.float32) * scale
    )
    probs = jnp.exp(jnp.where(allowed, scores_again, -1e30) - log_total)
    grad_probs = jnp.einsum(
        "thd,ld->thl", grad_attended, values, preferred_element_type=jnp.float32
    )
    row_term = jnp.sum(probs * grad_probs, axis=-1, keepdims=True)
    grad_scores = (probs * (grad_probs - row_term)).astype(jnp.bfloat16)
    grad_query = (
        jnp.einsum("thl,ld->thd", grad_scores, keys, preferred_element_type=jnp.float32) * scale
    )
    grad_keys = (
        jnp.einsum("thl,thd->ld", grad_scores, query, preferred_element_type=jnp.float32) * scale
    )
    grad_values = jnp.einsum(
        "thl,thd->ld", probs.astype(jnp.bfloat16), grad_attended, preferred_element_type=jnp.float32
    )
    empty = jnp.zeros((front + length, HD), jnp.float32)
    keys_spread = lax.dynamic_update_slice_in_dim(empty, grad_keys, first_row, 0)[front:]
    values_spread = lax.dynamic_update_slice_in_dim(empty, grad_values, first_row, 0)[front:]
    grad_key, grad_value = (
        lax.psum_scatter(keys_spread, "ctx", scatter_dimension=0, tiled=True),
        lax.psum_scatter(values_spread, "ctx", scatter_dimension=0, tiled=True),
    )
    grad_proj_query, grad_proj_key, grad_gain_query, grad_gain_key = rotate_back(
        (grad_query, grad_key)
    )
    grad_projected = jnp.concatenate(
        [grad_proj_query.reshape(rows, query_width), grad_proj_key, grad_value], axis=1
    ).astype(jnp.bfloat16)
    qkv_grad = contract_first(grad_projected, normed_low)
    grad_normed = jnp.dot(grad_projected, qkv_back, preferred_element_type=jnp.float32)
    grad_from_input, grad_gain_input = input_back(grad_normed)
    input_grad = grad_hidden + grad_from_input
    gains_grad = jnp.concatenate(
        [
            grad_gain_input,
            grad_gain_attend,
            grad_gain_pre,
            grad_gain_post,
            grad_gain_query,
            grad_gain_key,
        ]
    )
    qkv_part, out_part, gains_part = (
        lax.psum_scatter(qkv_grad, ("ctx", "fsdp"), scatter_dimension=0, tiled=True),
        lax.psum_scatter(out_grad, ("ctx", "fsdp"), scatter_dimension=0, tiled=True),
        lax.psum_scatter(gains_grad, ("ctx", "fsdp"), scatter_dimension=0, tiled=True),
    )
    qkv_total, out_total, gate_up_total, down_total, gains_total = (
        lax.psum(qkv_part.astype(jnp.bfloat16), "dp").astype(jnp.float32),
        lax.psum(out_part.astype(jnp.bfloat16), "dp").astype(jnp.float32),
        lax.psum(gate_up_part.astype(jnp.bfloat16), "dp").astype(jnp.float32),
        lax.psum(down_part.astype(jnp.bfloat16), "dp").astype(jnp.float32),
        lax.psum(gains_part.astype(jnp.bfloat16), "dp").astype(jnp.float32),
    )
    qkv_new, qkv_first_new, qkv_second_new = adamw(qkv_weight, qkv_total, qkv_first, qkv_second)
    out_new, out_first_new, out_second_new = adamw(out_weight, out_total, out_first, out_second)
    gate_up_new, gate_up_first_new, gate_up_second_new = adamw(
        gate_up_weight, gate_up_total, gate_up_first, gate_up_second
    )
    down_new, down_first_new, down_second_new = adamw(
        down_weight, down_total, down_first, down_second
    )
    gains_new, gains_first_new, gains_second_new = adamw(
        gains, gains_total, gains_first, gains_second
    )
    return (
        output[None],
        input_grad[None],
        qkv_total,
        out_total,
        gate_up_total,
        down_total,
        gains_total,
        qkv_new,
        out_new,
        gate_up_new,
        down_new,
        gains_new,
        qkv_first_new,
        out_first_new,
        gate_up_first_new,
        down_first_new,
        gains_first_new,
        qkv_second_new,
        out_second_new,
        gate_up_second_new,
        down_second_new,
        gains_second_new,
    )


def place():
    return lax.axis_index("dp"), lax.axis_index("ctx"), lax.axis_index("fsdp")


class Links:
    def __init__(self, send, recv):
        self.send, self.recv, self.used, self.sent, self.some = send, recv, 0, [], []

    def slot(self):
        self.used += 1
        return self.send.at[self.used - 1], self.recv.at[self.used - 1]

    def make(self, source, target, device):
        send, recv = self.slot()
        return pltpu.make_async_remote_copy(
            src_ref=source,
            dst_ref=target,
            send_sem=send,
            recv_sem=recv,
            device_id=device,
            device_id_type=MESH,
        )

    def go(self, source, target, device):
        copy = self.make(source, target, device)
        copy.start()
        self.sent.append(copy)
        return copy

    def go_if(self, condition, source, target, device):
        copy = self.make(source, target, device)
        pl.when(condition)(copy.start)
        self.some.append((condition, copy))
        return copy

    def drain(self):
        for copy in self.sent:
            copy.wait_send()
        for condition, copy in self.some:
            pl.when(condition)(copy.wait_send)
        self.sent, self.some = [], []


TILE = 16
AXES = (1, 2, 4)
ORDERS = ((0, 1, 2), (1, 2, 0), (2, 0, 1))


class Cube:
    def __init__(self, links, tiles):
        dp, ctx, x = place()
        self.links, self.tiles = links, tiles
        self.me = (ctx % 4) * 2 + x
        self.peers = (
            (dp, ctx, 1 - x),
            (dp, ctx + 1 - 2 * (ctx % 2), x),
            (dp, ctx + 2 - 4 * (ctx // 2 % 2), x),
        )
        third = -(-tiles // 3)
        self.parts = ((0, third), (third, third), (2 * third, tiles - 2 * third))

    def block(self, mask):
        result = 0
        for bit in AXES:
            own = self.me // bit % 2
            result = result + bit * (1 - own if mask & bit else own)
        return result

    def cut(self, buf, p, mask):
        start, size = self.parts[p]
        return buf.at[pl.ds(self.block(mask) * self.tiles + start, size)]

    def gather(self, buf):
        sent = {}

        def go(p, index, mask, dim):
            ref = self.cut(buf, p, mask)
            sent[p, index] = self.links.go(ref, ref, self.peers[dim])

        for index, where in ((0, 0), (1, 1), (3, 2)):
            for p, order in enumerate(ORDERS):
                go(p, index, 0, order[where])
        for p, (a, b, c) in enumerate(ORDERS):
            sent[p, 0].wait_recv()
            go(p, 2, AXES[a], b)
            go(p, 4, AXES[a], c)
        for p, (a, b, c) in enumerate(ORDERS):
            sent[p, 1].wait_recv()
            go(p, 5, AXES[b], c)
            sent[p, 2].wait_recv()
            go(p, 6, AXES[a] | AXES[b], c)
        for index in (3, 4, 5, 6):
            for p in range(3):
                sent[p, index].wait_recv()

    def scatter(self, buf, one, two, three, beside=None):
        sent = {}

        def go(p, index, mask, slot, dim):
            start, size = self.parts[p]
            target = slot.at[pl.ds(start, size)]
            sent[p, index] = self.links.go(self.cut(buf, p, mask), target, self.peers[dim])

        def add(p, mask, slot):
            start, size = self.parts[p]
            mine = self.cut(buf, p, mask)
            mine[...] = (mine[...].astype(F32) + slot[pl.ds(start, size)].astype(F32)).astype(BF)

        for index in range(4):
            for p, (a, b, c) in enumerate(ORDERS):
                mask = (AXES[b], AXES[b] | AXES[a], AXES[a], 0)[index]
                go(p, index, AXES[c] | mask, one.at[index], c)
        if beside is not None:
            beside()
        for index in range(2):
            for p, (a, b, c) in enumerate(ORDERS):
                mask = AXES[b] | (AXES[a], 0)[index]
                sent[p, 1 - index].wait_recv()
                add(p, mask, one.at[1 - index])
                go(p, 4 + index, mask, two.at[index], b)
        for p, (a, b, c) in enumerate(ORDERS):
            sent[p, 2].wait_recv()
            add(p, AXES[a], one.at[2])
            sent[p, 4].wait_recv()
            add(p, AXES[a], two.at[0])
            go(p, 6, AXES[a], three, a)
        for p in range(3):
            sent[p, 3].wait_recv()
            add(p, 0, one.at[3])
            sent[p, 5].wait_recv()
            add(p, 0, two.at[1])
            sent[p, 6].wait_recv()


def flat(value):
    return value.reshape(-1, value.shape[-1])


def tiled(value):
    return value.reshape(-1, TILE, value.shape[-1])


def norm_scale(value):
    return lax.rsqrt(jnp.mean(value * value, axis=-1, keepdims=True) + 1e-06)


def norm_back(value, scale, gained):
    inner = jnp.mean(gained * value, axis=-1, keepdims=True)
    return scale * gained - value * (scale * scale * scale * inner)


ROOT = 0.7978845608028654


def gelu_parts(v):
    t = jnp.tanh(ROOT * (v + 0.044715 * (v * v * v)))
    value = 0.5 * v * (1.0 + t)
    slope = 0.5 * (1.0 + t) + 0.5 * v * (1.0 - t * t) * (ROOT * (1.0 + 0.134145 * (v * v)))
    return value, slope


def add_low(left, right):
    return (left.astype(F32) + right.astype(F32)).astype(BF)


def layer_kernel(
    tok,
    cot,
    seg,
    gpad,
    wq,
    wo,
    wgu_in,
    wd_in,
    output,
    input_grad,
    rq,
    ro,
    rg,
    rgu,
    rd,
    qkv_w,
    out_w,
    gains,
    wgu,
    wd,
    stage,
    acts,
    downs,
    gate,
    up,
    mixed,
    sums,
    one,
    two,
    three,
    pairs,
    query,
    proj,
    probs,
    attended,
    xn,
    turn,
    dscores,
    dpairs,
    kv_in,
    kv_sum,
    kv_far,
    pool,
    q_two,
    o_two,
    q_far,
    o_far,
    g_in,
    g_sum,
    gu_in,
    gu_far,
    d_in,
    d_far,
    send,
    recv,
    local,
):
    dp, ctx, x = place()
    rows, width = tok.shape
    layers = pairs.shape[0]
    length = seg.shape[0] * seg.shape[1]
    tiles = rows // TILE
    hq, ho = qkv_w.shape[4], out_w.shape[4]
    tq, to = hq // TILE, ho // TILE
    half = wd_in.shape[0]
    units = 2 * half
    thalf = half // TILE
    wide = wd.shape[0] * TILE
    query_width = H * HD
    scale = HD ** (-0.5)
    z, y = ctx // 2, ctx % 2
    cube_of = ctx // 4
    links = Links(send, recv)
    cube = Cube(links, tiles)
    sibling = (1 - dp, ctx, x)
    beside = (dp, z * 2 + 1 - y, x)
    across = (dp, lax.rem(ctx + 4, 8), x)
    others = [(dp, lax.rem(z + step, layers) * 2 + y, x) for step in range(1, layers)]
    y2, x2 = jnp.where(dp == 0, 1 - y, y), jnp.where(dp == 0, x, 1 - x)
    y3, x3 = jnp.where(dp == 0, y, 1 - y), jnp.where(dp == 0, 1 - x, x)
    mine2, mine3 = jnp.where(dp == 0, y, x), jnp.where(dp == 0, x, y)
    second = (dp, z * 2 + y2, x2)
    third = (dp, z * 2 + y3, x3)
    group = (ctx % 4) * 2 + x
    user = (x, ctx // 2 + 4 * dp, ctx % 2)
    owner = (cube_of, group, dp)
    stays_in = (dp == x) & (ctx == ctx // 2 + 4 * dp) & (x == ctx % 2)
    stays_back = (dp == cube_of) & (ctx == group)  & (x == dp)

    def bring(source, first, index):
        copy = pltpu.make_async_copy(
            source, stage.at[pl.ds(first, source.shape[0])], local.at[index]
        )
        copy.start()
        return copy

    bring_q = bring(wq, 0, 0)
    bring_o = bring(wo, 2 * hq, 1)
    bring_gu = bring(wgu_in.at[pl.ds(dp * half, half)], 2 * hq + 2 * ho, 2)

    pairs[...] = jnp.zeros(pairs.shape, BF)
    barrier = pltpu.get_barrier_semaphore()
    for device in others + [second, third, sibling, cube.peers[2]]:
        pl.semaphore_signal(barrier, inc=1, device_id=device, device_id_type=MESH)

    @pl.when(jnp.logical_not(stays_in))
    def _():
        for device in (user, owner):
            pl.semaphore_signal(barrier, inc=1, device_id=device, device_id_type=MESH)

    gains[z, y, x, dp] = gpad[dp]
    bring_q.wait()
    qkv_w[z, y, x, dp] = stage[pl.ds(dp * hq, hq), :].astype(BF)
    pl.semaphore_wait(barrier, jnp.where(stays_in, layers + 3, layers + 5))
    fulls = (gains, qkv_w, out_w)

    def first_steps(full):
        part = full.at[z, y, x, dp]
        return [links.go(part, part, device) for device in others]

    def pass_on(zz, yy, xx, *devices):
        part = qkv_w.at[zz, yy, xx, dp]
        return [links.go(part, part, device) for device in devices]

    firsts = [first_steps(gains), first_steps(qkv_w)]
    passed = [pass_on(z, y, x, second, third, sibling)]
    bring_o.wait()
    out_w[z, y, x, dp] = stage[pl.ds(2 * hq + dp * ho, ho), :].astype(BF)
    bring_gu.wait()
    low = 2 * hq + 2 * ho
    wgu[cube_of, pl.ds(dp * half, half), :] = stage[low : low + half, :].astype(BF)
    bring_d = bring(wd_in, 0, 3)

    row_id = lax.broadcasted_iota(jnp.int32, (rows, rows), 0)
    lane_id = lax.broadcasted_iota(jnp.int32, (rows, rows), 1)
    own_ids = seg[pl.ds(ctx, 1), :]
    ids = jnp.sum(jnp.where(row_id == lane_id, own_ids, 0), axis=1, keepdims=True)
    start = jnp.zeros((rows, 1), jnp.int32)
    for b in range(length // rows):
        start = start + jnp.sum((seg[b : b + 1, :] < ids).astype(jnp.int32), axis=1, keepdims=True)
    position = ctx * rows + lax.broadcasted_iota(jnp.int32, (rows, 1), 0)
    offset = (position - start).astype(F32)
    lane = lax.broadcasted_iota(jnp.int32, (1, HD // 2), 1).astype(F32)
    angle = offset * jnp.exp(lane * (-2.0 * 13.815510557964274 / HD))
    turn[0] = jnp.cos(angle)
    turn[1] = jnp.sin(angle)

    bring_d.wait()
    d_in[...] = tiled(stage[0:half, :].astype(BF))
    bring_rest = bring(wgu_in.at[pl.ds((1 - dp) * half, half)], 0, 4)
    bring_rest.wait()
    wgu[cube_of, pl.ds((1 - dp) * half, half), :] = stage[0:half, :].astype(BF)
    wgu[:, units:, :] = jnp.zeros((2, wide - units, width), BF)
    wd[2 * thalf :] = jnp.zeros((wide // TILE - 2 * thalf, TILE, width), BF)

    sib, seconds, thirds = {0: [], 2: []}, {}, {}

    def second_steps(t):
        for copy in firsts[t]:
            copy.wait_recv()
        line = fulls[t].at[:, y, x, dp]
        seconds[t] = links.go(line, line, second)
        thirds[t] = [links.go(line, line, third)]
        sib[t].append(links.go(line, line, sibling))

    def third_steps(t):
        seconds[t].wait_recv()
        line = fulls[t].at[:, y2, x2, dp]
        thirds[t].append(links.go(line, line, third))
        sib[t].append(links.go(line, line, sibling))

    def last_steps(t):
        for copy, (yy, xx) in zip(thirds[t], ((y3, x3), (1 - y, 1 - x))):
            copy.wait_recv()
            line = fulls[t].at[:, yy, xx, dp]
            sib[t].append(links.go(line, line, sibling))

    second_steps(0)
    behind = [lax.rem(z + layers - 1 - i, layers) for i in range(layers - 1)]
    for i, copy in enumerate(firsts[1]):
        copy.wait_recv()
        passed.append(pass_on(behind[i], y, x, second, third, sibling))
    own_down = wd.at[pl.ds(x * thalf, thalf)]
    down_local = pltpu.make_async_copy(d_in, own_down, local.at[5])
    down_move = links.make(d_in, own_down, user)

    @pl.when(stays_in)
    def _():
        down_local.start()

    @pl.when(jnp.logical_not(stays_in))
    def _():
        down_move.start()

    firsts.append(first_steps(out_w))
    third_steps(0)
    line_order = [z] + behind
    far = []
    for i, zz in enumerate(line_order):
        passed[i][0].wait_recv()
        far.append(pass_on(zz, y2, x2, third, sibling))
    last_steps(0)
    ends_q = []
    for i, zz in enumerate(line_order):
        passed[i][1].wait_recv()
        ends_q += pass_on(zz, y3, x3, sibling)
        far[i][0].wait_recv()
        ends_q += pass_on(zz, 1 - y, 1 - x, sibling)
    second_steps(2)
    ends_q += [copies[2] for copies in passed] + [copies[1] for copies in far]
    for copy in ends_q + sib[0]:
        copy.wait_recv()

    total = jnp.zeros(gains.shape[-2:], F32)
    for h in range(2):
        part = jnp.zeros(gains.shape[-2:], F32)
        for zz in range(layers):
            for yy in range(2):
                for xx in range(2):
                    part = part + gains[zz, yy, xx, h]
        g_in[0, h * part.shape[0] : (h + 1) * part.shape[0], :] = part

    def gain_row(first, size):
        lo = first // 128
        return 1.0 + jnp.concatenate(
            [g_in[0, lo + i : lo + i + 1, :] for i in range(size // 128)], axis=1
        )

    gain_in = gain_row(0, width)
    gain_query = gain_row(4 * width, HD)
    gain_key = gain_row(4 * width + HD, HD)

    value = tok[...].astype(F32)
    xn[...] = (value * norm_scale(value) * gain_in).astype(BF)
    proj[...] = contract_last(xn[...], flat(qkv_w[...]))

    def turned(part, gain):
        part = part * norm_scale(part) * gain
        first, last = part[:, : HD // 2], part[:, HD // 2 :]
        cosine, sine = turn[0], turn[1]
        return jnp.concatenate(
            [first * cosine - last * sine, last * cosine + first * sine], axis=1
        )

    pairs[z, y, :, :HD] = turned(proj[:, query_width : query_width + HD], gain_key).astype(BF)
    pairs[z, y, :, HD:] = proj[:, query_width + HD :].astype(BF)
    own_pairs = pairs.at[z, y]
    upper = (dp, lax.rem(z + 1, layers) * 2 + y, x)
    rises = z < layers - 1
    pair_up = [links.go_if(rises, own_pairs, own_pairs, upper)]
    pair_side = [links.go(own_pairs, own_pairs, beside)]
    for h in range(H):
        query[h * rows : (h + 1) * rows, :] = turned(
            proj[:, h * HD : (h + 1) * HD], gain_query
        ).astype(BF)
    third_steps(2)
    for k in range(1, layers):
        below = z >= k
        part = pairs.at[lax.rem(z + layers - k, layers), y]
        pl.when(below)(pair_up[k - 1].wait_recv)
        if k < layers - 1:
            pair_up.append(links.go_if(below & rises, part, part, upper))
        pair_side.append(links.go_if(below, part, part, beside))
    last_steps(2)
    pair_side[0].wait_recv()
    for k in range(1, layers):
        pl.when(z >= k)(pair_side[k].wait_recv)

    half_rows = wgu.at[cube_of, pl.ds(dp * half, half)]
    gu_cross = links.go(half_rows, half_rows, across)
    def allowed(b):
        key_pos = b * rows + lax.broadcasted_iota(jnp.int32, (1, rows), 1)
        return (key_pos <= position) & (seg[b : b + 1, :] == ids)

    keep = jnp.concatenate([allowed(b) for b in range(length // rows)], axis=1)
    keys = flat(pairs[:, :, :, :HD])
    values = flat(pairs[:, :, :, HD:])
    for h in range(H):
        part = slice(h * rows, (h + 1) * rows)
        scores = jnp.where(keep, contract_last(query[part, :], keys) * scale, -1e30)
        largest = jnp.max(scores, axis=-1, keepdims=True)
        raised = jnp.exp(scores - largest)
        p = raised / jnp.sum(raised, axis=-1, keepdims=True)
        probs[part, :] = p
        attended[:, h * HD : (h + 1) * HD] = jnp.dot(
            p.astype(BF), values, preferred_element_type=F32
        ).astype(BF)
    for copy in sib[2]:
        copy.wait_recv()
    branch = stage.at[0:rows]
    hidden = stage.at[rows : 2 * rows]
    grad_hidden = stage.at[2 * rows : 3 * rows]
    branch[...] = jnp.dot(attended[...], flat(out_w[...]), preferred_element_type=F32)
    gain_attend = gain_row(width, width)
    value = branch[...]
    hidden[...] = tok[...].astype(F32) + value * norm_scale(value) * gain_attend
    value = hidden[...]
    gain_pre = gain_row(2 * width, width)
    gain_post = gain_row(3 * width, width)

    def block_of(buf, j):
        return flat(buf[pl.ds(j * tiles, tiles)])

    def put_block(buf, j, block):
        buf[pl.ds(j * tiles, tiles)] = tiled(block)

    me = cube.me
    put_block(acts, me, (value * norm_scale(value) * gain_pre).astype(BF))
    cube.gather(acts)
    gu_cross.wait_recv()
    landed = wgu.at[1 - cube_of, pl.ds(dp * half, half)]
    links.go(landed, landed, sibling).wait_recv()

    def forward(j, carry):
        a = block_of(acts, j)
        g = contract_last(a, wgu[0])
        u = contract_last(a, wgu[1])
        gate[j] = g
        up[j] = u
        mixed[j] = (gelu_parts(g)[0] * u).astype(BF)
        return carry

    lax.fori_loop(0, 8, forward, 0)

    @pl.when(stays_in)
    def _():
        down_local.wait()

    @pl.when(jnp.logical_not(stays_in))
    def _():
        down_move.wait_send()

    @pl.when(jnp.logical_not(stays_in))
    def _():
        down_move.wait_recv()

    landed = wd.at[pl.ds(dp * thalf, thalf)]
    links.go(landed, landed, sibling).wait_recv()

    def project(j, carry):
        put_block(sums, j, jnp.dot(mixed[j], flat(wd[...]), preferred_element_type=F32).astype(BF))
        return carry

    lax.fori_loop(0, 8, project, 0)
    links.drain()
    cube.scatter(sums, one, two, three)
    links.drain()
    down = block_of(sums, me).astype(F32) + flat(three[...]).astype(F32)
    down_scale = norm_scale(down)
    normal = down * down_scale
    output[...] = (hidden[...] + normal * gain_post).astype(BF)
    dy = cot[...].astype(F32)
    put_block(downs, me, norm_back(down, down_scale, dy * gain_post).astype(BF))

    def put_gain(first, row):
        lo = first // 128
        for i in range(row.shape[1] // 128):
            g_sum[0, lo + i : lo + i + 1, :] = row[:, i * 128 : (i + 1) * 128]

    g_sum[0] = jnp.zeros(g_sum.shape[1:], F32)
    put_gain(3 * width, jnp.sum(dy * normal, axis=0, keepdims=True))
    cube.gather(downs)

    def put_rows(first, limit, block):
        kept = min(block.shape[0], limit)
        pool[first // TILE : (first + kept) // TILE] = tiled(block[:kept].astype(BF))

    downs_all = flat(downs[...])
    acts_all = flat(acts[...])
    tokens = 8 * rows
    for lo in range(0, wide, 128):
        cut = slice(lo, lo + 128)
        mx = mixed[:, :, cut].reshape(tokens, 128)
        put_rows(2 * units + lo, units - lo, contract_first(mx, downs_all))

    def slab(first, size):
        return pool.at[pl.ds(first, size)]

    d_swap = links.go(slab(4 * thalf + (1 - dp) * thalf, thalf), d_in, sibling)

    def backward(j, carry):
        d = contract_last(block_of(downs, j), flat(wd[...]))
        value, slope = gelu_parts(gate[j])
        dg = (d * up[j] * slope).astype(BF)
        du = (d * value).astype(BF)
        gate[j] = dg.astype(F32)
        up[j] = du.astype(F32)
        put_block(
            sums,
            j,
            (
                jnp.dot(dg, wgu[0], preferred_element_type=F32)
                + jnp.dot(du, wgu[1], preferred_element_type=F32)
            ).astype(BF),
        )
        return carry

    links.drain()
    lax.fori_loop(0, 8, backward, 0)
    moved = {}

    def weights():
        d_swap.wait_recv()
        d_in[...] = add_low(d_in[...], pool[pl.ds(4 * thalf + dp * thalf, thalf)])
        moved["local"] = pltpu.make_async_copy(d_in, d_far.at[cube_of], local.at[6])
        moved["down"] = links.make(d_in, d_far.at[cube_of], owner)

        @pl.when(stays_back)
        def _():
            moved["local"].start()

        @pl.when(jnp.logical_not(stays_back))
        def _():
            moved["down"].start()

        for lo in range(0, wide, 128):
            cut = slice(lo, lo + 128)
            for i, buf in enumerate((gate, up)):
                grad = buf[:, :, cut].reshape(tokens, 128).astype(BF)
                put_rows(i * units + lo, units - lo, contract_first(grad, acts_all))
        swap = [
            links.go(slab(i * 2 * thalf + (1 - dp) * thalf, thalf), gu_in.at[i], sibling)
            for i in range(2)
        ]
        for i in range(2):
            swap[i].wait_recv()
            gu_in[i] = add_low(gu_in[i], pool[pl.ds(i * 2 * thalf + dp * thalf, thalf)])
        moved["gu"] = links.go(gu_in.at[1 - cube_of], gu_far, across)

    cube.scatter(sums, one, two, three, weights)
    value = hidden[...]
    hidden_scale = norm_scale(value)
    total = block_of(sums, me).astype(F32) + flat(three[...]).astype(F32)
    put_gain(2 * width, jnp.sum(total * (value * hidden_scale), axis=0, keepdims=True))
    grad = cot[...].astype(F32) + norm_back(value, hidden_scale, total * gain_pre)
    grad_hidden[...] = grad
    value = branch[...]
    branch_scale = norm_scale(value)
    put_gain(width, jnp.sum(grad * (value * branch_scale), axis=0, keepdims=True))
    grad_branch = norm_back(value, branch_scale, grad * gain_attend).astype(BF)
    links.drain()

    def spot(h, zz, yy, xx):
        a, b = (yy, xx) if h == 0 else (xx, yy)
        return (b * 2 + a) * layers + zz

    def put_parts(base, count, block):
        for zz in range(layers):
            for yy in range(2):
                for xx in range(2):
                    for h in range(2):
                        first = (((zz * 2 + yy) * 2 + xx) * 2 + h) * count * TILE
                        at = base + (h * 4 * layers + spot(h, zz, yy, xx)) * count
                        pool[at : at + count] = tiled(
                            block[first : first + count * TILE].astype(BF)
                        )

    base_out = 8 * layers * tq
    q_in = downs.at[pl.ds(0, 4 * layers * tq)]
    o_in = acts.at[pl.ds(0, 4 * layers * to)]
    q_one = acts.at[pl.ds(4 * layers * to, 2 * layers * tq)]
    o_one = downs.at[pl.ds(4 * layers * tq, 2 * layers * to)]
    put_parts(base_out, to, contract_first(attended[...], grad_branch))
    per_out = 4 * layers * to
    per_qkv = 4 * layers * tq
    o_swap = links.go(slab(base_out + (1 - dp) * per_out, per_out), o_in, sibling)
    grad_att = contract_last(grad_branch, flat(out_w[...])).astype(BF)
    for h in range(H):
        part = slice(h * rows, (h + 1) * rows)
        p = probs[part, :]
        grad_p = contract_last(grad_att[:, h * HD : (h + 1) * HD], values)
        row = jnp.sum(p * grad_p, axis=-1, keepdims=True)
        dscores[part, :] = (p * (grad_p - row)).astype(BF)
    grad_heads = jnp.concatenate([grad_att[:, h * HD : (h + 1) * HD] for h in range(H)], axis=0)
    grad_keys = contract_first(dscores[...], query[...]) * scale
    dpairs[:, :, :, :HD] = grad_keys.astype(BF).reshape(layers, 2, rows, HD)
    grad_values = contract_first(probs[...].astype(BF), grad_heads)
    dpairs[:, :, :, HD:] = grad_values.astype(BF).reshape(layers, 2, rows, HD)
    kv_line = links.go(dpairs.at[:, 1 - y], kv_in, beside)

    def turned_back(part, gain, grad):
        cosine, sine = turn[0], turn[1]
        first, last = grad[:, : HD // 2], grad[:, HD // 2 :]
        grad = jnp.concatenate(
            [first * cosine + last * sine, last * cosine - first * sine], axis=1
        )
        part_scale = norm_scale(part)
        gain_term = jnp.sum(grad * (part * part_scale), axis=0, keepdims=True)
        return norm_back(part, part_scale, grad * gain), gain_term

    o_swap.wait_recv()
    mine_out = pl.ds(base_out + dp * per_out, per_out)
    pool[mine_out] = add_low(pool[mine_out], o_in[...])
    o_third = links.go(
        slab(base_out + dp * per_out + (1 - mine3) * per_out // 2, per_out // 2), o_one, third
    )
    query_term = jnp.zeros((1, HD), F32)
    grads = []
    for h in range(H):
        part = slice(h * rows, (h + 1) * rows)
        grad_query = jnp.dot(dscores[part, :], keys, preferred_element_type=F32) * scale
        grad, term = turned_back(proj[:, h * HD : (h + 1) * HD], gain_query, grad_query)
        grads.append(grad.astype(BF))
        query_term = query_term + term
    put_gain(4 * width, query_term)
    kv_line.wait_recv()
    for i in range(layers):
        kv_sum[i] = add_low(kv_in[i], dpairs[i, y])
    kv_copies = []
    for i, device in enumerate(others):
        to_layer = lax.rem(z + i + 1, layers)
        kv_copies.append(
            links.go_if(to_layer < z, kv_sum.at[to_layer], kv_far.at[i], device)
        )
    o_third.wait_recv()
    quarter_out = per_out // 4
    at_out = base_out + dp * per_out + mine3 * (per_out // 2)
    near = pl.ds(at_out, per_out // 2)
    pool[near] = add_low(pool[near], o_one[...])
    o_second = links.go(slab(at_out + (1 - mine2) * quarter_out, quarter_out), o_two, second)
    kv_total = stage.at[3 * rows : 4 * rows, 0 : 2 * HD]
    kv_total[...] = kv_sum[z].astype(F32)
    for i, copy in enumerate(kv_copies):

        @pl.when(behind[i] > z)
        def _():
            copy.wait_recv()
            kv_total[...] += kv_far[i].astype(F32)

    grad_pair = kv_total[...]
    grad, term = turned_back(
        proj[:, query_width : query_width + HD], gain_key, grad_pair[:, :HD]
    )
    put_gain(4 * width + HD, term)
    grads += [grad.astype(BF), grad_pair[:, HD:].astype(BF)]
    grad_proj = jnp.concatenate(grads, axis=1)
    put_parts(0, tq, contract_first(grad_proj, xn[...]))
    q_swap = links.go(slab((1 - dp) * per_qkv, per_qkv), q_in, sibling)
    grad_normed = jnp.dot(grad_proj, flat(qkv_w[...]), preferred_element_type=F32)
    value = tok[...].astype(F32)
    in_scale = norm_scale(value)
    put_gain(0, jnp.sum(grad_normed * (value * in_scale), axis=0, keepdims=True))
    g_swap = links.go(g_sum.at[0], g_in.at[1], sibling)
    input_grad[...] = grad_hidden[...] + norm_back(value, in_scale, grad_normed * gain_in)
    o_second.wait_recv()
    at_out = at_out + mine2 * quarter_out
    near = pl.ds(at_out, quarter_out)
    pool[near] = add_low(pool[near], o_two[...])
    o_fars = [
        links.go(slab(at_out + lax.rem(z + i + 1, layers) * to, to), o_far.at[i], device)
        for i, device in enumerate(others)
    ]
    g_swap.wait_recv()
    g_sum[1] = g_sum[0] + g_in[1]
    g_x = links.go(g_sum.at[1], g_in.at[2], cube.peers[0])
    q_swap.wait_recv()
    mine_qkv = pl.ds(dp * per_qkv, per_qkv)
    pool[mine_qkv] = add_low(pool[mine_qkv], q_in[...])
    q_third = links.go(slab(dp * per_qkv + (1 - mine3) * per_qkv // 2, per_qkv // 2), q_one, third)
    g_x.wait_recv()
    g_sum[2] = g_sum[1] + g_in[2]
    g_y = links.go(g_sum.at[2], g_in.at[3], beside)
    q_third.wait_recv()
    quarter_qkv = per_qkv // 4
    at_qkv = dp * per_qkv + mine3 * (per_qkv // 2)
    near = pl.ds(at_qkv, per_qkv // 2)
    pool[near] = add_low(pool[near], q_one[...])
    q_second = links.go(slab(at_qkv + (1 - mine2) * quarter_qkv, quarter_qkv), q_two, second)
    g_y.wait_recv()
    g_sum[3] = g_sum[2] + g_in[3]
    g_in[4 + z] = g_sum[3]
    g_z = [links.go(g_sum.at[3], g_in.at[4 + z], device) for device in others]
    q_second.wait_recv()
    at_qkv = at_qkv + mine2 * quarter_qkv
    near = pl.ds(at_qkv, quarter_qkv)
    pool[near] = add_low(pool[near], q_two[...])
    q_fars = [
        links.go(slab(at_qkv + lax.rem(z + i + 1, layers) * tq, tq), q_far.at[i], device)
        for i, device in enumerate(others)
    ]
    ends = []

    def finish(fars, far, at, count, result):
        value = pool[pl.ds(at + z * count, count)].astype(F32)
        for i, copy in enumerate(fars):
            copy.wait_recv()
            value = value + far[i].astype(F32)
        result[dp] = value.astype(BF)
        ends.append(links.go(result.at[dp], result.at[dp], sibling))

    finish(o_fars, o_far, at_out, to, ro)
    for copy in g_z:
        copy.wait_recv()
    value = g_in[4]
    for i in range(1, layers):
        value = value + g_in[4 + i]
    rg[...] = value

    @pl.when(stays_back)
    def _():
        moved["local"].wait()

    @pl.when(jnp.logical_not(stays_back))
    def _():
        moved["down"].wait_send()

    @pl.when(jnp.logical_not(stays_back))
    def _():
        moved["down"].wait_recv()

    landed = d_far.at[dp]
    d_end = links.go(landed, landed, sibling)
    finish(q_fars, q_far, at_qkv, tq, rq)
    d_end.wait_recv()
    d_in[...] = add_low(d_far[0], d_far[1])
    keep_d = pltpu.make_async_copy(d_in, rd, local.at[7])
    keep_d.start()
    moved["gu"].wait_recv()
    gu_far[...] = add_low(gu_in[cube_of], gu_far[...])
    keep_gu = pltpu.make_async_copy(gu_far, rgu.at[dp], local.at[8])
    keep_gu.start()
    ends.append(links.go(gu_far, rgu.at[dp], sibling))
    for copy in ends:
        copy.wait_recv()
    keep_d.wait()
    keep_gu.wait()
    links.drain()


def whole_layer(tok, cot, seg, gpad, wq, wo, wgu, wd, layers):
    rows, width = tok.shape
    units = 2 * wd.shape[0]
    wide = -(-units // 128) * 128
    hq, ho, half = wq.shape[0] // 2, wo.shape[0] // 2, wd.shape[0]
    tq, to, thalf, tiles = hq // TILE, ho // TILE, half // TILE, rows // TILE
    gain_rows = gpad.shape[0] * gpad.shape[1]
    length = seg.shape[0] * seg.shape[1]
    pool = max(6 * thalf, 8 * layers * (tq + to))

    def low(*shape):
        return pltpu.VMEM(shape, BF)

    def full(*shape):
        return pltpu.VMEM(shape, F32)

    def tile(*lead):
        return pltpu.VMEM(lead + (TILE, width), BF)

    return pl.pallas_call(
        layer_kernel,
        out_shape=(
            jax.ShapeDtypeStruct((rows, width), BF),
            jax.ShapeDtypeStruct((rows, width), F32),
            jax.ShapeDtypeStruct((2, tq, TILE, width), BF),
            jax.ShapeDtypeStruct((2, to, TILE, width), BF),
            jax.ShapeDtypeStruct((gain_rows, 128), F32),
            jax.ShapeDtypeStruct((2, thalf, TILE, width), BF),
            jax.ShapeDtypeStruct((thalf, TILE, width), BF),
        ),
        in_specs=[VMEM] * 4 + [ANY] * 4,
        out_specs=(VMEM,) * 5 + (ANY, ANY),
        scratch_shapes=[
            low(layers, 2, 2, 2, hq, width),
            low(layers, 2, 2, 2, ho, width),
            full(layers, 2, 2, 2, gain_rows // 2, 128),
            low(2, wide, width),
            tile(wide // TILE),
            full(2 * hq + 2 * ho + half, width),
            tile(8 * tiles),
            tile(8 * tiles),
            full(8, rows, wide),
            full(8, rows, wide),
            low(8, rows, wide),
            tile(8 * tiles),
            tile(4, tiles),
            tile(2, tiles),
            tile(tiles),
            low(layers, 2, rows, 2 * HD),
            low(H * rows, HD),
            full(rows, (H + 2) * HD),
            full(H * rows, length),
            low(rows, H * HD),
            low(rows, width),
            full(2, rows, HD // 2),
            low(H * rows, length),
            low(layers, 2, rows, 2 * HD),
            low(layers, rows, 2 * HD),
            low(layers, rows, 2 * HD),
            low(layers - 1, rows, 2 * HD),
            tile(pool),
            tile(layers * tq),
            tile(layers * to),
            tile(layers - 1, tq),
            tile(layers - 1, to),
            full(4 + layers, gain_rows, 128),
            full(4, gain_rows, 128),
            tile(2, thalf),
            tile(thalf),
            tile(thalf),
            tile(2, thalf),
            pltpu.SemaphoreType.DMA((220,)),
            pltpu.SemaphoreType.DMA((220,)),
            pltpu.SemaphoreType.DMA((9,)),
        ],
        compiler_params=pltpu.CompilerParams(
            collective_id=0, has_side_effects=True, vmem_limit_bytes=62 * 2**20
        ),
    )(tok, cot, seg, gpad, wq, wo, wgu, wd)


def moves_tokens(mesh):
    return mesh.shape["ctx"] == 8 and mesh.shape["fsdp"] == 2 and mesh.shape["dp"] == 2


def move_tokens_body(
    tokens,
    cotangent,
    segments,
    qkv_weight,
    out_weight,
    gate_up_weight,
    down_weight,
    gains,
    qkv_first,
    out_first,
    gate_up_first,
    down_first,
    gains_first,
    qkv_second,
    out_second,
    gate_up_second,
    down_second,
    gains_second,
):
    rows = tokens.shape[1]
    width = tokens.shape[2]
    layers = lax.axis_size("ctx") // 2
    chip = lax.axis_index("ctx") * 2 + lax.axis_index("fsdp")
    own_gains = gains.shape[0]
    gain_rows = -(-own_gains * 4 * layers // 1024) * 8 + 8
    gain_part = lax.dynamic_update_slice_in_dim(
        jnp.zeros((gain_rows * 128,), F32),
        gains.astype(BF).astype(F32),
        chip * own_gains,
        0,
    )
    output, input_grad, qkv_low, out_low, gains_sum, gate_up_low, down_low = whole_layer(
        tokens[0],
        cotangent[0],
        segments.reshape(-1, rows),
        gain_part.reshape(2, gain_rows // 2, 128),
        qkv_weight,
        out_weight,
        gate_up_weight,
        down_weight,
        layers,
    )
    qkv_total = qkv_low.reshape(-1, width).astype(F32)
    out_total = out_low.reshape(-1, width).astype(F32)
    gate_up_total = gate_up_low.reshape(-1, width).astype(F32)
    down_total = down_low.reshape(-1, width).astype(F32)
    gains_total = lax.dynamic_slice_in_dim(gains_sum.reshape(-1), chip * own_gains, own_gains, 0)
    qkv_new, qkv_first_new, qkv_second_new = adamw(qkv_weight, qkv_total, qkv_first, qkv_second)
    out_new, out_first_new, out_second_new = adamw(out_weight, out_total, out_first, out_second)
    gate_up_new, gate_up_first_new, gate_up_second_new = adamw(
        gate_up_weight, gate_up_total, gate_up_first, gate_up_second
    )
    down_new, down_first_new, down_second_new = adamw(
        down_weight, down_total, down_first, down_second
    )
    gains_new, gains_first_new, gains_second_new = adamw(
        gains, gains_total, gains_first, gains_second
    )
    return (
        output[None],
        input_grad[None],
        qkv_total,
        out_total,
        gate_up_total,
        down_total,
        gains_total,
        qkv_new,
        out_new,
        gate_up_new,
        down_new,
        gains_new,
        qkv_first_new,
        out_first_new,
        gate_up_first_new,
        down_first_new,
        gains_first_new,
        qkv_second_new,
        out_second_new,
        gate_up_second_new,
        down_second_new,
        gains_second_new,
    )


def solution(mesh):
    in_specs = (
        P(("dp", "fsdp"), "ctx", None),
        P(("dp", "fsdp"), "ctx", None),
        P(("dp", "fsdp"), None),
        P(("ctx", "fsdp"), None),
        P(("ctx", "fsdp"), None),
        P(("ctx", "fsdp"), None),
        P(("ctx", "fsdp"), None),
        P(("ctx", "fsdp")),
        P(("ctx", "fsdp"), None),
        P(("ctx", "fsdp"), None),
        P(("ctx", "fsdp"), None),
        P(("ctx", "fsdp"), None),
        P(("ctx", "fsdp")),
        P(("ctx", "fsdp"), None),
        P(("ctx", "fsdp"), None),
        P(("ctx", "fsdp"), None),
        P(("ctx", "fsdp"), None),
        P(("ctx", "fsdp")),
    )
    out_specs = (
        P(("dp", "fsdp"), "ctx", None),
        P(("dp", "fsdp"), "ctx", None),
        P(("ctx", "fsdp"), None),
        P(("ctx", "fsdp"), None),
        P(("ctx", "fsdp"), None),
        P(("ctx", "fsdp"), None),
        P(("ctx", "fsdp")),
        P(("ctx", "fsdp"), None),
        P(("ctx", "fsdp"), None),
        P(("ctx", "fsdp"), None),
        P(("ctx", "fsdp"), None),
        P(("ctx", "fsdp")),
        P(("ctx", "fsdp"), None),
        P(("ctx", "fsdp"), None),
        P(("ctx", "fsdp"), None),
        P(("ctx", "fsdp"), None),
        P(("ctx", "fsdp")),
        P(("ctx", "fsdp"), None),
        P(("ctx", "fsdp"), None),
        P(("ctx", "fsdp"), None),
        P(("ctx", "fsdp"), None),
        P(("ctx", "fsdp")),
    )
    body = move_tokens_body if moves_tokens(mesh) else gather_weights_body
    return jax.shard_map(body, mesh=mesh, in_specs=in_specs, out_specs=out_specs, check_vma=False)
```

```python
import functools

import jax
import jax.numpy as jnp
from jax import lax
from jax.experimental import pallas as pl
from jax.experimental.pallas import tpu as pltpu
from jax.sharding import PartitionSpec as P

MESH = pl.DeviceIdType.MESH
ANY = pl.BlockSpec(memory_space=pl.ANY)
VMEM = pl.BlockSpec(memory_space=pltpu.VMEM)
BF = jnp.bfloat16
F32 = jnp.float32

H = 4
HD = 256
STEP = 5


def normalize(value, gain):
    scale = lax.rsqrt(jnp.mean(value * value, axis=-1, keepdims=True) + 1e-06)
    return value * scale * (1.0 + gain)


def rotate(value, angles):
    half = value.shape[-1] // 2
    first = value[..., :half]
    second = value[..., half:]
    cosine = jnp.cos(angles)
    sine = jnp.sin(angles)
    return jnp.concatenate(
        [first * cosine - second * sine, second * cosine + first * sine], axis=-1
    )


def rope_angles(segments, first, rows):
    own = lax.dynamic_slice_in_dim(segments, first, rows, 0)
    starts = jnp.sum((segments[None, :] < own[:, None]).astype(jnp.int32), axis=1)
    offset = (first + jnp.arange(rows, dtype=jnp.int32) - starts).astype(jnp.float32)
    inverse = jnp.exp(-jnp.log(1000000.0) * (2.0 * jnp.arange(HD // 2, dtype=jnp.float32)) / HD)
    return offset[:, None] * inverse[None, :]


def contract_last(left, right):
    return lax.dot_general(
        left, right, (((1,), (1,)), ((), ())), preferred_element_type=jnp.float32
    )


def contract_first(left, right):
    return lax.dot_general(
        left, right, (((0,), (0,)), ((), ())), preferred_element_type=jnp.float32
    )


def activate(gate_up):
    half = gate_up.shape[-1] // 2
    return jax.nn.gelu(gate_up[:, :half], approximate=True) * gate_up[:, half:]


def adamw(weight, grad, first, second):
    first_new = 0.9 * first + 0.1 * grad
    second_new = 0.95 * second + 0.05 * grad * grad
    first_hat = first_new / (1.0 - 0.9**STEP)
    second_hat = second_new / (1.0 - 0.95**STEP)
    weight_new = weight - 0.03 * (first_hat / (jnp.sqrt(second_hat) + 1e-08) + 0.1 * weight)
    return (weight_new, first_new, second_new)


def gather_weights_body(
    tokens,
    cotangent,
    segments,
    qkv_weight,
    out_weight,
    gate_up_weight,
    down_weight,
    gains,
    qkv_first,
    out_first,
    gate_up_first,
    down_first,
    gains_first,
    qkv_second,
    out_second,
    gate_up_second,
    down_second,
    gains_second,
):
    rows = tokens.shape[1]
    width = tokens.shape[2]
    length = segments.shape[1]
    query_width = H * HD
    scale = HD ** (-0.5)
    reach = lax.axis_size("ctx") // 2 + 1
    front = reach * rows
    window = front + rows
    qkv_full, out_full, gains_full = (
        lax.all_gather(qkv_weight.astype(jnp.bfloat16), ("ctx", "fsdp"), axis=0, tiled=True),
        lax.all_gather(out_weight.astype(jnp.bfloat16), ("ctx", "fsdp"), axis=0, tiled=True),
        lax.all_gather(gains.astype(jnp.bfloat16), ("ctx", "fsdp"), axis=0, tiled=True),
    )
    gain_all = gains_full.astype(jnp.float32)
    gain_input = gain_all[:width]
    gain_attend = gain_all[width : 2 * width]
    gain_pre = gain_all[2 * width : 3 * width]
    gain_post = gain_all[3 * width : 4 * width]
    gain_query = gain_all[4 * width : 4 * width + HD]
    gain_key = gain_all[4 * width + HD :]
    first_row = lax.axis_index("ctx") * rows
    sequence_ids = segments[0]
    angles = rope_angles(sequence_ids, first_row, rows)
    query_ids = lax.dynamic_slice_in_dim(sequence_ids, first_row, rows, 0)
    query_pos = first_row + jnp.arange(rows, dtype=jnp.int32)
    window_pos = first_row - front + jnp.arange(window, dtype=jnp.int32)
    padded_ids = jnp.concatenate([jnp.full((front,), -1, dtype=jnp.int32), sequence_ids])
    window_ids = lax.dynamic_slice_in_dim(padded_ids, first_row, window, 0)
    allowed = (window_pos[None, :] <= query_pos[:, None]) & (
        window_ids[None, :] == query_ids[:, None]
    )
    allowed = allowed[:, None, :]
    x_rows = tokens[0].astype(jnp.float32)
    normed, input_back = jax.vjp(normalize, x_rows, gain_input)
    normed_low = normed.astype(jnp.bfloat16)
    projected = contract_last(normed_low, qkv_full)
    proj_query = projected[:, :query_width].reshape(rows, H, HD)
    proj_key = projected[:, query_width : query_width + HD]
    proj_value = projected[:, query_width + HD :]

    def query_key(part_query, part_key, query_gain, key_gain):
        return (
            rotate(normalize(part_query, query_gain), angles[:, None, :]),
            rotate(normalize(part_key, key_gain), angles),
        )

    (rotated_query, rotated_key), rotate_back = jax.vjp(
        query_key, proj_query, proj_key, gain_query, gain_key
    )
    query = rotated_query.astype(jnp.bfloat16)
    key_low = rotated_key.astype(jnp.bfloat16)
    value_low = proj_value.astype(jnp.bfloat16)
    keys_all, values_all = (
        lax.all_gather(key_low, "ctx", axis=0, tiled=True),
        lax.all_gather(value_low, "ctx", axis=0, tiled=True),
    )
    blank = jnp.zeros((front, HD), jnp.bfloat16)
    keys = lax.dynamic_slice_in_dim(jnp.concatenate([blank, keys_all]), first_row, window, 0)
    values = lax.dynamic_slice_in_dim(jnp.concatenate([blank, values_all]), first_row, window, 0)
    scores = jnp.einsum("thd,ld->thl", query, keys, preferred_element_type=jnp.float32) * scale
    masked = jnp.where(allowed, scores, -1e30)
    largest = jnp.max(masked, axis=-1, keepdims=True)
    log_total = largest + jnp.log(jnp.sum(jnp.exp(masked - largest), axis=-1, keepdims=True))
    probs_low = jnp.exp(masked - log_total).astype(jnp.bfloat16)
    attended = jnp.einsum("thl,ld->thd", probs_low, values, preferred_element_type=jnp.float32)
    attended = attended.reshape(rows, query_width).astype(jnp.bfloat16)
    branch = jnp.dot(attended, out_full, preferred_element_type=jnp.float32)
    branch_normed, attend_back = jax.vjp(normalize, branch, gain_attend)
    hidden = x_rows + branch_normed
    gate_up_full, down_full = (
        lax.all_gather(gate_up_weight.astype(jnp.bfloat16), ("ctx", "fsdp"), axis=0, tiled=True),
        lax.all_gather(down_weight.astype(jnp.bfloat16), ("ctx", "fsdp"), axis=0, tiled=True),
    )
    hidden_normed, pre_back = jax.vjp(normalize, hidden, gain_pre)
    hidden_low = hidden_normed.astype(jnp.bfloat16)
    gate_up = contract_last(hidden_low, gate_up_full)
    mixed, mix_back = jax.vjp(activate, gate_up)
    mixed_low = mixed.astype(jnp.bfloat16)
    down = jnp.dot(mixed_low, down_full, preferred_element_type=jnp.float32)
    down_normed, post_back = jax.vjp(normalize, down, gain_post)
    output = (hidden + down_normed).astype(jnp.bfloat16)
    gate_up_back, down_back = (
        lax.all_gather(gate_up_weight.astype(jnp.bfloat16), ("ctx", "fsdp"), axis=0, tiled=True),
        lax.all_gather(down_weight.astype(jnp.bfloat16), ("ctx", "fsdp"), axis=0, tiled=True),
    )
    grad_rows = cotangent[0].astype(jnp.float32)
    grad_down, grad_gain_post = post_back(grad_rows)
    grad_down_low = grad_down.astype(jnp.bfloat16)
    down_grad = contract_first(mixed_low, grad_down_low)
    grad_mixed = contract_last(grad_down_low, down_back)
    (grad_gate_up,) = mix_back(grad_mixed)
    grad_gate_up_low = grad_gate_up.astype(jnp.bfloat16)
    gate_up_grad = contract_first(grad_gate_up_low, hidden_low)
    grad_hidden_low = jnp.dot(grad_gate_up_low, gate_up_back, preferred_element_type=jnp.float32)
    grad_from_pre, grad_gain_pre = pre_back(grad_hidden_low)
    grad_hidden = grad_rows + grad_from_pre
    gate_up_part, down_part = (
        lax.psum_scatter(gate_up_grad, ("ctx", "fsdp"), scatter_dimension=0, tiled=True),
        lax.psum_scatter(down_grad, ("ctx", "fsdp"), scatter_dimension=0, tiled=True),
    )
    qkv_back, out_back = (
        lax.all_gather(qkv_weight.astype(jnp.bfloat16), ("ctx", "fsdp"), axis=0, tiled=True),
        lax.all_gather(out_weight.astype(jnp.bfloat16), ("ctx", "fsdp"), axis=0, tiled=True),
    )
    grad_branch, grad_gain_attend = attend_back(grad_hidden)
    grad_branch_low = grad_branch.astype(jnp.bfloat16)
    out_grad = contract_first(attended, grad_branch_low)
    grad_attended = (
        contract_last(grad_branch_low, out_back).astype(jnp.bfloat16).reshape(rows, H, HD)
    )
    scores_again = (
        jnp.einsum("thd,ld->thl", query, keys, preferred_element_type=jnp.float32) * scale
    )
    probs = jnp.exp(jnp.where(allowed, scores_again, -1e30) - log_total)
    grad_probs = jnp.einsum(
        "thd,ld->thl", grad_attended, values, preferred_element_type=jnp.float32
    )
    row_term = jnp.sum(probs * grad_probs, axis=-1, keepdims=True)
    grad_scores = (probs * (grad_probs - row_term)).astype(jnp.bfloat16)
    grad_query = (
        jnp.einsum("thl,ld->thd", grad_scores, keys, preferred_element_type=jnp.float32) * scale
    )
    grad_keys = (
        jnp.einsum("thl,thd->ld", grad_scores, query, preferred_element_type=jnp.float32) * scale
    )
    grad_values = jnp.einsum(
        "thl,thd->ld", probs.astype(jnp.bfloat16), grad_attended, preferred_element_type=jnp.float32
    )
    empty = jnp.zeros((front + length, HD), jnp.float32)
    keys_spread = lax.dynamic_update_slice_in_dim(empty, grad_keys, first_row, 0)[front:]
    values_spread = lax.dynamic_update_slice_in_dim(empty, grad_values, first_row, 0)[front:]
    grad_key, grad_value = (
        lax.psum_scatter(keys_spread, "ctx", scatter_dimension=0, tiled=True),
        lax.psum_scatter(values_spread, "ctx", scatter_dimension=0, tiled=True),
    )
    grad_proj_query, grad_proj_key, grad_gain_query, grad_gain_key = rotate_back(
        (grad_query, grad_key)
    )
    grad_projected = jnp.concatenate(
        [grad_proj_query.reshape(rows, query_width), grad_proj_key, grad_value], axis=1
    ).astype(jnp.bfloat16)
    qkv_grad = contract_first(grad_projected, normed_low)
    grad_normed = jnp.dot(grad_projected, qkv_back, preferred_element_type=jnp.float32)
    grad_from_input, grad_gain_input = input_back(grad_normed)
    input_grad = grad_hidden + grad_from_input
    gains_grad = jnp.concatenate(
        [
            grad_gain_input,
            grad_gain_attend,
            grad_gain_pre,
            grad_gain_post,
            grad_gain_query,
            grad_gain_key,
        ]
    )
    qkv_part, out_part, gains_part = (
        lax.psum_scatter(qkv_grad, ("ctx", "fsdp"), scatter_dimension=0, tiled=True),
        lax.psum_scatter(out_grad, ("ctx", "fsdp"), scatter_dimension=0, tiled=True),
        lax.psum_scatter(gains_grad, ("ctx", "fsdp"), scatter_dimension=0, tiled=True),
    )
    qkv_total, out_total, gate_up_total, down_total, gains_total = (
        lax.psum(qkv_part.astype(jnp.bfloat16), "dp").astype(jnp.float32),
        lax.psum(out_part.astype(jnp.bfloat16), "dp").astype(jnp.float32),
        lax.psum(gate_up_part.astype(jnp.bfloat16), "dp").astype(jnp.float32),
        lax.psum(down_part.astype(jnp.bfloat16), "dp").astype(jnp.float32),
        lax.psum(gains_part.astype(jnp.bfloat16), "dp").astype(jnp.float32),
    )
    qkv_new, qkv_first_new, qkv_second_new = adamw(qkv_weight, qkv_total, qkv_first, qkv_second)
    out_new, out_first_new, out_second_new = adamw(out_weight, out_total, out_first, out_second)
    gate_up_new, gate_up_first_new, gate_up_second_new = adamw(
        gate_up_weight, gate_up_total, gate_up_first, gate_up_second
    )
    down_new, down_first_new, down_second_new = adamw(
        down_weight, down_total, down_first, down_second
    )
    gains_new, gains_first_new, gains_second_new = adamw(
        gains, gains_total, gains_first, gains_second
    )
    return (
        output[None],
        input_grad[None],
        qkv_total,
        out_total,
        gate_up_total,
        down_total,
        gains_total,
        qkv_new,
        out_new,
        gate_up_new,
        down_new,
        gains_new,
        qkv_first_new,
        out_first_new,
        gate_up_first_new,
        down_first_new,
        gains_first_new,
        qkv_second_new,
        out_second_new,
        gate_up_second_new,
        down_second_new,
        gains_second_new,
    )


def place():
    return lax.axis_index("dp"), lax.axis_index("ctx"), lax.axis_index("fsdp")


class Links:
    def __init__(self, send, recv):
        self.send, self.recv, self.used, self.sent, self.some = send, recv, 0, [], []

    def slot(self):
        self.used += 1
        return self.send.at[self.used - 1], self.recv.at[self.used - 1]

    def make(self, source, target, device):
        send, recv = self.slot()
        return pltpu.make_async_remote_copy(
            src_ref=source,
            dst_ref=target,
            send_sem=send,
            recv_sem=recv,
            device_id=device,
            device_id_type=MESH,
        )

    def go(self, source, target, device):
        copy = self.make(source, target, device)
        copy.start()
        self.sent.append(copy)
        return copy

    def go_if(self, condition, source, target, device):
        copy = self.make(source, target, device)
        pl.when(condition)(copy.start)
        self.some.append((condition, copy))
        return copy

    def drain(self):
        for copy in self.sent:
            copy.wait_send()
        for condition, copy in self.some:
            pl.when(condition)(copy.wait_send)
        self.sent, self.some = [], []


TILE = 16
AXES = (1, 2, 4)
ORDERS = ((0, 1, 2), (1, 2, 0), (2, 0, 1))


class Cube:
    def __init__(self, links, tiles):
        dp, ctx, x = place()
        self.links, self.tiles = links, tiles
        self.me = (ctx % 4) * 2 + x
        self.peers = (
            (dp, ctx, 1 - x),
            (dp, ctx + 1 - 2 * (ctx % 2), x),
            (dp, ctx + 2 - 4 * (ctx // 2 % 2), x),
        )
        third = -(-tiles // 3)
        self.parts = ((0, third), (third, third), (2 * third, tiles - 2 * third))

    def block(self, mask):
        result = 0
        for bit in AXES:
            own = self.me // bit % 2
            result = result + bit * (1 - own if mask & bit else own)
        return result

    def cut(self, buf, p, mask):
        start, size = self.parts[p]
        return buf.at[pl.ds(self.block(mask) * self.tiles + start, size)]

    def gather(self, buf):
        sent = {}

        def go(p, index, mask, dim):
            ref = self.cut(buf, p, mask)
            sent[p, index] = self.links.go(ref, ref, self.peers[dim])

        for index, where in ((0, 0), (1, 1), (3, 2)):
            for p, order in enumerate(ORDERS):
                go(p, index, 0, order[where])
        for p, (a, b, c) in enumerate(ORDERS):
            sent[p, 0].wait_recv()
            go(p, 2, AXES[a], b)
            go(p, 4, AXES[a], c)
        for p, (a, b, c) in enumerate(ORDERS):
            sent[p, 1].wait_recv()
            go(p, 5, AXES[b], c)
            sent[p, 2].wait_recv()
            go(p, 6, AXES[a] | AXES[b], c)
        for index in (3, 4, 5, 6):
            for p in range(3):
                sent[p, index].wait_recv()

    def scatter(self, buf, one, two, three, beside=None):
        sent = {}

        def go(p, index, mask, slot, dim):
            start, size = self.parts[p]
            target = slot.at[pl.ds(start, size)]
            sent[p, index] = self.links.go(self.cut(buf, p, mask), target, self.peers[dim])

        def add(p, mask, slot):
            start, size = self.parts[p]
            mine = self.cut(buf, p, mask)
            mine[...] = (mine[...].astype(F32) + slot[pl.ds(start, size)].astype(F32)).astype(BF)

        for index in range(4):
            for p, (a, b, c) in enumerate(ORDERS):
                mask = (AXES[b], AXES[b] | AXES[a], AXES[a], 0)[index]
                go(p, index, AXES[c] | mask, one.at[index], c)
        if beside is not None:
            beside()
        for index in range(2):
            for p, (a, b, c) in enumerate(ORDERS):
                mask = AXES[b] | (AXES[a], 0)[index]
                sent[p, 1 - index].wait_recv()
                add(p, mask, one.at[1 - index])
                go(p, 4 + index, mask, two.at[index], b)
        for p, (a, b, c) in enumerate(ORDERS):
            sent[p, 2].wait_recv()
            add(p, AXES[a], one.at[2])
            sent[p, 4].wait_recv()
            add(p, AXES[a], two.at[0])
            go(p, 6, AXES[a], three, a)
        for p in range(3):
            sent[p, 3].wait_recv()
            add(p, 0, one.at[3])
            sent[p, 5].wait_recv()
            add(p, 0, two.at[1])
            sent[p, 6].wait_recv()


def flat(value):
    return value.reshape(-1, value.shape[-1])


def tiled(value):
    return value.reshape(-1, TILE, value.shape[-1])


def norm_scale(value):
    return lax.rsqrt(jnp.mean(value * value, axis=-1, keepdims=True) + 1e-06)


def norm_back(value, scale, gained):
    inner = jnp.mean(gained * value, axis=-1, keepdims=True)
    return scale * gained - value * (scale * scale * scale * inner)


ROOT = 0.7978845608028654


def gelu_parts(v):
    t = jnp.tanh(ROOT * (v + 0.044715 * (v * v * v)))
    value = 0.5 * v * (1.0 + t)
    slope = 0.5 * (1.0 + t) + 0.5 * v * (1.0 - t * t) * (ROOT * (1.0 + 0.134145 * (v * v)))
    return value, slope


def add_low(left, right):
    return (left.astype(F32) + right.astype(F32)).astype(BF)


def layer_kernel(
    tok,
    cot,
    seg,
    gpad,
    wq,
    wo,
    wgu_in,
    wd_in,
    output,
    input_grad,
    rq,
    ro,
    rg,
    rgu,
    rd,
    qkv_w,
    out_w,
    gains,
    wgu,
    wd,
    stage,
    acts,
    downs,
    ff,
    mixed,
    sums,
    one,
    two,
    three,
    pairs,
    query,
    proj,
    probs,
    attended,
    xn,
    turn,
    dscores,
    dpairs,
    kv_in,
    kv_sum,
    kv_far,
    pool,
    q_two,
    o_two,
    q_far,
    o_far,
    g_in,
    g_sum,
    gu_in,
    gu_far,
    d_in,
    d_far,
    send,
    recv,
    local,
):
    dp, ctx, x = place()
    rows, width = tok.shape
    layers = pairs.shape[0]
    length = seg.shape[0] * seg.shape[1]
    tiles = rows // TILE
    hq, ho = qkv_w.shape[4], out_w.shape[4]
    tq, to = hq // TILE, ho // TILE
    half = wd_in.shape[0]
    units = 2 * half
    thalf = half // TILE
    wide = wd.shape[0] * TILE
    query_width = H * HD
    scale = HD ** (-0.5)
    z, y = ctx // 2, ctx % 2
    cube_of = ctx // 4
    links = Links(send, recv)
    cube = Cube(links, tiles)
    sibling = (1 - dp, ctx, x)
    beside = (dp, z * 2 + 1 - y, x)
    across = (dp, lax.rem(ctx + 4, 8), x)
    others = [(dp, lax.rem(z + step, layers) * 2 + y, x) for step in range(1, layers)]
    y2, x2 = jnp.where(dp == 0, 1 - y, y), jnp.where(dp == 0, x, 1 - x)
    y3, x3 = jnp.where(dp == 0, y, 1 - y), jnp.where(dp == 0, 1 - x, x)
    mine2, mine3 = jnp.where(dp == 0, y, x), jnp.where(dp == 0, x, y)
    second = (dp, z * 2 + y2, x2)
    third = (dp, z * 2 + y3, x3)
    group = (ctx % 4) * 2 + x
    user = (x, ctx // 2 + 4 * dp, ctx % 2)
    owner = (cube_of, group, dp)
    stays_in = (dp == x) & (ctx == ctx // 2 + 4 * dp) & (x == ctx % 2)
    stays_back = (dp == cube_of) & (ctx == group)  & (x == dp)

    def bring(source, first, index):
        copy = pltpu.make_async_copy(
            source, stage.at[pl.ds(first, source.shape[0])], local.at[index]
        )
        copy.start()
        return copy

    bring_q = bring(wq, 0, 0)
    bring_o = bring(wo, 2 * hq, 1)
    bring_gu = bring(wgu_in.at[pl.ds(dp * half, half)], 2 * hq + 2 * ho, 2)

    pairs[...] = jnp.zeros(pairs.shape, BF)
    barrier = pltpu.get_barrier_semaphore()
    for device in others + [second, third, sibling, cube.peers[2]]:
        pl.semaphore_signal(barrier, inc=1, device_id=device, device_id_type=MESH)

    @pl.when(jnp.logical_not(stays_in))
    def _():
        for device in (user, owner):
            pl.semaphore_signal(barrier, inc=1, device_id=device, device_id_type=MESH)

    gains[z, y, x, dp] = gpad[dp]
    bring_q.wait()
    qkv_w[z, y, x, dp] = stage[pl.ds(dp * hq, hq), :].astype(BF)
    pl.semaphore_wait(barrier, jnp.where(stays_in, layers + 3, layers + 5))
    fulls = (gains, qkv_w, out_w)

    def first_steps(full):
        part = full.at[z, y, x, dp]
        return [links.go(part, part, device) for device in others]

    def pass_on(zz, yy, xx, *devices):
        part = qkv_w.at[zz, yy, xx, dp]
        return [links.go(part, part, device) for device in devices]

    firsts = [first_steps(gains), first_steps(qkv_w)]
    passed = [pass_on(z, y, x, second, third, sibling)]
    bring_o.wait()
    out_w[z, y, x, dp] = stage[pl.ds(2 * hq + dp * ho, ho), :].astype(BF)
    bring_gu.wait()
    low = 2 * hq + 2 * ho
    wgu[cube_of, pl.ds(dp * half, half), :] = stage[low : low + half, :].astype(BF)
    bring_d = bring(wd_in, 0, 3)

    row_id = lax.broadcasted_iota(jnp.int32, (rows, rows), 0)
    lane_id = lax.broadcasted_iota(jnp.int32, (rows, rows), 1)
    own_ids = seg[pl.ds(ctx, 1), :]
    ids = jnp.sum(jnp.where(row_id == lane_id, own_ids, 0), axis=1, keepdims=True)
    start = jnp.zeros((rows, 1), jnp.int32)
    for b in range(length // rows):
        start = start + jnp.sum((seg[b : b + 1, :] < ids).astype(jnp.int32), axis=1, keepdims=True)
    position = ctx * rows + lax.broadcasted_iota(jnp.int32, (rows, 1), 0)
    offset = (position - start).astype(F32)
    lane = lax.broadcasted_iota(jnp.int32, (1, HD // 2), 1).astype(F32)
    angle = offset * jnp.exp(lane * (-2.0 * 13.815510557964274 / HD))
    turn[0] = jnp.cos(angle)
    turn[1] = jnp.sin(angle)

    bring_d.wait()
    d_in[...] = tiled(stage[0:half, :].astype(BF))
    bring_rest = bring(wgu_in.at[pl.ds((1 - dp) * half, half)], 0, 4)
    bring_rest.wait()
    wgu[cube_of, pl.ds((1 - dp) * half, half), :] = stage[0:half, :].astype(BF)
    wgu[:, units:, :] = jnp.zeros((2, wide - units, width), BF)
    wd[2 * thalf :] = jnp.zeros((wide // TILE - 2 * thalf, TILE, width), BF)

    sib, seconds, thirds = {0: [], 2: []}, {}, {}

    def second_steps(t):
        for copy in firsts[t]:
            copy.wait_recv()
        line = fulls[t].at[:, y, x, dp]
        seconds[t] = links.go(line, line, second)
        thirds[t] = [links.go(line, line, third)]
        sib[t].append(links.go(line, line, sibling))

    def third_steps(t):
        seconds[t].wait_recv()
        line = fulls[t].at[:, y2, x2, dp]
        thirds[t].append(links.go(line, line, third))
        sib[t].append(links.go(line, line, sibling))

    def last_steps(t):
        for copy, (yy, xx) in zip(thirds[t], ((y3, x3), (1 - y, 1 - x))):
            copy.wait_recv()
            line = fulls[t].at[:, yy, xx, dp]
            sib[t].append(links.go(line, line, sibling))

    second_steps(0)
    behind = [lax.rem(z + layers - 1 - i, layers) for i in range(layers - 1)]
    for i, copy in enumerate(firsts[1]):
        copy.wait_recv()
        passed.append(pass_on(behind[i], y, x, second, third, sibling))
    own_down = wd.at[pl.ds(x * thalf, thalf)]
    down_local = pltpu.make_async_copy(d_in, own_down, local.at[5])
    down_move = links.make(d_in, own_down, user)

    @pl.when(stays_in)
    def _():
        down_local.start()

    @pl.when(jnp.logical_not(stays_in))
    def _():
        down_move.start()

    firsts.append(first_steps(out_w))
    third_steps(0)
    line_order = [z] + behind
    far = []
    for i, zz in enumerate(line_order):
        passed[i][0].wait_recv()
        far.append(pass_on(zz, y2, x2, third, sibling))
    last_steps(0)
    ends_q = []
    for i, zz in enumerate(line_order):
        passed[i][1].wait_recv()
        ends_q += pass_on(zz, y3, x3, sibling)
        far[i][0].wait_recv()
        ends_q += pass_on(zz, 1 - y, 1 - x, sibling)
    second_steps(2)
    ends_q += [copies[2] for copies in passed] + [copies[1] for copies in far]
    for copy in ends_q + sib[0]:
        copy.wait_recv()

    total = jnp.zeros(gains.shape[-2:], F32)
    for h in range(2):
        part = jnp.zeros(gains.shape[-2:], F32)
        for zz in range(layers):
            for yy in range(2):
                for xx in range(2):
                    part = part + gains[zz, yy, xx, h]
        g_in[0, h * part.shape[0] : (h + 1) * part.shape[0], :] = part

    def gain_row(first, size):
        lo = first // 128
        return 1.0 + jnp.concatenate(
            [g_in[0, lo + i : lo + i + 1, :] for i in range(size // 128)], axis=1
        )

    gain_in = gain_row(0, width)
    gain_query = gain_row(4 * width, HD)
    gain_key = gain_row(4 * width + HD, HD)

    value = tok[...].astype(F32)
    xn[...] = (value * norm_scale(value) * gain_in).astype(BF)
    proj[...] = contract_last(xn[...], flat(qkv_w[...]))

    def turned(part, gain):
        part = part * norm_scale(part) * gain
        first, last = part[:, : HD // 2], part[:, HD // 2 :]
        cosine, sine = turn[0], turn[1]
        return jnp.concatenate(
            [first * cosine - last * sine, last * cosine + first * sine], axis=1
        )

    pairs[z, y, :, :HD] = turned(proj[:, query_width : query_width + HD], gain_key).astype(BF)
    pairs[z, y, :, HD:] = proj[:, query_width + HD :].astype(BF)
    own_pairs = pairs.at[z, y]
    upper = (dp, lax.rem(z + 1, layers) * 2 + y, x)
    rises = z < layers - 1
    pair_up = [links.go_if(rises, own_pairs, own_pairs, upper)]
    pair_side = [links.go(own_pairs, own_pairs, beside)]
    for h in range(H):
        query[h * rows : (h + 1) * rows, :] = turned(
            proj[:, h * HD : (h + 1) * HD], gain_query
        ).astype(BF)
    third_steps(2)
    for k in range(1, layers):
        below = z >= k
        part = pairs.at[lax.rem(z + layers - k, layers), y]
        pl.when(below)(pair_up[k - 1].wait_recv)
        if k < layers - 1:
            pair_up.append(links.go_if(below & rises, part, part, upper))
        pair_side.append(links.go_if(below, part, part, beside))
    last_steps(2)
    pair_side[0].wait_recv()
    for k in range(1, layers):
        pl.when(z >= k)(pair_side[k].wait_recv)

    half_rows = wgu.at[cube_of, pl.ds(dp * half, half)]
    gu_cross = links.go(half_rows, half_rows, across)
    def allowed(b):
        key_pos = b * rows + lax.broadcasted_iota(jnp.int32, (1, rows), 1)
        return (key_pos <= position) & (seg[b : b + 1, :] == ids)

    keep = jnp.concatenate([allowed(b) for b in range(length // rows)], axis=1)
    keys = flat(pairs[:, :, :, :HD])
    values = flat(pairs[:, :, :, HD:])
    for h in range(H):
        part = slice(h * rows, (h + 1) * rows)
        scores = jnp.where(keep, contract_last(query[part, :], keys) * scale, -1e30)
        largest = jnp.max(scores, axis=-1, keepdims=True)
        raised = jnp.exp(scores - largest)
        p = raised / jnp.sum(raised, axis=-1, keepdims=True)
        probs[part, :] = p
        attended[:, h * HD : (h + 1) * HD] = jnp.dot(
            p.astype(BF), values, preferred_element_type=F32
        ).astype(BF)
    for copy in sib[2]:
        copy.wait_recv()
    branch = stage.at[0:rows]
    hidden = stage.at[rows : 2 * rows]
    grad_hidden = stage.at[2 * rows : 3 * rows]
    branch[...] = jnp.dot(attended[...], flat(out_w[...]), preferred_element_type=F32)
    gain_attend = gain_row(width, width)
    value = branch[...]
    hidden[...] = tok[...].astype(F32) + value * norm_scale(value) * gain_attend
    value = hidden[...]
    gain_pre = gain_row(2 * width, width)
    gain_post = gain_row(3 * width, width)

    def block_of(buf, j):
        return flat(buf[pl.ds(j * tiles, tiles)])

    def put_block(buf, j, block):
        buf[pl.ds(j * tiles, tiles)] = tiled(block)

    me = cube.me
    put_block(acts, me, (value * norm_scale(value) * gain_pre).astype(BF))
    cube.gather(acts)
    pair = 2

    def pair_of(buf, j):
        return flat(buf[pl.ds(j * pair * tiles, pair * tiles)])

    def put_pair(buf, j, block):
        buf[pl.ds(j * pair * tiles, pair * tiles)] = tiled(block)

    def spread(block):
        return block.reshape(pair, rows, block.shape[-1])

    def near(j, carry):
        ff[cube_of, pl.ds(j * pair, pair)] = spread(
            contract_last(pair_of(acts, j), wgu[cube_of])
        )
        return carry

    lax.fori_loop(0, 8 // pair, near, 0)
    gu_cross.wait_recv()
    landed = wgu.at[1 - cube_of, pl.ds(dp * half, half)]
    links.go(landed, landed, sibling).wait_recv()

    def forward(j, carry):
        here = pl.ds(j * pair, pair)
        ff[1 - cube_of, here] = spread(contract_last(pair_of(acts, j), wgu[1 - cube_of]))
        mixed[here] = (gelu_parts(ff[0, here])[0] * ff[1, here]).astype(BF)
        return carry

    lax.fori_loop(0, 8 // pair, forward, 0)

    @pl.when(stays_in)
    def _():
        down_local.wait()

    @pl.when(jnp.logical_not(stays_in))
    def _():
        down_move.wait_send()

    @pl.when(jnp.logical_not(stays_in))
    def _():
        down_move.wait_recv()

    landed = wd.at[pl.ds(dp * thalf, thalf)]
    links.go(landed, landed, sibling).wait_recv()

    def project(j, carry):
        m = flat(mixed[pl.ds(j * pair, pair)])
        put_pair(sums, j, jnp.dot(m, flat(wd[...]), preferred_element_type=F32).astype(BF))
        return carry

    lax.fori_loop(0, 8 // pair, project, 0)
    links.drain()
    cube.scatter(sums, one, two, three)
    links.drain()
    down = block_of(sums, me).astype(F32) + flat(three[...]).astype(F32)
    down_scale = norm_scale(down)
    normal = down * down_scale
    output[...] = (hidden[...] + normal * gain_post).astype(BF)
    dy = cot[...].astype(F32)
    put_block(downs, me, norm_back(down, down_scale, dy * gain_post).astype(BF))

    def put_gain(first, row):
        lo = first // 128
        for i in range(row.shape[1] // 128):
            g_sum[0, lo + i : lo + i + 1, :] = row[:, i * 128 : (i + 1) * 128]

    g_sum[0] = jnp.zeros(g_sum.shape[1:], F32)
    put_gain(3 * width, jnp.sum(dy * normal, axis=0, keepdims=True))
    cube.gather(downs)

    def put_rows(first, limit, block):
        kept = min(block.shape[0], limit)
        pool[first // TILE : (first + kept) // TILE] = tiled(block[:kept].astype(BF))

    downs_all = flat(downs[...])
    acts_all = flat(acts[...])
    tokens = 8 * rows
    for lo in range(0, wide, 128):
        cut = slice(lo, lo + 128)
        mx = mixed[:, :, cut].reshape(tokens, 128)
        put_rows(2 * units + lo, units - lo, contract_first(mx, downs_all))

    def slab(first, size):
        return pool.at[pl.ds(first, size)]

    d_swap = links.go(slab(4 * thalf + (1 - dp) * thalf, thalf), d_in, sibling)

    def backward(j, carry):
        here = pl.ds(j * pair, pair)
        d = spread(contract_last(pair_of(downs, j), flat(wd[...])))
        value, slope = gelu_parts(ff[0, here])
        dg = (d * ff[1, here] * slope).astype(BF)
        du = (d * value).astype(BF)
        ff[0, here] = dg.astype(F32)
        ff[1, here] = du.astype(F32)
        put_pair(
            sums,
            j,
            (
                jnp.dot(flat(dg), wgu[0], preferred_element_type=F32)
                + jnp.dot(flat(du), wgu[1], preferred_element_type=F32)
            ).astype(BF),
        )
        return carry

    links.drain()
    lax.fori_loop(0, 8 // pair, backward, 0)
    moved = {}

    def weights():
        d_swap.wait_recv()
        d_in[...] = add_low(d_in[...], pool[pl.ds(4 * thalf + dp * thalf, thalf)])
        moved["local"] = pltpu.make_async_copy(d_in, d_far.at[cube_of], local.at[6])
        moved["down"] = links.make(d_in, d_far.at[cube_of], owner)

        @pl.when(stays_back)
        def _():
            moved["local"].start()

        @pl.when(jnp.logical_not(stays_back))
        def _():
            moved["down"].start()

        for lo in range(0, wide, 128):
            cut = slice(lo, lo + 128)
            for i in range(2):
                grad = ff[i, :, :, cut].reshape(tokens, 128).astype(BF)
                put_rows(i * units + lo, units - lo, contract_first(grad, acts_all))
        swap = [
            links.go(slab(i * 2 * thalf + (1 - dp) * thalf, thalf), gu_in.at[i], sibling)
            for i in range(2)
        ]
        for i in range(2):
            swap[i].wait_recv()
            gu_in[i] = add_low(gu_in[i], pool[pl.ds(i * 2 * thalf + dp * thalf, thalf)])
        moved["gu"] = links.go(gu_in.at[1 - cube_of], gu_far, across)

    cube.scatter(sums, one, two, three, weights)
    value = hidden[...]
    hidden_scale = norm_scale(value)
    total = block_of(sums, me).astype(F32) + flat(three[...]).astype(F32)
    put_gain(2 * width, jnp.sum(total * (value * hidden_scale), axis=0, keepdims=True))
    grad = cot[...].astype(F32) + norm_back(value, hidden_scale, total * gain_pre)
    grad_hidden[...] = grad
    value = branch[...]
    branch_scale = norm_scale(value)
    put_gain(width, jnp.sum(grad * (value * branch_scale), axis=0, keepdims=True))
    grad_branch = norm_back(value, branch_scale, grad * gain_attend).astype(BF)
    links.drain()

    class Reduce:
        def __init__(self, base, count, layers_in, came, one_in, two_in, far_in):
            self.base, self.count, self.layers_in = base, count, layers_in
            self.size = len(layers_in)
            self.per = 4 * self.size * count
            self.quarter = self.per // 4
            self.came, self.one_in, self.two_in, self.far_in = came, one_in, two_in, far_in
            self.whole = self.size == layers
            self.takes = (z >= layers_in[0]) & (z <= layers_in[-1])

        def put(self, block):
            size = self.count * TILE
            for zi in range(self.size):
                for yy in range(2):
                    for xx in range(2):
                        for h in range(2):
                            a, b = (yy, xx) if h == 0 else (xx, yy)
                            first = (((zi * 2 + yy) * 2 + xx) * 2 + h) * size
                            spot = (b * 2 + a) * self.size + zi
                            at = self.base + h * self.per + spot * self.count
                            pool[at : at + self.count] = tiled(
                                block[first : first + size].astype(BF)
                            )
            self.swap = links.go(
                slab(self.base + (1 - dp) * self.per, self.per), self.came, sibling
            )

        def on_chip(self):
            self.swap.wait_recv()
            mine = pl.ds(self.base + dp * self.per, self.per)
            pool[mine] = add_low(pool[mine], self.came[...])
            away = self.base + dp * self.per + (1 - mine3) * 2 * self.quarter
            self.at = self.base + dp * self.per + mine3 * 2 * self.quarter
            self.steps = []
            for a in (1 - mine2, mine2):
                cut = pl.ds(a * self.quarter, self.quarter)
                part = slab(away + a * self.quarter, self.quarter)
                self.steps.append((a, links.go(part, self.one_in.at[cut], third)))

        def across_third(self):
            for i, (a, copy) in enumerate(self.steps):
                copy.wait_recv()
                near = pl.ds(self.at + a * self.quarter, self.quarter)
                cut = pl.ds(a * self.quarter, self.quarter)
                pool[near] = add_low(pool[near], self.one_in[cut])
                if i == 0:
                    self.step = links.go(pool.at[near], self.two_in, second)
            self.at = self.at + mine2 * self.quarter

        def across_second(self):
            self.step.wait_recv()
            near = pl.ds(self.at, self.quarter)
            pool[near] = add_low(pool[near], self.two_in[...])
            self.fars = []
            for i, device in enumerate(others):
                to_layer = lax.rem(z + i + 1, layers)
                if self.whole:
                    part = slab(self.at + to_layer * self.count, self.count)
                    self.fars.append(links.go(part, self.far_in.at[i], device))
                    continue
                inside = (to_layer >= self.layers_in[0]) & (to_layer <= self.layers_in[-1])
                index = jnp.where(inside, to_layer - self.layers_in[0], 0)
                part = slab(self.at + index * self.count, self.count)
                self.fars.append(links.go_if(inside, part, self.far_in.at[i], device))

        def along(self, result):
            def add():
                index = z if self.whole else z - self.layers_in[0]
                value = pool[pl.ds(self.at + index * self.count, self.count)].astype(F32)
                for i, copy in enumerate(self.fars):
                    copy.wait_recv()
                    value = value + self.far_in[i].astype(F32)
                result[dp] = value.astype(BF)

            if self.whole:
                add()
            else:
                pl.when(self.takes)(add)

    per_qkv = 2 * layers * tq
    q_buf = downs.at[pl.ds(0, 2 * per_qkv)]
    o_in = acts.at[pl.ds(0, 4 * layers * to)]
    q_one = acts.at[pl.ds(4 * layers * to, per_qkv)]
    o_one = downs.at[pl.ds(2 * per_qkv, 2 * layers * to)]
    few = layers // 2
    sets = [
        Reduce(
            i * 2 * per_qkv,
            tq,
            tuple(range(i * few, (i + 1) * few)),
            q_buf.at[pl.ds(i * per_qkv, per_qkv)],
            q_one.at[pl.ds(i * per_qkv // 2, per_qkv // 2)],
            q_two.at[pl.ds(i * per_qkv // 4, per_qkv // 4)],
            q_far,
        )
        for i in range(2)
    ]
    outs = Reduce(4 * per_qkv, to, tuple(range(layers)), o_in, o_one, o_two, o_far)
    outs.put(contract_first(attended[...], grad_branch))
    grad_att = contract_last(grad_branch, flat(out_w[...])).astype(BF)
    for h in range(H):
        part = slice(h * rows, (h + 1) * rows)
        p = probs[part, :]
        grad_p = contract_last(grad_att[:, h * HD : (h + 1) * HD], values)
        row = jnp.sum(p * grad_p, axis=-1, keepdims=True)
        dscores[part, :] = (p * (grad_p - row)).astype(BF)
    grad_heads = jnp.concatenate([grad_att[:, h * HD : (h + 1) * HD] for h in range(H)], axis=0)
    grad_keys = contract_first(dscores[...], query[...]) * scale
    dpairs[:, :, :, :HD] = grad_keys.astype(BF).reshape(layers, 2, rows, HD)
    grad_values = contract_first(probs[...].astype(BF), grad_heads)
    dpairs[:, :, :, HD:] = grad_values.astype(BF).reshape(layers, 2, rows, HD)
    kv_lines = [
        links.go_if(z >= zz, dpairs.at[zz, 1 - y], kv_in.at[zz], beside) for zz in range(layers)
    ]

    def turned_back(part, gain, grad):
        cosine, sine = turn[0], turn[1]
        first, last = grad[:, : HD // 2], grad[:, HD // 2 :]
        grad = jnp.concatenate(
            [first * cosine + last * sine, last * cosine - first * sine], axis=1
        )
        part_scale = norm_scale(part)
        gain_term = jnp.sum(grad * (part * part_scale), axis=0, keepdims=True)
        return norm_back(part, part_scale, grad * gain), gain_term

    outs.on_chip()
    query_term = jnp.zeros((1, HD), F32)
    grads = []
    for h in range(H):
        part = slice(h * rows, (h + 1) * rows)
        grad_query = jnp.dot(dscores[part, :], keys, preferred_element_type=F32) * scale
        grad, term = turned_back(proj[:, h * HD : (h + 1) * HD], gain_query, grad_query)
        grads.append(grad.astype(BF))
        query_term = query_term + term
    put_gain(4 * width, query_term)
    grad_queries = jnp.concatenate(grads, axis=1)
    half_cols = (H + 2) * HD // 2

    kv_copies = []
    for i, device in enumerate(others):
        to_layer = lax.rem(z + i + 1, layers)
        copy = links.make(kv_sum.at[to_layer], kv_far.at[i], device)
        links.some.append((to_layer < z, copy))
        kv_copies.append((to_layer, copy))
    for zz in range(layers):

        @pl.when(z >= zz)
        def _():
            kv_lines[zz].wait_recv()
            kv_sum[zz] = add_low(kv_in[zz], dpairs[zz, y])

        for to_layer, copy in kv_copies:
            pl.when((to_layer == zz) & (z > zz))(copy.start)
    sets[0].put(contract_first(grad_queries[:, :half_cols], xn[...]))
    outs.across_third()
    sets[0].on_chip()
    kv_total = stage.at[3 * rows : 4 * rows, 0 : 2 * HD]
    kv_total[...] = kv_sum[z].astype(F32)
    for i, (_, copy) in enumerate(kv_copies):

        @pl.when(behind[i] > z)
        def _():
            copy.wait_recv()
            kv_total[...] += kv_far[i].astype(F32)

    grad_pair = kv_total[...]
    grad, term = turned_back(
        proj[:, query_width : query_width + HD], gain_key, grad_pair[:, :HD]
    )
    put_gain(4 * width + HD, term)
    grad_proj = jnp.concatenate(
        [grad_queries, grad.astype(BF), grad_pair[:, HD:].astype(BF)], axis=1
    )
    sets[1].put(contract_first(grad_proj[:, half_cols:], xn[...]))
    sets[0].across_third()
    sets[1].on_chip()
    grad_normed = jnp.dot(grad_proj, flat(qkv_w[...]), preferred_element_type=F32)
    value = tok[...].astype(F32)
    in_scale = norm_scale(value)
    put_gain(0, jnp.sum(grad_normed * (value * in_scale), axis=0, keepdims=True))
    g_swap = links.go(g_sum.at[0], g_in.at[1], sibling)
    input_grad[...] = grad_hidden[...] + norm_back(value, in_scale, grad_normed * gain_in)
    outs.across_second()
    g_swap.wait_recv()
    g_sum[1] = g_sum[0] + g_in[1]
    g_x = links.go(g_sum.at[1], g_in.at[2], cube.peers[0])
    sets[0].across_second()
    sets[1].across_third()
    g_x.wait_recv()
    g_sum[2] = g_sum[1] + g_in[2]
    g_y = links.go(g_sum.at[2], g_in.at[3], beside)
    sets[1].across_second()
    g_y.wait_recv()
    g_sum[3] = g_sum[2] + g_in[3]
    g_in[4 + z] = g_sum[3]
    g_z = [links.go(g_sum.at[3], g_in.at[4 + z], device) for device in others]
    ends = []
    outs.along(ro)
    ends.append(links.go(ro.at[dp], ro.at[dp], sibling))
    sets[0].along(rq)
    sets[1].along(rq)
    ends.append(links.go(rq.at[dp], rq.at[dp], sibling))
    for copy in g_z:
        copy.wait_recv()
    value = g_in[4]
    for i in range(1, layers):
        value = value + g_in[4 + i]
    rg[...] = value

    @pl.when(stays_back)
    def _():
        moved["local"].wait()

    @pl.when(jnp.logical_not(stays_back))
    def _():
        moved["down"].wait_send()

    @pl.when(jnp.logical_not(stays_back))
    def _():
        moved["down"].wait_recv()

    landed = d_far.at[dp]
    d_end = links.go(landed, landed, sibling)
    d_end.wait_recv()
    d_in[...] = add_low(d_far[0], d_far[1])
    keep_d = pltpu.make_async_copy(d_in, rd, local.at[7])
    keep_d.start()
    moved["gu"].wait_recv()
    gu_far[...] = add_low(gu_in[cube_of], gu_far[...])
    keep_gu = pltpu.make_async_copy(gu_far, rgu.at[dp], local.at[8])
    keep_gu.start()
    ends.append(links.go(gu_far, rgu.at[dp], sibling))
    for copy in ends:
        copy.wait_recv()
    keep_d.wait()
    keep_gu.wait()
    links.drain()


def whole_layer(tok, cot, seg, gpad, wq, wo, wgu, wd, layers):
    rows, width = tok.shape
    units = 2 * wd.shape[0]
    wide = -(-units // 128) * 128
    hq, ho, half = wq.shape[0] // 2, wo.shape[0] // 2, wd.shape[0]
    tq, to, thalf, tiles = hq // TILE, ho // TILE, half // TILE, rows // TILE
    gain_rows = gpad.shape[0] * gpad.shape[1]
    length = seg.shape[0] * seg.shape[1]
    pool = max(6 * thalf, 8 * layers * (tq + to))

    def low(*shape):
        return pltpu.VMEM(shape, BF)

    def full(*shape):
        return pltpu.VMEM(shape, F32)

    def tile(*lead):
        return pltpu.VMEM(lead + (TILE, width), BF)

    return pl.pallas_call(
        layer_kernel,
        out_shape=(
            jax.ShapeDtypeStruct((rows, width), BF),
            jax.ShapeDtypeStruct((rows, width), F32),
            jax.ShapeDtypeStruct((2, tq, TILE, width), BF),
            jax.ShapeDtypeStruct((2, to, TILE, width), BF),
            jax.ShapeDtypeStruct((gain_rows, 128), F32),
            jax.ShapeDtypeStruct((2, thalf, TILE, width), BF),
            jax.ShapeDtypeStruct((thalf, TILE, width), BF),
        ),
        in_specs=[VMEM] * 4 + [ANY] * 4,
        out_specs=(VMEM,) * 5 + (ANY, ANY),
        scratch_shapes=[
            low(layers, 2, 2, 2, hq, width),
            low(layers, 2, 2, 2, ho, width),
            full(layers, 2, 2, 2, gain_rows // 2, 128),
            low(2, wide, width),
            tile(wide // TILE),
            full(2 * hq + 2 * ho + half, width),
            tile(8 * tiles),
            tile(8 * tiles),
            full(2, 8, rows, wide),
            low(8, rows, wide),
            tile(8 * tiles),
            tile(4, tiles),
            tile(2, tiles),
            tile(tiles),
            low(layers, 2, rows, 2 * HD),
            low(H * rows, HD),
            full(rows, (H + 2) * HD),
            full(H * rows, length),
            low(rows, H * HD),
            low(rows, width),
            full(2, rows, HD // 2),
            low(H * rows, length),
            low(layers, 2, rows, 2 * HD),
            low(layers, rows, 2 * HD),
            low(layers, rows, 2 * HD),
            low(layers - 1, rows, 2 * HD),
            tile(pool),
            tile(layers * tq),
            tile(layers * to),
            tile(layers - 1, tq),
            tile(layers - 1, to),
            full(4 + layers, gain_rows, 128),
            full(4, gain_rows, 128),
            tile(2, thalf),
            tile(thalf),
            tile(thalf),
            tile(2, thalf),
            pltpu.SemaphoreType.DMA((220,)),
            pltpu.SemaphoreType.DMA((220,)),
            pltpu.SemaphoreType.DMA((9,)),
        ],
        compiler_params=pltpu.CompilerParams(
            collective_id=0, has_side_effects=True, vmem_limit_bytes=62 * 2**20
        ),
    )(tok, cot, seg, gpad, wq, wo, wgu, wd)


def moves_tokens(mesh):
    return mesh.shape["ctx"] == 8 and mesh.shape["fsdp"] == 2 and mesh.shape["dp"] == 2


def move_tokens_body(
    tokens,
    cotangent,
    segments,
    qkv_weight,
    out_weight,
    gate_up_weight,
    down_weight,
    gains,
    qkv_first,
    out_first,
    gate_up_first,
    down_first,
    gains_first,
    qkv_second,
    out_second,
    gate_up_second,
    down_second,
    gains_second,
):
    rows = tokens.shape[1]
    width = tokens.shape[2]
    layers = lax.axis_size("ctx") // 2
    chip = lax.axis_index("ctx") * 2 + lax.axis_index("fsdp")
    own_gains = gains.shape[0]
    gain_rows = -(-own_gains * 4 * layers // 1024) * 8 + 8
    gain_part = lax.dynamic_update_slice_in_dim(
        jnp.zeros((gain_rows * 128,), F32),
        gains.astype(BF).astype(F32),
        chip * own_gains,
        0,
    )
    output, input_grad, qkv_low, out_low, gains_sum, gate_up_low, down_low = whole_layer(
        tokens[0],
        cotangent[0],
        segments.reshape(-1, rows),
        gain_part.reshape(2, gain_rows // 2, 128),
        qkv_weight,
        out_weight,
        gate_up_weight,
        down_weight,
        layers,
    )
    qkv_total = qkv_low.reshape(-1, width).astype(F32)
    out_total = out_low.reshape(-1, width).astype(F32)
    gate_up_total = gate_up_low.reshape(-1, width).astype(F32)
    down_total = down_low.reshape(-1, width).astype(F32)
    gains_total = lax.dynamic_slice_in_dim(gains_sum.reshape(-1), chip * own_gains, own_gains, 0)
    qkv_new, qkv_first_new, qkv_second_new = adamw(qkv_weight, qkv_total, qkv_first, qkv_second)
    out_new, out_first_new, out_second_new = adamw(out_weight, out_total, out_first, out_second)
    gate_up_new, gate_up_first_new, gate_up_second_new = adamw(
        gate_up_weight, gate_up_total, gate_up_first, gate_up_second
    )
    down_new, down_first_new, down_second_new = adamw(
        down_weight, down_total, down_first, down_second
    )
    gains_new, gains_first_new, gains_second_new = adamw(
        gains, gains_total, gains_first, gains_second
    )
    return (
        output[None],
        input_grad[None],
        qkv_total,
        out_total,
        gate_up_total,
        down_total,
        gains_total,
        qkv_new,
        out_new,
        gate_up_new,
        down_new,
        gains_new,
        qkv_first_new,
        out_first_new,
        gate_up_first_new,
        down_first_new,
        gains_first_new,
        qkv_second_new,
        out_second_new,
        gate_up_second_new,
        down_second_new,
        gains_second_new,
    )


def solution(mesh):
    in_specs = (
        P(("dp", "fsdp"), "ctx", None),
        P(("dp", "fsdp"), "ctx", None),
        P(("dp", "fsdp"), None),
        P(("ctx", "fsdp"), None),
        P(("ctx", "fsdp"), None),
        P(("ctx", "fsdp"), None),
        P(("ctx", "fsdp"), None),
        P(("ctx", "fsdp")),
        P(("ctx", "fsdp"), None),
        P(("ctx", "fsdp"), None),
        P(("ctx", "fsdp"), None),
        P(("ctx", "fsdp"), None),
        P(("ctx", "fsdp")),
        P(("ctx", "fsdp"), None),
        P(("ctx", "fsdp"), None),
        P(("ctx", "fsdp"), None),
        P(("ctx", "fsdp"), None),
        P(("ctx", "fsdp")),
    )
    out_specs = (
        P(("dp", "fsdp"), "ctx", None),
        P(("dp", "fsdp"), "ctx", None),
        P(("ctx", "fsdp"), None),
        P(("ctx", "fsdp"), None),
        P(("ctx", "fsdp"), None),
        P(("ctx", "fsdp"), None),
        P(("ctx", "fsdp")),
        P(("ctx", "fsdp"), None),
        P(("ctx", "fsdp"), None),
        P(("ctx", "fsdp"), None),
        P(("ctx", "fsdp"), None),
        P(("ctx", "fsdp")),
        P(("ctx", "fsdp"), None),
        P(("ctx", "fsdp"), None),
        P(("ctx", "fsdp"), None),
        P(("ctx", "fsdp"), None),
        P(("ctx", "fsdp")),
        P(("ctx", "fsdp"), None),
        P(("ctx", "fsdp"), None),
        P(("ctx", "fsdp"), None),
        P(("ctx", "fsdp"), None),
        P(("ctx", "fsdp")),
    )
    body = move_tokens_body if moves_tokens(mesh) else gather_weights_body
    return jax.shard_map(body, mesh=mesh, in_specs=in_specs, out_specs=out_specs, check_vma=False)
```

```python
import functools

import jax
import jax.numpy as jnp
from jax import lax
from jax.experimental import pallas as pl
from jax.experimental.pallas import tpu as pltpu
from jax.sharding import PartitionSpec as P

MESH = pl.DeviceIdType.MESH
ANY = pl.BlockSpec(memory_space=pl.ANY)
VMEM = pl.BlockSpec(memory_space=pltpu.VMEM)
BF = jnp.bfloat16
F32 = jnp.float32

H = 4
HD = 256
STEP = 5


def normalize(value, gain):
    scale = lax.rsqrt(jnp.mean(value * value, axis=-1, keepdims=True) + 1e-06)
    return value * scale * (1.0 + gain)


def rotate(value, angles):
    half = value.shape[-1] // 2
    first = value[..., :half]
    second = value[..., half:]
    cosine = jnp.cos(angles)
    sine = jnp.sin(angles)
    return jnp.concatenate(
        [first * cosine - second * sine, second * cosine + first * sine], axis=-1
    )


def rope_angles(segments, first, rows):
    own = lax.dynamic_slice_in_dim(segments, first, rows, 0)
    starts = jnp.sum((segments[None, :] < own[:, None]).astype(jnp.int32), axis=1)
    offset = (first + jnp.arange(rows, dtype=jnp.int32) - starts).astype(jnp.float32)
    inverse = jnp.exp(-jnp.log(1000000.0) * (2.0 * jnp.arange(HD // 2, dtype=jnp.float32)) / HD)
    return offset[:, None] * inverse[None, :]


def contract_last(left, right):
    return lax.dot_general(
        left, right, (((1,), (1,)), ((), ())), preferred_element_type=jnp.float32
    )


def contract_first(left, right):
    return lax.dot_general(
        left, right, (((0,), (0,)), ((), ())), preferred_element_type=jnp.float32
    )


def activate(gate_up):
    half = gate_up.shape[-1] // 2
    return jax.nn.gelu(gate_up[:, :half], approximate=True) * gate_up[:, half:]


def adamw(weight, grad, first, second):
    first_new = 0.9 * first + 0.1 * grad
    second_new = 0.95 * second + 0.05 * grad * grad
    first_hat = first_new / (1.0 - 0.9**STEP)
    second_hat = second_new / (1.0 - 0.95**STEP)
    weight_new = weight - 0.03 * (first_hat / (jnp.sqrt(second_hat) + 1e-08) + 0.1 * weight)
    return (weight_new, first_new, second_new)


def gather_weights_body(
    tokens,
    cotangent,
    segments,
    qkv_weight,
    out_weight,
    gate_up_weight,
    down_weight,
    gains,
    qkv_first,
    out_first,
    gate_up_first,
    down_first,
    gains_first,
    qkv_second,
    out_second,
    gate_up_second,
    down_second,
    gains_second,
):
    rows = tokens.shape[1]
    width = tokens.shape[2]
    length = segments.shape[1]
    query_width = H * HD
    scale = HD ** (-0.5)
    reach = lax.axis_size("ctx") // 2 + 1
    front = reach * rows
    window = front + rows
    qkv_full, out_full, gains_full = (
        lax.all_gather(qkv_weight.astype(jnp.bfloat16), ("ctx", "fsdp"), axis=0, tiled=True),
        lax.all_gather(out_weight.astype(jnp.bfloat16), ("ctx", "fsdp"), axis=0, tiled=True),
        lax.all_gather(gains.astype(jnp.bfloat16), ("ctx", "fsdp"), axis=0, tiled=True),
    )
    gain_all = gains_full.astype(jnp.float32)
    gain_input = gain_all[:width]
    gain_attend = gain_all[width : 2 * width]
    gain_pre = gain_all[2 * width : 3 * width]
    gain_post = gain_all[3 * width : 4 * width]
    gain_query = gain_all[4 * width : 4 * width + HD]
    gain_key = gain_all[4 * width + HD :]
    first_row = lax.axis_index("ctx") * rows
    sequence_ids = segments[0]
    angles = rope_angles(sequence_ids, first_row, rows)
    query_ids = lax.dynamic_slice_in_dim(sequence_ids, first_row, rows, 0)
    query_pos = first_row + jnp.arange(rows, dtype=jnp.int32)
    window_pos = first_row - front + jnp.arange(window, dtype=jnp.int32)
    padded_ids = jnp.concatenate([jnp.full((front,), -1, dtype=jnp.int32), sequence_ids])
    window_ids = lax.dynamic_slice_in_dim(padded_ids, first_row, window, 0)
    allowed = (window_pos[None, :] <= query_pos[:, None]) & (
        window_ids[None, :] == query_ids[:, None]
    )
    allowed = allowed[:, None, :]
    x_rows = tokens[0].astype(jnp.float32)
    normed, input_back = jax.vjp(normalize, x_rows, gain_input)
    normed_low = normed.astype(jnp.bfloat16)
    projected = contract_last(normed_low, qkv_full)
    proj_query = projected[:, :query_width].reshape(rows, H, HD)
    proj_key = projected[:, query_width : query_width + HD]
    proj_value = projected[:, query_width + HD :]

    def query_key(part_query, part_key, query_gain, key_gain):
        return (
            rotate(normalize(part_query, query_gain), angles[:, None, :]),
            rotate(normalize(part_key, key_gain), angles),
        )

    (rotated_query, rotated_key), rotate_back = jax.vjp(
        query_key, proj_query, proj_key, gain_query, gain_key
    )
    query = rotated_query.astype(jnp.bfloat16)
    key_low = rotated_key.astype(jnp.bfloat16)
    value_low = proj_value.astype(jnp.bfloat16)
    keys_all, values_all = (
        lax.all_gather(key_low, "ctx", axis=0, tiled=True),
        lax.all_gather(value_low, "ctx", axis=0, tiled=True),
    )
    blank = jnp.zeros((front, HD), jnp.bfloat16)
    keys = lax.dynamic_slice_in_dim(jnp.concatenate([blank, keys_all]), first_row, window, 0)
    values = lax.dynamic_slice_in_dim(jnp.concatenate([blank, values_all]), first_row, window, 0)
    scores = jnp.einsum("thd,ld->thl", query, keys, preferred_element_type=jnp.float32) * scale
    masked = jnp.where(allowed, scores, -1e30)
    largest = jnp.max(masked, axis=-1, keepdims=True)
    log_total = largest + jnp.log(jnp.sum(jnp.exp(masked - largest), axis=-1, keepdims=True))
    probs_low = jnp.exp(masked - log_total).astype(jnp.bfloat16)
    attended = jnp.einsum("thl,ld->thd", probs_low, values, preferred_element_type=jnp.float32)
    attended = attended.reshape(rows, query_width).astype(jnp.bfloat16)
    branch = jnp.dot(attended, out_full, preferred_element_type=jnp.float32)
    branch_normed, attend_back = jax.vjp(normalize, branch, gain_attend)
    hidden = x_rows + branch_normed
    gate_up_full, down_full = (
        lax.all_gather(gate_up_weight.astype(jnp.bfloat16), ("ctx", "fsdp"), axis=0, tiled=True),
        lax.all_gather(down_weight.astype(jnp.bfloat16), ("ctx", "fsdp"), axis=0, tiled=True),
    )
    hidden_normed, pre_back = jax.vjp(normalize, hidden, gain_pre)
    hidden_low = hidden_normed.astype(jnp.bfloat16)
    gate_up = contract_last(hidden_low, gate_up_full)
    mixed, mix_back = jax.vjp(activate, gate_up)
    mixed_low = mixed.astype(jnp.bfloat16)
    down = jnp.dot(mixed_low, down_full, preferred_element_type=jnp.float32)
    down_normed, post_back = jax.vjp(normalize, down, gain_post)
    output = (hidden + down_normed).astype(jnp.bfloat16)
    gate_up_back, down_back = (
        lax.all_gather(gate_up_weight.astype(jnp.bfloat16), ("ctx", "fsdp"), axis=0, tiled=True),
        lax.all_gather(down_weight.astype(jnp.bfloat16), ("ctx", "fsdp"), axis=0, tiled=True),
    )
    grad_rows = cotangent[0].astype(jnp.float32)
    grad_down, grad_gain_post = post_back(grad_rows)
    grad_down_low = grad_down.astype(jnp.bfloat16)
    down_grad = contract_first(mixed_low, grad_down_low)
    grad_mixed = contract_last(grad_down_low, down_back)
    (grad_gate_up,) = mix_back(grad_mixed)
    grad_gate_up_low = grad_gate_up.astype(jnp.bfloat16)
    gate_up_grad = contract_first(grad_gate_up_low, hidden_low)
    grad_hidden_low = jnp.dot(grad_gate_up_low, gate_up_back, preferred_element_type=jnp.float32)
    grad_from_pre, grad_gain_pre = pre_back(grad_hidden_low)
    grad_hidden = grad_rows + grad_from_pre
    gate_up_part, down_part = (
        lax.psum_scatter(gate_up_grad, ("ctx", "fsdp"), scatter_dimension=0, tiled=True),
        lax.psum_scatter(down_grad, ("ctx", "fsdp"), scatter_dimension=0, tiled=True),
    )
    qkv_back, out_back = (
        lax.all_gather(qkv_weight.astype(jnp.bfloat16), ("ctx", "fsdp"), axis=0, tiled=True),
        lax.all_gather(out_weight.astype(jnp.bfloat16), ("ctx", "fsdp"), axis=0, tiled=True),
    )
    grad_branch, grad_gain_attend = attend_back(grad_hidden)
    grad_branch_low = grad_branch.astype(jnp.bfloat16)
    out_grad = contract_first(attended, grad_branch_low)
    grad_attended = (
        contract_last(grad_branch_low, out_back).astype(jnp.bfloat16).reshape(rows, H, HD)
    )
    scores_again = (
        jnp.einsum("thd,ld->thl", query, keys, preferred_element_type=jnp.float32) * scale
    )
    probs = jnp.exp(jnp.where(allowed, scores_again, -1e30) - log_total)
    grad_probs = jnp.einsum(
        "thd,ld->thl", grad_attended, values, preferred_element_type=jnp.float32
    )
    row_term = jnp.sum(probs * grad_probs, axis=-1, keepdims=True)
    grad_scores = (probs * (grad_probs - row_term)).astype(jnp.bfloat16)
    grad_query = (
        jnp.einsum("thl,ld->thd", grad_scores, keys, preferred_element_type=jnp.float32) * scale
    )
    grad_keys = (
        jnp.einsum("thl,thd->ld", grad_scores, query, preferred_element_type=jnp.float32) * scale
    )
    grad_values = jnp.einsum(
        "thl,thd->ld", probs.astype(jnp.bfloat16), grad_attended, preferred_element_type=jnp.float32
    )
    empty = jnp.zeros((front + length, HD), jnp.float32)
    keys_spread = lax.dynamic_update_slice_in_dim(empty, grad_keys, first_row, 0)[front:]
    values_spread = lax.dynamic_update_slice_in_dim(empty, grad_values, first_row, 0)[front:]
    grad_key, grad_value = (
        lax.psum_scatter(keys_spread, "ctx", scatter_dimension=0, tiled=True),
        lax.psum_scatter(values_spread, "ctx", scatter_dimension=0, tiled=True),
    )
    grad_proj_query, grad_proj_key, grad_gain_query, grad_gain_key = rotate_back(
        (grad_query, grad_key)
    )
    grad_projected = jnp.concatenate(
        [grad_proj_query.reshape(rows, query_width), grad_proj_key, grad_value], axis=1
    ).astype(jnp.bfloat16)
    qkv_grad = contract_first(grad_projected, normed_low)
    grad_normed = jnp.dot(grad_projected, qkv_back, preferred_element_type=jnp.float32)
    grad_from_input, grad_gain_input = input_back(grad_normed)
    input_grad = grad_hidden + grad_from_input
    gains_grad = jnp.concatenate(
        [
            grad_gain_input,
            grad_gain_attend,
            grad_gain_pre,
            grad_gain_post,
            grad_gain_query,
            grad_gain_key,
        ]
    )
    qkv_part, out_part, gains_part = (
        lax.psum_scatter(qkv_grad, ("ctx", "fsdp"), scatter_dimension=0, tiled=True),
        lax.psum_scatter(out_grad, ("ctx", "fsdp"), scatter_dimension=0, tiled=True),
        lax.psum_scatter(gains_grad, ("ctx", "fsdp"), scatter_dimension=0, tiled=True),
    )
    qkv_total, out_total, gate_up_total, down_total, gains_total = (
        lax.psum(qkv_part.astype(jnp.bfloat16), "dp").astype(jnp.float32),
        lax.psum(out_part.astype(jnp.bfloat16), "dp").astype(jnp.float32),
        lax.psum(gate_up_part.astype(jnp.bfloat16), "dp").astype(jnp.float32),
        lax.psum(down_part.astype(jnp.bfloat16), "dp").astype(jnp.float32),
        lax.psum(gains_part.astype(jnp.bfloat16), "dp").astype(jnp.float32),
    )
    qkv_new, qkv_first_new, qkv_second_new = adamw(qkv_weight, qkv_total, qkv_first, qkv_second)
    out_new, out_first_new, out_second_new = adamw(out_weight, out_total, out_first, out_second)
    gate_up_new, gate_up_first_new, gate_up_second_new = adamw(
        gate_up_weight, gate_up_total, gate_up_first, gate_up_second
    )
    down_new, down_first_new, down_second_new = adamw(
        down_weight, down_total, down_first, down_second
    )
    gains_new, gains_first_new, gains_second_new = adamw(
        gains, gains_total, gains_first, gains_second
    )
    return (
        output[None],
        input_grad[None],
        qkv_total,
        out_total,
        gate_up_total,
        down_total,
        gains_total,
        qkv_new,
        out_new,
        gate_up_new,
        down_new,
        gains_new,
        qkv_first_new,
        out_first_new,
        gate_up_first_new,
        down_first_new,
        gains_first_new,
        qkv_second_new,
        out_second_new,
        gate_up_second_new,
        down_second_new,
        gains_second_new,
    )


def place():
    return lax.axis_index("dp"), lax.axis_index("ctx"), lax.axis_index("fsdp")


class Links:
    def __init__(self, send, recv):
        self.send, self.recv, self.used, self.sent, self.some = send, recv, 0, [], []

    def slot(self):
        self.used += 1
        return self.send.at[self.used - 1], self.recv.at[self.used - 1]

    def make(self, source, target, device):
        send, recv = self.slot()
        return pltpu.make_async_remote_copy(
            src_ref=source,
            dst_ref=target,
            send_sem=send,
            recv_sem=recv,
            device_id=device,
            device_id_type=MESH,
        )

    def go(self, source, target, device):
        copy = self.make(source, target, device)
        copy.start()
        self.sent.append(copy)
        return copy

    def go_if(self, condition, source, target, device):
        copy = self.make(source, target, device)
        pl.when(condition)(copy.start)
        self.some.append((condition, copy))
        return copy

    def drain(self):
        for copy in self.sent:
            copy.wait_send()
        for condition, copy in self.some:
            pl.when(condition)(copy.wait_send)
        self.sent, self.some = [], []


class Feed:
    def __init__(self, links):
        self.links, self.copies, self.begun = links, [], 0

    def add(self, source, target, device, condition=None):
        self.copies.append((condition, self.links.make(source, target, device)))

    def do(self, condition, action):
        if condition is None:
            action()
        else:
            pl.when(condition)(action)

    def __call__(self, count=1):
        for condition, copy in self.copies[self.begun : self.begun + count]:
            self.do(condition, copy.start)
        self.begun = min(self.begun + count, len(self.copies))

    def arrive(self, first, last):
        for condition, copy in self.copies[first:last]:
            self.do(condition, copy.wait_recv)

    def drain(self):
        assert self.begun == len(self.copies)
        for condition, copy in self.copies:
            self.do(condition, copy.wait_send)


TILE = 16
CHUNK = 3
AXES = (1, 2, 4)
ORDERS = ((0, 1, 2), (1, 2, 0), (2, 0, 1))


class Cube:
    def __init__(self, links, tiles):
        dp, ctx, x = place()
        self.links, self.tiles = links, tiles
        self.me = (ctx % 4) * 2 + x
        self.peers = (
            (dp, ctx, 1 - x),
            (dp, ctx + 1 - 2 * (ctx % 2), x),
            (dp, ctx + 2 - 4 * (ctx // 2 % 2), x),
        )
        third = -(-tiles // 3)
        self.parts = ((0, third), (third, third), (2 * third, tiles - 2 * third))

    def block(self, mask):
        result = 0
        for bit in AXES:
            own = self.me // bit % 2
            result = result + bit * (1 - own if mask & bit else own)
        return result

    def cut(self, buf, p, mask):
        start, size = self.parts[p]
        return buf.at[pl.ds(self.block(mask) * self.tiles + start, size)]

    def gather(self, buf, feed=lambda: None):
        sent = {}

        def go(p, index, mask, dim):
            ref = self.cut(buf, p, mask)
            sent[p, index] = self.links.go(ref, ref, self.peers[dim])

        for index, where in ((0, 0), (1, 1), (3, 2)):
            for p, order in enumerate(ORDERS):
                go(p, index, 0, order[where])
        feed()
        for p, (a, b, c) in enumerate(ORDERS):
            sent[p, 0].wait_recv()
            go(p, 2, AXES[a], b)
            go(p, 4, AXES[a], c)
        feed()
        for p, (a, b, c) in enumerate(ORDERS):
            sent[p, 1].wait_recv()
            go(p, 5, AXES[b], c)
            sent[p, 2].wait_recv()
            go(p, 6, AXES[a] | AXES[b], c)
        feed()
        for index in (3, 4, 5, 6):
            for p in range(3):
                sent[p, index].wait_recv()

    def pair(self, step):
        high = (self.me // 4 + (3 - step) // 2) % 2
        return 2 * high + (self.me // 2 + 3 - step) % 2

    def first_copies(self, buf, one):
        copies = {}
        for index in range(4):
            for p, (a, b, c) in enumerate(ORDERS):
                mask = (AXES[b], AXES[b] | AXES[a], AXES[a], 0)[index] | AXES[c]
                start, size = self.parts[p]
                target = one.at[index, pl.ds(start, size)]
                copies[p, index] = (
                    3 - mask // 2,
                    self.links.make(self.cut(buf, p, mask), target, self.peers[c]),
                )
        return copies

    def release(self, copies, step):
        for turn in range(4):

            @pl.when(step == turn)
            def _():
                for when, copy in copies.values():
                    if when == turn:
                        copy.start()

    def scatter(self, buf, copies, one, two, three, beside=None, feed=lambda: None):
        sent = {key: copy for key, (_, copy) in copies.items()}
        self.links.sent += list(sent.values())

        def go(p, index, mask, slot, dim):
            start, size = self.parts[p]
            target = slot.at[pl.ds(start, size)]
            sent[p, index] = self.links.go(self.cut(buf, p, mask), target, self.peers[dim])

        def add(p, mask, slot):
            start, size = self.parts[p]
            mine = self.cut(buf, p, mask)
            mine[...] = (mine[...].astype(F32) + slot[pl.ds(start, size)].astype(F32)).astype(BF)

        if beside is not None:
            beside()
        for index in range(2):
            for p, (a, b, c) in enumerate(ORDERS):
                mask = AXES[b] | (AXES[a], 0)[index]
                sent[p, 1 - index].wait_recv()
                add(p, mask, one.at[1 - index])
                go(p, 4 + index, mask, two.at[index], b)
            feed()
        for p, (a, b, c) in enumerate(ORDERS):
            sent[p, 2].wait_recv()
            add(p, AXES[a], one.at[2])
            sent[p, 4].wait_recv()
            add(p, AXES[a], two.at[0])
            go(p, 6, AXES[a], three, a)
        feed()
        for p in range(3):
            sent[p, 3].wait_recv()
            add(p, 0, one.at[3])
            sent[p, 5].wait_recv()
            add(p, 0, two.at[1])
            sent[p, 6].wait_recv()


def flat(value):
    return value.reshape(-1, value.shape[-1])


def tiled(value):
    return value.reshape(-1, TILE, value.shape[-1])


def norm_scale(value):
    return lax.rsqrt(jnp.mean(value * value, axis=-1, keepdims=True) + 1e-06)


def norm_back(value, scale, gained):
    inner = jnp.mean(gained * value, axis=-1, keepdims=True)
    return scale * gained - value * (scale * scale * scale * inner)


ROOT = 0.7978845608028654


def gelu_parts(v):
    t = jnp.tanh(ROOT * (v + 0.044715 * (v * v * v)))
    value = 0.5 * v * (1.0 + t)
    slope = 0.5 * (1.0 + t) + 0.5 * v * (1.0 - t * t) * (ROOT * (1.0 + 0.134145 * (v * v)))
    return value, slope


def add_low(left, right):
    return (left.astype(F32) + right.astype(F32)).astype(BF)


def layer_kernel(
    tok,
    cot,
    seg,
    gpad,
    wq,
    wo,
    wgu_in,
    wd_in,
    output,
    input_grad,
    rq,
    ro,
    rg,
    rgu,
    rd,
    qkv_w,
    out_w,
    gains,
    wgu,
    wd,
    stage,
    acts,
    downs,
    ff,
    mixed,
    sums,
    one,
    two,
    three,
    pairs,
    query,
    proj,
    probs,
    attended,
    xn,
    turn,
    dscores,
    dpairs,
    kv_in,
    kv_sum,
    kv_far,
    pool,
    q_two,
    o_two,
    q_far,
    o_far,
    g_in,
    g_sum,
    gu_in,
    gu_far,
    d_in,
    d_far,
    send,
    recv,
    local,
):
    dp, ctx, x = place()
    rows, width = tok.shape
    layers = pairs.shape[0]
    length = seg.shape[0] * seg.shape[1]
    tiles = rows // TILE
    hq, ho = qkv_w.shape[4], out_w.shape[4]
    tq, to = hq // TILE, ho // TILE
    half = wd_in.shape[0]
    units = 2 * half
    thalf = half // TILE
    wide = wd.shape[0] * TILE
    query_width = H * HD
    scale = HD ** (-0.5)
    z, y = ctx // 2, ctx % 2
    cube_of = ctx // 4
    links = Links(send, recv)
    cube = Cube(links, tiles)
    sibling = (1 - dp, ctx, x)
    beside = (dp, z * 2 + 1 - y, x)
    across = (dp, lax.rem(ctx + 4, 8), x)
    others = [(dp, lax.rem(z + step, layers) * 2 + y, x) for step in range(1, layers)]
    y2, x2 = jnp.where(dp == 0, 1 - y, y), jnp.where(dp == 0, x, 1 - x)
    y3, x3 = jnp.where(dp == 0, y, 1 - y), jnp.where(dp == 0, 1 - x, x)
    mine2, mine3 = jnp.where(dp == 0, y, x), jnp.where(dp == 0, x, y)
    second = (dp, z * 2 + y2, x2)
    third = (dp, z * 2 + y3, x3)
    group = (ctx % 4) * 2 + x
    user = (x, ctx // 2 + 4 * dp, ctx % 2)
    owner = (cube_of, group, dp)
    stays_in = (dp == x) & (ctx == ctx // 2 + 4 * dp) & (x == ctx % 2)
    stays_back = (dp == cube_of) & (ctx == group)  & (x == dp)

    def bring(source, first, index):
        copy = pltpu.make_async_copy(
            source, stage.at[pl.ds(first, source.shape[0])], local.at[index]
        )
        copy.start()
        return copy

    bring_q = bring(wq, 0, 0)
    bring_o = bring(wo, 2 * hq, 1)
    bring_gu = bring(wgu_in.at[pl.ds(dp * half, half)], 2 * hq + 2 * ho, 2)

    pairs[...] = jnp.zeros(pairs.shape, BF)
    barrier = pltpu.get_barrier_semaphore()
    for device in others + [second, third, sibling, cube.peers[2]]:
        pl.semaphore_signal(barrier, inc=1, device_id=device, device_id_type=MESH)

    @pl.when(jnp.logical_not(stays_in))
    def _():
        for device in (user, owner):
            pl.semaphore_signal(barrier, inc=1, device_id=device, device_id_type=MESH)

    gains[z, y, x, dp] = gpad[dp]
    bring_q.wait()
    qkv_w[z, y, x, dp] = stage[pl.ds(dp * hq, hq), :].astype(BF)
    pl.semaphore_wait(barrier, jnp.where(stays_in, layers + 3, layers + 5))
    fulls = (gains, qkv_w, out_w)

    def first_steps(full):
        part = full.at[z, y, x, dp]
        return [links.go(part, part, device) for device in others]

    def pass_on(zz, yy, xx, *devices):
        part = qkv_w.at[zz, yy, xx, dp]
        return [links.go(part, part, device) for device in devices]

    firsts = [first_steps(gains), first_steps(qkv_w)]
    passed = [pass_on(z, y, x, second, third, sibling)]
    bring_o.wait()
    out_w[z, y, x, dp] = stage[pl.ds(2 * hq + dp * ho, ho), :].astype(BF)
    bring_gu.wait()
    low = 2 * hq + 2 * ho
    wgu[cube_of, pl.ds(dp * half, half), :] = stage[low : low + half, :].astype(BF)
    bring_d = bring(wd_in, 0, 3)

    row_id = lax.broadcasted_iota(jnp.int32, (rows, rows), 0)
    lane_id = lax.broadcasted_iota(jnp.int32, (rows, rows), 1)
    own_ids = seg[pl.ds(ctx, 1), :]
    ids = jnp.sum(jnp.where(row_id == lane_id, own_ids, 0), axis=1, keepdims=True)
    start = jnp.zeros((rows, 1), jnp.int32)
    for b in range(length // rows):
        start = start + jnp.sum((seg[b : b + 1, :] < ids).astype(jnp.int32), axis=1, keepdims=True)
    position = ctx * rows + lax.broadcasted_iota(jnp.int32, (rows, 1), 0)
    offset = (position - start).astype(F32)
    lane = lax.broadcasted_iota(jnp.int32, (1, HD // 2), 1).astype(F32)
    angle = offset * jnp.exp(lane * (-2.0 * 13.815510557964274 / HD))
    turn[0] = jnp.cos(angle)
    turn[1] = jnp.sin(angle)

    bring_d.wait()
    d_in[...] = tiled(stage[0:half, :].astype(BF))
    bring_rest = bring(wgu_in.at[pl.ds((1 - dp) * half, half)], 0, 4)
    bring_rest.wait()
    wgu[cube_of, pl.ds((1 - dp) * half, half), :] = stage[0:half, :].astype(BF)
    wgu[:, units:, :] = jnp.zeros((2, wide - units, width), BF)
    wd[2 * thalf :] = jnp.zeros((wide // TILE - 2 * thalf, TILE, width), BF)

    sib, seconds, thirds = {0: [], 2: []}, {}, {}

    def second_steps(t):
        for copy in firsts[t]:
            copy.wait_recv()
        line = fulls[t].at[:, y, x, dp]
        seconds[t] = links.go(line, line, second)
        thirds[t] = [links.go(line, line, third)]
        sib[t].append(links.go(line, line, sibling))

    def third_steps(t):
        seconds[t].wait_recv()
        line = fulls[t].at[:, y2, x2, dp]
        thirds[t].append(links.go(line, line, third))
        sib[t].append(links.go(line, line, sibling))

    def last_steps(t):
        for copy, (yy, xx) in zip(thirds[t], ((y3, x3), (1 - y, 1 - x))):
            copy.wait_recv()
            line = fulls[t].at[:, yy, xx, dp]
            sib[t].append(links.go(line, line, sibling))

    cuts = [(i, min(CHUNK, thalf - i)) for i in range(0, thalf, CHUNK)]
    down_local = pltpu.make_async_copy(d_in, wd.at[pl.ds(x * thalf, thalf)], local.at[5])
    pl.when(stays_in)(down_local.start)
    leaves_in = jnp.logical_not(stays_in)
    down_feed, gu_feed = Feed(links), Feed(links)
    for first, size in cuts:
        target = wd.at[pl.ds(x * thalf + first, size)]
        down_feed.add(d_in.at[pl.ds(first, size)], target, user, leaves_in)
        part = wgu.at[cube_of, pl.ds(dp * half + first * TILE, size * TILE)]
        gu_feed.add(part, part, across)
    down_feed(0)
    gu_feed(0)
    second_steps(0)
    behind = [lax.rem(z + layers - 1 - i, layers) for i in range(layers - 1)]
    for i, copy in enumerate(firsts[1]):
        copy.wait_recv()
        passed.append(pass_on(behind[i], y, x, second, third, sibling))
        down_feed(3)
        gu_feed(0)
    firsts.append(first_steps(out_w))
    third_steps(0)
    line_order = [z] + behind
    far = []
    for i, zz in enumerate(line_order):
        passed[i][0].wait_recv()
        far.append(pass_on(zz, y2, x2, third, sibling))
        down_feed(0)
        gu_feed(0)
    last_steps(0)
    ends_q = []
    for i, zz in enumerate(line_order):
        passed[i][1].wait_recv()
        ends_q += pass_on(zz, y3, x3, sibling)
        far[i][0].wait_recv()
        ends_q += pass_on(zz, 1 - y, 1 - x, sibling)
        down_feed(0)
        gu_feed(0)
    second_steps(2)
    ends_q += [copies[2] for copies in passed] + [copies[1] for copies in far]
    for copy in ends_q + sib[0]:
        copy.wait_recv()

    total = jnp.zeros(gains.shape[-2:], F32)
    for h in range(2):
        part = jnp.zeros(gains.shape[-2:], F32)
        for zz in range(layers):
            for yy in range(2):
                for xx in range(2):
                    part = part + gains[zz, yy, xx, h]
        g_in[0, h * part.shape[0] : (h + 1) * part.shape[0], :] = part

    def gain_row(first, size):
        lo = first // 128
        return 1.0 + jnp.concatenate(
            [g_in[0, lo + i : lo + i + 1, :] for i in range(size // 128)], axis=1
        )

    gain_in = gain_row(0, width)
    gain_query = gain_row(4 * width, HD)
    gain_key = gain_row(4 * width + HD, HD)

    value = tok[...].astype(F32)
    xn[...] = (value * norm_scale(value) * gain_in).astype(BF)
    proj[...] = contract_last(xn[...], flat(qkv_w[...]))

    def turned(part, gain):
        part = part * norm_scale(part) * gain
        first, last = part[:, : HD // 2], part[:, HD // 2 :]
        cosine, sine = turn[0], turn[1]
        return jnp.concatenate(
            [first * cosine - last * sine, last * cosine + first * sine], axis=1
        )

    pairs[z, y, :, :HD] = turned(proj[:, query_width : query_width + HD], gain_key).astype(BF)
    pairs[z, y, :, HD:] = proj[:, query_width + HD :].astype(BF)
    own_pairs = pairs.at[z, y]
    upper = (dp, lax.rem(z + 1, layers) * 2 + y, x)
    rises = z < layers - 1
    pair_up = [links.go_if(rises, own_pairs, own_pairs, upper)]
    pair_side = [links.go(own_pairs, own_pairs, beside)]
    for h in range(H):
        query[h * rows : (h + 1) * rows, :] = turned(
            proj[:, h * HD : (h + 1) * HD], gain_query
        ).astype(BF)
    third_steps(2)
    for k in range(1, layers):
        below = z >= k
        part = pairs.at[lax.rem(z + layers - k, layers), y]
        pl.when(below)(pair_up[k - 1].wait_recv)
        if k < layers - 1:
            pair_up.append(links.go_if(below & rises, part, part, upper))
        pair_side.append(links.go_if(below, part, part, beside))
    last_steps(2)
    pair_side[0].wait_recv()
    for k in range(1, layers):
        pl.when(z >= k)(pair_side[k].wait_recv)

    down_feed(0)
    gu_feed(3)
    def allowed(b):
        key_pos = b * rows + lax.broadcasted_iota(jnp.int32, (1, rows), 1)
        return (key_pos <= position) & (seg[b : b + 1, :] == ids)

    keep = jnp.concatenate([allowed(b) for b in range(length // rows)], axis=1)
    keys = flat(pairs[:, :, :, :HD])
    values = flat(pairs[:, :, :, HD:])
    for h in range(H):
        part = slice(h * rows, (h + 1) * rows)
        scores = jnp.where(keep, contract_last(query[part, :], keys) * scale, -1e30)
        largest = jnp.max(scores, axis=-1, keepdims=True)
        raised = jnp.exp(scores - largest)
        p = raised / jnp.sum(raised, axis=-1, keepdims=True)
        probs[part, :] = p
        attended[:, h * HD : (h + 1) * HD] = jnp.dot(
            p.astype(BF), values, preferred_element_type=F32
        ).astype(BF)
    for copy in sib[2]:
        copy.wait_recv()
    branch = stage.at[0:rows]
    hidden = stage.at[rows : 2 * rows]
    grad_hidden = stage.at[2 * rows : 3 * rows]
    branch[...] = jnp.dot(attended[...], flat(out_w[...]), preferred_element_type=F32)
    gain_attend = gain_row(width, width)
    value = branch[...]
    hidden[...] = tok[...].astype(F32) + value * norm_scale(value) * gain_attend
    value = hidden[...]
    gain_pre = gain_row(2 * width, width)
    gain_post = gain_row(3 * width, width)

    def block_of(buf, j):
        return flat(buf[pl.ds(j * tiles, tiles)])

    def put_block(buf, j, block):
        buf[pl.ds(j * tiles, tiles)] = tiled(block)

    me = cube.me
    put_block(acts, me, (value * norm_scale(value) * gain_pre).astype(BF))
    gu_feed(0)
    cube.gather(acts, lambda: gu_feed(2))
    gu_feed(len(cuts))
    down_feed(len(cuts))
    pair = 2

    def pair_of(buf, j):
        return flat(buf[pl.ds(j * pair * tiles, pair * tiles)])

    def put_pair(buf, j, block):
        buf[pl.ds(j * pair * tiles, pair * tiles)] = tiled(block)

    def spread(block):
        return block.reshape(pair, rows, block.shape[-1])

    def near(j, carry):
        ff[cube_of, pl.ds(j * pair, pair)] = spread(
            contract_last(pair_of(acts, j), wgu[cube_of])
        )
        return carry

    lax.fori_loop(0, 8 // pair, near, 0)
    def hand_on(feed, ref, base, unit):
        handed = []
        for i in range(0, len(cuts), 3):
            chunk = cuts[i : i + 3]
            feed.arrive(i, i + 3)
            first, size = chunk[0][0], sum(size for _, size in chunk)
            part = ref.at[pl.ds(base + first * unit, size * unit)]
            handed.append(links.go(part, part, sibling))
        for copy in handed:
            copy.wait_recv()

    hand_on(gu_feed, wgu.at[1 - cube_of], dp * half, TILE)

    def forward(j, carry):
        here = pl.ds(j * pair, pair)
        ff[1 - cube_of, here] = spread(contract_last(pair_of(acts, j), wgu[1 - cube_of]))
        mixed[here] = (gelu_parts(ff[0, here])[0] * ff[1, here]).astype(BF)
        return carry

    lax.fori_loop(0, 8 // pair, forward, 0)

    pl.when(stays_in)(down_local.wait)
    down_feed.drain()
    gu_feed.drain()
    hand_on(down_feed, wd, dp * thalf, 1)
    links.drain()
    first_sums = cube.first_copies(sums, one)

    def project(i, carry):
        j = cube.pair(i)
        m = flat(mixed[pl.ds(j * pair, pair)])
        put_pair(sums, j, jnp.dot(m, flat(wd[...]), preferred_element_type=F32).astype(BF))
        cube.release(first_sums, i)
        return carry

    lax.fori_loop(0, 8 // pair, project, 0)
    cube.scatter(sums, first_sums, one, two, three)
    links.drain()
    down = block_of(sums, me).astype(F32) + flat(three[...]).astype(F32)
    down_scale = norm_scale(down)
    normal = down * down_scale
    output[...] = (hidden[...] + normal * gain_post).astype(BF)
    dy = cot[...].astype(F32)
    put_block(downs, me, norm_back(down, down_scale, dy * gain_post).astype(BF))

    def put_gain(first, row):
        lo = first // 128
        for i in range(row.shape[1] // 128):
            g_sum[0, lo + i : lo + i + 1, :] = row[:, i * 128 : (i + 1) * 128]

    g_sum[0] = jnp.zeros(g_sum.shape[1:], F32)
    put_gain(3 * width, jnp.sum(dy * normal, axis=0, keepdims=True))
    cube.gather(downs)

    tokens = 8 * rows
    whole_chunks = units // 128

    def weight_grad(part, tokens_in, base):
        def chunk(first, size, at):
            left = part(pl.ds(first, 128)).reshape(tokens, 128)
            block = contract_first(left, flat(tokens_in[...]))[:size].astype(BF)
            pool[pl.ds(at, size // TILE)] = tiled(block)

        def body(i, carry):
            chunk(pl.multiple_of(i * 128, 128), 128, base + i * (128 // TILE))
            return carry

        lax.fori_loop(0, whole_chunks, body, 0)
        if units % 128:
            chunk(whole_chunks * 128, units % 128, base + whole_chunks * (128 // TILE))

    weight_grad(lambda cut: mixed[:, :, cut], downs, 4 * thalf)

    def slab(first, size):
        return pool.at[pl.ds(first, size)]

    d_swap = links.go(slab(4 * thalf + (1 - dp) * thalf, thalf), d_in, sibling)

    def backward(i, carry):
        first = cube.pair(i) * pair
        for j in range(pair):
            here = first + j
            d = contract_last(flat(downs[pl.ds(here * tiles, tiles)]), flat(wd[...]))
            value, slope = gelu_parts(ff[0, here])
            dg = (d * ff[1, here] * slope).astype(BF)
            du = (d * value).astype(BF)
            ff[0, here] = dg.astype(F32)
            ff[1, here] = du.astype(F32)
            total = jnp.dot(dg, wgu[0], preferred_element_type=F32) + jnp.dot(
                du, wgu[1], preferred_element_type=F32
            )
            sums[pl.ds(here * tiles, tiles)] = tiled(total.astype(BF))
        cube.release(first_sums, i)
        return carry

    links.drain()
    first_sums = cube.first_copies(sums, one)
    lax.fori_loop(0, 8 // pair, backward, 0)
    moved = {}
    leaves_back = jnp.logical_not(stays_back)
    down_stay = pltpu.make_async_copy(d_in, d_far.at[cube_of], local.at[6])
    down_back, gu_back = Feed(links), Feed(links)
    for first, size in cuts:
        cut = pl.ds(first, size)
        down_back.add(d_in.at[cut], d_far.at[cube_of, cut], owner, leaves_back)
        gu_back.add(gu_in.at[1 - cube_of, cut], gu_far.at[cut], across)

    def feed_back(downs_count, gu_count):
        down_back(downs_count)
        gu_back(gu_count)


    def weights():
        d_swap.wait_recv()
        d_in[...] = add_low(d_in[...], pool[pl.ds(4 * thalf + dp * thalf, thalf)])
        pl.when(stays_back)(down_stay.start)
        down_back(2)

        for turn in range(2):
            side = cube_of if turn else 1 - cube_of
            weight_grad(lambda cut: ff[side, :, :, cut].astype(BF), acts, side * 2 * thalf)
            swap = links.go(
                slab(side * 2 * thalf + (1 - dp) * thalf, thalf), gu_in.at[side], sibling
            )
            if turn:
                moved["swap"] = swap
                continue
            swap.wait_recv()
            gu_in[side] = add_low(gu_in[side], pool[pl.ds(side * 2 * thalf + dp * thalf, thalf)])
            feed_back(2, 1)

    cube.scatter(sums, first_sums, one, two, three, weights, lambda: feed_back(1, 1))
    value = hidden[...]
    hidden_scale = norm_scale(value)
    total = block_of(sums, me).astype(F32) + flat(three[...]).astype(F32)
    put_gain(2 * width, jnp.sum(total * (value * hidden_scale), axis=0, keepdims=True))
    grad = cot[...].astype(F32) + norm_back(value, hidden_scale, total * gain_pre)
    grad_hidden[...] = grad
    value = branch[...]
    branch_scale = norm_scale(value)
    put_gain(width, jnp.sum(grad * (value * branch_scale), axis=0, keepdims=True))
    grad_branch = norm_back(value, branch_scale, grad * gain_attend).astype(BF)
    moved["swap"].wait_recv()
    gu_in[cube_of] = add_low(
        gu_in[cube_of], pool[pl.ds(cube_of * 2 * thalf + dp * thalf, thalf)]
    )
    links.drain()

    class Reduce:
        def __init__(self, base, count, layers_in, came, one_in, two_in, far_in):
            self.base, self.count, self.layers_in = base, count, layers_in
            self.size = len(layers_in)
            self.per = 4 * self.size * count
            self.quarter = self.per // 4
            self.came, self.one_in, self.two_in, self.far_in = came, one_in, two_in, far_in
            self.whole = self.size == layers
            self.takes = (z >= layers_in[0]) & (z <= layers_in[-1])

        def put(self, make):
            size = self.count * TILE
            for zi in range(self.size):
                block = make(pl.ds(zi * 8 * size, 8 * size)).astype(BF)
                for yy in range(2):
                    for xx in range(2):
                        for h in range(2):
                            a, b = (yy, xx) if h == 0 else (xx, yy)
                            first = ((yy * 2 + xx) * 2 + h) * size
                            spot = (b * 2 + a) * self.size + zi
                            at = self.base + h * self.per + spot * self.count
                            pool[at : at + self.count] = tiled(block[first : first + size])
            self.swap = links.go(
                slab(self.base + (1 - dp) * self.per, self.per), self.came, sibling
            )

        def on_chip(self):
            self.swap.wait_recv()
            mine = pl.ds(self.base + dp * self.per, self.per)
            pool[mine] = add_low(pool[mine], self.came[...])
            away = self.base + dp * self.per + (1 - mine3) * 2 * self.quarter
            self.at = self.base + dp * self.per + mine3 * 2 * self.quarter
            self.steps = []
            for a in (1 - mine2, mine2):
                cut = pl.ds(a * self.quarter, self.quarter)
                part = slab(away + a * self.quarter, self.quarter)
                self.steps.append((a, links.go(part, self.one_in.at[cut], third)))

        def across_third(self):
            for i, (a, copy) in enumerate(self.steps):
                copy.wait_recv()
                near = pl.ds(self.at + a * self.quarter, self.quarter)
                cut = pl.ds(a * self.quarter, self.quarter)
                pool[near] = add_low(pool[near], self.one_in[cut])
                if i == 0:
                    self.step = links.go(pool.at[near], self.two_in, second)
            self.at = self.at + mine2 * self.quarter

        def across_second(self):
            self.step.wait_recv()
            near = pl.ds(self.at, self.quarter)
            pool[near] = add_low(pool[near], self.two_in[...])
            self.fars = []
            for i, device in enumerate(others):
                to_layer = lax.rem(z + i + 1, layers)
                if self.whole:
                    part = slab(self.at + to_layer * self.count, self.count)
                    self.fars.append(links.go(part, self.far_in.at[i], device))
                    continue
                inside = (to_layer >= self.layers_in[0]) & (to_layer <= self.layers_in[-1])
                index = jnp.where(inside, to_layer - self.layers_in[0], 0)
                part = slab(self.at + index * self.count, self.count)
                self.fars.append(links.go_if(inside, part, self.far_in.at[i], device))

        def along(self, result):
            def add():
                index = z if self.whole else z - self.layers_in[0]
                value = pool[pl.ds(self.at + index * self.count, self.count)].astype(F32)
                for i, copy in enumerate(self.fars):
                    copy.wait_recv()
                    value = value + self.far_in[i].astype(F32)
                result[dp] = value.astype(BF)

            if self.whole:
                add()
            else:
                pl.when(self.takes)(add)

    per_qkv = 2 * layers * tq
    q_buf = downs.at[pl.ds(0, 2 * per_qkv)]
    o_in = acts.at[pl.ds(0, 4 * layers * to)]
    q_one = acts.at[pl.ds(4 * layers * to, per_qkv)]
    o_one = downs.at[pl.ds(2 * per_qkv, 2 * layers * to)]
    few = layers // 2
    sets = [
        Reduce(
            i * 2 * per_qkv,
            tq,
            tuple(range(i * few, (i + 1) * few)),
            q_buf.at[pl.ds(i * per_qkv, per_qkv)],
            q_one.at[pl.ds(i * per_qkv // 2, per_qkv // 2)],
            q_two.at[pl.ds(i * per_qkv // 4, per_qkv // 4)],
            q_far,
        )
        for i in range(2)
    ]
    outs = Reduce(4 * per_qkv, to, tuple(range(layers)), o_in, o_one, o_two, o_far)
    outs.put(lambda cut: contract_first(attended[:, cut], grad_branch))
    keys = flat(pairs[:, :, :, :HD])
    values = flat(pairs[:, :, :, HD:])
    feed_back(1, 1)
    grad_att = contract_last(grad_branch, flat(out_w[...])).astype(BF)
    for h in range(H):
        part = slice(h * rows, (h + 1) * rows)
        p = probs[part, :]
        grad_p = contract_last(grad_att[:, h * HD : (h + 1) * HD], values)
        row = jnp.sum(p * grad_p, axis=-1, keepdims=True)
        dscores[part, :] = (p * (grad_p - row)).astype(BF)
    grad_heads = jnp.concatenate([grad_att[:, h * HD : (h + 1) * HD] for h in range(H)], axis=0)
    grad_keys = contract_first(dscores[...], query[...]) * scale
    dpairs[:, :, :, :HD] = grad_keys.astype(BF).reshape(layers, 2, rows, HD)
    grad_values = contract_first(probs[...].astype(BF), grad_heads)
    dpairs[:, :, :, HD:] = grad_values.astype(BF).reshape(layers, 2, rows, HD)
    kv_lines = [
        links.go_if(z >= zz, dpairs.at[zz, 1 - y], kv_in.at[zz], beside) for zz in range(layers)
    ]

    def turned_back(part, gain, grad):
        cosine, sine = turn[0], turn[1]
        first, last = grad[:, : HD // 2], grad[:, HD // 2 :]
        grad = jnp.concatenate(
            [first * cosine + last * sine, last * cosine - first * sine], axis=1
        )
        part_scale = norm_scale(part)
        gain_term = jnp.sum(grad * (part * part_scale), axis=0, keepdims=True)
        return norm_back(part, part_scale, grad * gain), gain_term

    outs.on_chip()
    feed_back(0, 1)
    query_term = jnp.zeros((1, HD), F32)
    grads = []
    for h in range(H):
        part = slice(h * rows, (h + 1) * rows)
        grad_query = jnp.dot(dscores[part, :], keys, preferred_element_type=F32) * scale
        grad, term = turned_back(proj[:, h * HD : (h + 1) * HD], gain_query, grad_query)
        grads.append(grad.astype(BF))
        query_term = query_term + term
    put_gain(4 * width, query_term)
    grad_queries = jnp.concatenate(grads, axis=1)
    half_cols = (H + 2) * HD // 2

    kv_copies = []
    for i, device in enumerate(others):
        to_layer = lax.rem(z + i + 1, layers)
        copy = links.make(kv_sum.at[to_layer], kv_far.at[i], device)
        links.some.append((to_layer < z, copy))
        kv_copies.append((to_layer, copy))
    for zz in range(layers):

        @pl.when(z >= zz)
        def _():
            kv_lines[zz].wait_recv()
            kv_sum[zz] = add_low(kv_in[zz], dpairs[zz, y])

        for to_layer, copy in kv_copies:
            pl.when((to_layer == zz) & (z > zz))(copy.start)
    feed_back(0, 0)

    def columns(value, first, cut):
        return value[:, first + cut.start : first + cut.start + cut.size]

    sets[0].put(lambda cut: contract_first(columns(grad_queries, 0, cut), xn[...]))
    outs.across_third()
    sets[0].on_chip()
    kv_total = stage.at[3 * rows : 4 * rows, 0 : 2 * HD]
    kv_total[...] = kv_sum[z].astype(F32)
    for i, (_, copy) in enumerate(kv_copies):

        @pl.when(behind[i] > z)
        def _():
            copy.wait_recv()
            kv_total[...] += kv_far[i].astype(F32)

    feed_back(0, 2)
    grad_pair = kv_total[...]
    grad, term = turned_back(
        proj[:, query_width : query_width + HD], gain_key, grad_pair[:, :HD]
    )
    put_gain(4 * width + HD, term)
    grad_proj = jnp.concatenate(
        [grad_queries, grad.astype(BF), grad_pair[:, HD:].astype(BF)], axis=1
    )
    sets[1].put(lambda cut: contract_first(columns(grad_proj, half_cols, cut), xn[...]))
    sets[0].across_third()
    sets[1].on_chip()
    feed_back(len(cuts), len(cuts))
    grad_normed = jnp.dot(grad_proj, flat(qkv_w[...]), preferred_element_type=F32)
    value = tok[...].astype(F32)
    in_scale = norm_scale(value)
    put_gain(0, jnp.sum(grad_normed * (value * in_scale), axis=0, keepdims=True))
    g_swap = links.go(g_sum.at[0], g_in.at[1], sibling)
    input_grad[...] = grad_hidden[...] + norm_back(value, in_scale, grad_normed * gain_in)
    outs.across_second()
    g_swap.wait_recv()
    g_sum[1] = g_sum[0] + g_in[1]
    g_x = links.go(g_sum.at[1], g_in.at[2], cube.peers[0])
    sets[0].across_second()
    sets[1].across_third()
    g_x.wait_recv()
    g_sum[2] = g_sum[1] + g_in[2]
    g_y = links.go(g_sum.at[2], g_in.at[3], beside)
    sets[1].across_second()
    g_y.wait_recv()
    g_sum[3] = g_sum[2] + g_in[3]
    g_in[4 + z] = g_sum[3]
    g_z = [links.go(g_sum.at[3], g_in.at[4 + z], device) for device in others]
    ends = []
    outs.along(ro)
    ends.append(links.go(ro.at[dp], ro.at[dp], sibling))
    sets[0].along(rq)
    sets[1].along(rq)
    ends.append(links.go(rq.at[dp], rq.at[dp], sibling))
    for copy in g_z:
        copy.wait_recv()
    value = g_in[4]
    for i in range(1, layers):
        value = value + g_in[4 + i]
    rg[...] = value

    pl.when(stays_back)(down_stay.wait)
    down_back.arrive(0, len(cuts))
    down_back.drain()
    landed = d_far.at[dp]
    d_end = links.go(landed, landed, sibling)
    d_end.wait_recv()
    d_in[...] = add_low(d_far[0], d_far[1])
    keep_d = pltpu.make_async_copy(d_in, rd, local.at[7])
    keep_d.start()
    gu_back.arrive(0, len(cuts))
    gu_back.drain()
    gu_far[...] = add_low(gu_in[cube_of], gu_far[...])
    keep_gu = pltpu.make_async_copy(gu_far, rgu.at[dp], local.at[8])
    keep_gu.start()
    ends.append(links.go(gu_far, rgu.at[dp], sibling))
    for copy in ends:
        copy.wait_recv()
    keep_d.wait()
    keep_gu.wait()
    links.drain()


def whole_layer(tok, cot, seg, gpad, wq, wo, wgu, wd, layers):
    rows, width = tok.shape
    units = 2 * wd.shape[0]
    wide = -(-units // 128) * 128
    hq, ho, half = wq.shape[0] // 2, wo.shape[0] // 2, wd.shape[0]
    tq, to, thalf, tiles = hq // TILE, ho // TILE, half // TILE, rows // TILE
    gain_rows = gpad.shape[0] * gpad.shape[1]
    length = seg.shape[0] * seg.shape[1]
    pool = max(6 * thalf, 8 * layers * (tq + to))

    def low(*shape):
        return pltpu.VMEM(shape, BF)

    def full(*shape):
        return pltpu.VMEM(shape, F32)

    def tile(*lead):
        return pltpu.VMEM(lead + (TILE, width), BF)

    return pl.pallas_call(
        layer_kernel,
        out_shape=(
            jax.ShapeDtypeStruct((rows, width), BF),
            jax.ShapeDtypeStruct((rows, width), F32),
            jax.ShapeDtypeStruct((2, tq, TILE, width), BF),
            jax.ShapeDtypeStruct((2, to, TILE, width), BF),
            jax.ShapeDtypeStruct((gain_rows, 128), F32),
            jax.ShapeDtypeStruct((2, thalf, TILE, width), BF),
            jax.ShapeDtypeStruct((thalf, TILE, width), BF),
        ),
        in_specs=[VMEM] * 4 + [ANY] * 4,
        out_specs=(VMEM,) * 5 + (ANY, ANY),
        scratch_shapes=[
            low(layers, 2, 2, 2, hq, width),
            low(layers, 2, 2, 2, ho, width),
            full(layers, 2, 2, 2, gain_rows // 2, 128),
            low(2, wide, width),
            tile(wide // TILE),
            full(2 * hq + 2 * ho + half, width),
            tile(8 * tiles),
            tile(8 * tiles),
            full(2, 8, rows, wide),
            low(8, rows, wide),
            tile(8 * tiles),
            tile(4, tiles),
            tile(2, tiles),
            tile(tiles),
            low(layers, 2, rows, 2 * HD),
            low(H * rows, HD),
            full(rows, (H + 2) * HD),
            full(H * rows, length),
            low(rows, H * HD),
            low(rows, width),
            full(2, rows, HD // 2),
            low(H * rows, length),
            low(layers, 2, rows, 2 * HD),
            low(layers, rows, 2 * HD),
            low(layers, rows, 2 * HD),
            low(layers - 1, rows, 2 * HD),
            tile(pool),
            tile(layers * tq),
            tile(layers * to),
            tile(layers - 1, tq),
            tile(layers - 1, to),
            full(4 + layers, gain_rows, 128),
            full(4, gain_rows, 128),
            tile(2, thalf),
            tile(thalf),
            tile(thalf),
            tile(2, thalf),
            pltpu.SemaphoreType.DMA((300,)),
            pltpu.SemaphoreType.DMA((300,)),
            pltpu.SemaphoreType.DMA((9,)),
        ],
        compiler_params=pltpu.CompilerParams(
            collective_id=0, has_side_effects=True, vmem_limit_bytes=62 * 2**20
        ),
    )(tok, cot, seg, gpad, wq, wo, wgu, wd)


def moves_tokens(mesh):
    return mesh.shape["ctx"] == 8 and mesh.shape["fsdp"] == 2 and mesh.shape["dp"] == 2


def move_tokens_body(
    tokens,
    cotangent,
    segments,
    qkv_weight,
    out_weight,
    gate_up_weight,
    down_weight,
    gains,
    qkv_first,
    out_first,
    gate_up_first,
    down_first,
    gains_first,
    qkv_second,
    out_second,
    gate_up_second,
    down_second,
    gains_second,
):
    rows = tokens.shape[1]
    width = tokens.shape[2]
    layers = lax.axis_size("ctx") // 2
    chip = lax.axis_index("ctx") * 2 + lax.axis_index("fsdp")
    own_gains = gains.shape[0]
    gain_rows = -(-own_gains * 4 * layers // 1024) * 8 + 8
    gain_part = lax.dynamic_update_slice_in_dim(
        jnp.zeros((gain_rows * 128,), F32),
        gains.astype(BF).astype(F32),
        chip * own_gains,
        0,
    )
    output, input_grad, qkv_low, out_low, gains_sum, gate_up_low, down_low = whole_layer(
        tokens[0],
        cotangent[0],
        segments.reshape(-1, rows),
        gain_part.reshape(2, gain_rows // 2, 128),
        qkv_weight,
        out_weight,
        gate_up_weight,
        down_weight,
        layers,
    )
    qkv_total = qkv_low.reshape(-1, width).astype(F32)
    out_total = out_low.reshape(-1, width).astype(F32)
    gate_up_total = gate_up_low.reshape(-1, width).astype(F32)
    down_total = down_low.reshape(-1, width).astype(F32)
    gains_total = lax.dynamic_slice_in_dim(gains_sum.reshape(-1), chip * own_gains, own_gains, 0)
    qkv_new, qkv_first_new, qkv_second_new = adamw(qkv_weight, qkv_total, qkv_first, qkv_second)
    out_new, out_first_new, out_second_new = adamw(out_weight, out_total, out_first, out_second)
    gate_up_new, gate_up_first_new, gate_up_second_new = adamw(
        gate_up_weight, gate_up_total, gate_up_first, gate_up_second
    )
    down_new, down_first_new, down_second_new = adamw(
        down_weight, down_total, down_first, down_second
    )
    gains_new, gains_first_new, gains_second_new = adamw(
        gains, gains_total, gains_first, gains_second
    )
    return (
        output[None],
        input_grad[None],
        qkv_total,
        out_total,
        gate_up_total,
        down_total,
        gains_total,
        qkv_new,
        out_new,
        gate_up_new,
        down_new,
        gains_new,
        qkv_first_new,
        out_first_new,
        gate_up_first_new,
        down_first_new,
        gains_first_new,
        qkv_second_new,
        out_second_new,
        gate_up_second_new,
        down_second_new,
        gains_second_new,
    )


def solution(mesh):
    in_specs = (
        P(("dp", "fsdp"), "ctx", None),
        P(("dp", "fsdp"), "ctx", None),
        P(("dp", "fsdp"), None),
        P(("ctx", "fsdp"), None),
        P(("ctx", "fsdp"), None),
        P(("ctx", "fsdp"), None),
        P(("ctx", "fsdp"), None),
        P(("ctx", "fsdp")),
        P(("ctx", "fsdp"), None),
        P(("ctx", "fsdp"), None),
        P(("ctx", "fsdp"), None),
        P(("ctx", "fsdp"), None),
        P(("ctx", "fsdp")),
        P(("ctx", "fsdp"), None),
        P(("ctx", "fsdp"), None),
        P(("ctx", "fsdp"), None),
        P(("ctx", "fsdp"), None),
        P(("ctx", "fsdp")),
    )
    out_specs = (
        P(("dp", "fsdp"), "ctx", None),
        P(("dp", "fsdp"), "ctx", None),
        P(("ctx", "fsdp"), None),
        P(("ctx", "fsdp"), None),
        P(("ctx", "fsdp"), None),
        P(("ctx", "fsdp"), None),
        P(("ctx", "fsdp")),
        P(("ctx", "fsdp"), None),
        P(("ctx", "fsdp"), None),
        P(("ctx", "fsdp"), None),
        P(("ctx", "fsdp"), None),
        P(("ctx", "fsdp")),
        P(("ctx", "fsdp"), None),
        P(("ctx", "fsdp"), None),
        P(("ctx", "fsdp"), None),
        P(("ctx", "fsdp"), None),
        P(("ctx", "fsdp")),
        P(("ctx", "fsdp"), None),
        P(("ctx", "fsdp"), None),
        P(("ctx", "fsdp"), None),
        P(("ctx", "fsdp"), None),
        P(("ctx", "fsdp")),
    )
    body = move_tokens_body if moves_tokens(mesh) else gather_weights_body
    return jax.shard_map(body, mesh=mesh, in_specs=in_specs, out_specs=out_specs, check_vma=False)
```
